32 devices in a mesh: dp: 8 (over z, x), seq: 4 (over y, core).
Axes of the slice: x: 2, y: 2, z: 4, core: 2. Of those that a mesh axis runs over, the one named last changes fastest.
Arguments:
- tokens: bfloat16 [24, 1024, 768], P('dp', 'seq'), may hold values from -6 to 6
- cotangent: bfloat16 [24, 1024, 768], P('dp', 'seq'), may hold values from -6 to 6
- segment_ids: int32 [24, 1024], P('dp', 'seq'), may hold values from 0 to 1, as said below
- bucket_ids: int32 [24, 1024], P('dp', 'seq'), may hold values from 0 to 31
- key_mask: int32 [24, 1024], P('dp', 'seq'), may hold values from 0 to 1, as said below
- query_weight: bfloat16 [768, 768], P('dp'), may hold values from -0.21875 to 0.21875
- key_weight: bfloat16 [768, 768], P('dp'), may hold values from -0.21875 to 0.21875
- value_weight: bfloat16 [768, 768], P('dp'), may hold values from -0.21875 to 0.21875
- output_weight: bfloat16 [768, 768], P('dp'), may hold values from -0.21875 to 0.21875
- query_bias: bfloat16 [768], P('dp'), may hold values from -3 to 3
- value_bias: bfloat16 [768], P('dp'), may hold values from -3 to 3
- output_bias: bfloat16 [768], P('dp'), may hold values from -3 to 3
- first_gain: bfloat16 [768], P('dp'), may hold values from 0.5 to 1.5
- first_shift: bfloat16 [768], P('dp'), may hold values from -2 to 2
- mixed_gain: bfloat16 [768], P('dp'), may hold values from 0.5 to 1.5
- mixed_shift: bfloat16 [768], P('dp'), may hold values from -2 to 2
- up_weight: bfloat16 [768, 3072], P('dp'), may hold values from -0.21875 to 0.21875
- down_weight: bfloat16 [3072, 768], P('dp'), may hold values from -0.109375 to 0.109375
- up_bias: bfloat16 [3072], P('dp'), may hold values from -3 to 3
- down_bias: bfloat16 [768], P('dp'), may hold values from -3 to 3
- second_gain: bfloat16 [768], P('dp'), may hold values from 0.5 to 1.5
- second_shift: bfloat16 [768], P('dp'), may hold values from -2 to 2
- inner_gain: bfloat16 [3072], P('dp'), may hold values from 0.5 to 1.5
- inner_shift: bfloat16 [3072], P('dp'), may hold values from -2 to 2
- bias_table: bfloat16 [64, 12], replicated, may hold values from -4 to 4
- head_scale: bfloat16 [12], replicated, may hold values from 0.5 to 2
Outputs:
- result: bfloat16 [24, 1024, 768], P('dp', 'seq')
- tokens_grad: float32 [24, 1024, 768], P('dp', 'seq')
- query_weight_grad: float32 [768, 768], P('dp')
- key_weight_grad: float32 [768, 768], P('dp')
- value_weight_grad: float32 [768, 768], P('dp')
- output_weight_grad: float32 [768, 768], P('dp')
- query_bias_grad: float32 [768], P('dp')
- value_bias_grad: float32 [768], P('dp')
- output_bias_grad: float32 [768], P('dp')
- first_gain_grad: float32 [768], P('dp')
- first_shift_grad: float32 [768], P('dp')
- mixed_gain_grad: float32 [768], P('dp')
- mixed_shift_grad: float32 [768], P('dp')
- up_weight_grad: float32 [768, 3072], P('dp')
- down_weight_grad: float32 [3072, 768], P('dp')
- up_bias_grad: float32 [3072], P('dp')
- down_bias_grad: float32 [768], P('dp')
- second_gain_grad: float32 [768], P('dp')
- second_shift_grad: float32 [768], P('dp')
- inner_gain_grad: float32 [3072], P('dp')
- inner_shift_grad: float32 [3072], P('dp')
- bias_table_grad: float32 [64, 12], replicated
- head_scale_grad: float32 [12], replicated
The draws below stay inside these ranges and needn't reach their ends.
Inputs may be any that keep to these rules, and one draw needn't show every extreme that they name: `segment_ids`: each item's ids are 0 on a first run of rows and 1 on the rest. `key_mask`: the first row of every item is 1.
All inputs are finite; a program needn't handle non-finite values.
Results may differ from the reference program's by a relative error of at most 0.039.
Values may be sent and summed in bfloat16 or wider, within the bound.
No kernel may reach another device: no remote copies, remote signals or barrier semaphores. Data moves between devices by JAX's collectives and lax.ppermute only.
A program may use at most 320 MiB of HBM per device.

```python
import math
import jax
import jax.numpy as jnp
from jax import lax

D = 768
HEADS = 12
FF = 3072
HD = 64
NB = 32
LEN = 1024
ITEMS_ALL = 24


def item_layout(key):
    text_key, pad_key, start_key, span_key = jax.random.split(key, 4)
    text_rows = jax.random.randint(text_key, (ITEMS_ALL,), LEN // 16, LEN // 8 + 1)
    pad_rows = jax.random.randint(pad_key, (ITEMS_ALL,), 0, text_rows // 4 + 1)
    image_rows = LEN - text_rows
    start = jax.random.randint(start_key, (ITEMS_ALL,), 1, image_rows // 2)
    extent = jax.random.randint(span_key, (ITEMS_ALL,), 0, image_rows // 4 + 1)
    places = jnp.arange(LEN, dtype=jnp.int32)[None, :]
    return (image_rows, pad_rows, start, extent, places)


def draw_segment_ids(key, part):
    image_rows, pad_rows, start, extent, places = item_layout(key)
    return (places >= image_rows[:, None]).astype(jnp.int32)


def draw_key_mask(key, part):
    image_rows, pad_rows, start, extent, places = item_layout(key)
    padding = places >= (LEN - pad_rows)[:, None]
    infill = (places >= start[:, None]) & (places < (start + extent)[:, None])
    return jnp.where(padding | infill, 0, 1).astype(jnp.int32)


def touch_ends(result, key, smallest, largest):
    spot = [jax.random.randint(jax.random.fold_in(key, axis), (), 0, length) for axis, length in enumerate(result.shape)]
    widest = result.shape.index(max(result.shape))
    beside = spot[:widest] + [(spot[widest] + 1) % result.shape[widest]] + spot[widest + 1:]
    return result.at[tuple(spot)].set(smallest).at[tuple(beside)].set(largest)


def steps_of(key, shape, cuts, least, top_value):
    loudness = 1.0
    for axis_at, blocks in cuts:
        heights = jax.random.uniform(jax.random.fold_in(jax.random.fold_in(key, 6), axis_at), (blocks,), jnp.float32, least / len(cuts), top_value / len(cuts))
        loudness = loudness * jnp.repeat(jnp.exp(heights), shape[axis_at] // blocks).reshape((-1,) + (1,) * (len(shape) - 1 - axis_at))
    return loudness


def normal_values(stream_key, dims, deviation, limit, shards=(), kind=jnp.bfloat16):
    factor_of = steps_of(stream_key, dims, shards, -0.22, 0.18) if shards else 1.0
    entries = jax.random.normal(stream_key, dims, jnp.float32) * deviation * factor_of
    return jnp.minimum(jnp.maximum(entries, -limit), limit).astype(kind)


def setup_inputs(seed: int = 0) -> dict:
    seeds = jax.random.split(jax.random.key(seed), 27)
    return {
        "tokens": normal_values(seeds[0], (ITEMS_ALL, LEN, D), 1.0, 6.0, ((0, 8), (1, 4))),
        "cotangent": normal_values(seeds[1], (ITEMS_ALL, LEN, D), 1.0, 6.0, ((0, 8), (1, 4))),
        "segment_ids": draw_segment_ids(jax.random.fold_in(seeds[26], 71), 0),
        "bucket_ids": touch_ends(jax.random.randint(seeds[3], (ITEMS_ALL, LEN), 0, NB), jax.random.fold_in(seeds[3], 1), 0, NB - 1).astype(jnp.int32),
        "key_mask": draw_key_mask(jax.random.fold_in(seeds[26], 71), 0),
        "query_weight": normal_values(seeds[5], (D, D), D ** -0.5, 0.21875, ((0, 8),)),
        "key_weight": normal_values(seeds[6], (D, D), D ** -0.5, 0.21875, ((0, 8),)),
        "value_weight": normal_values(seeds[7], (D, D), D ** -0.5, 0.21875, ((0, 8),)),
        "output_weight": normal_values(seeds[8], (D, D), D ** -0.5, 0.21875, ((0, 8),)),
        "query_bias": normal_values(seeds[9], (D,), 0.5, 3.0, ((0, 8),)),
        "value_bias": normal_values(seeds[10], (D,), 0.5, 3.0, ((0, 8),)),
        "output_bias": normal_values(seeds[11], (D,), 0.5, 3.0, ((0, 8),)),
        "first_gain": jnp.clip(1.0 + 0.1 * jax.random.normal(seeds[12], (D,), jnp.float32), 0.5, 1.5).astype(jnp.bfloat16),
        "first_shift": normal_values(seeds[13], (D,), 0.3, 2.0, ((0, 8),)),
        "mixed_gain": jnp.clip(1.0 + 0.1 * jax.random.normal(seeds[14], (D,), jnp.float32), 0.5, 1.5).astype(jnp.bfloat16),
        "mixed_shift": normal_values(seeds[15], (D,), 0.3, 2.0, ((0, 8),)),
        "up_weight": normal_values(seeds[16], (D, FF), D ** -0.5, 0.21875, ((0, 8),)),
        "down_weight": normal_values(seeds[17], (FF, D), FF ** -0.5, 0.109375, ((0, 8),)),
        "up_bias": normal_values(seeds[18], (FF,), 0.5, 3.0, ((0, 8),)),
        "down_bias": normal_values(seeds[19], (D,), 0.5, 3.0, ((0, 8),)),
        "second_gain": jnp.clip(1.0 + 0.1 * jax.random.normal(seeds[20], (D,), jnp.float32), 0.5, 1.5).astype(jnp.bfloat16),
        "second_shift": normal_values(seeds[21], (D,), 0.3, 2.0, ((0, 8),)),
        "inner_gain": jnp.clip(1.0 + 0.1 * jax.random.normal(seeds[22], (FF,), jnp.float32), 0.5, 1.5).astype(jnp.bfloat16),
        "inner_shift": normal_values(seeds[23], (FF,), 0.3, 2.0, ((0, 8),)),
        "bias_table": normal_values(seeds[24], (2 * NB, HEADS), 1.0, 4.0),
        "head_scale": jnp.clip(jnp.exp(jax.random.uniform(seeds[25], (HEADS,), jnp.float32, math.log(0.5), math.log(2.0))), 0.5, 2.0).astype(jnp.bfloat16),
    }


@jax.custom_vjp
def low(v):
    return lax.optimization_barrier(v.astype(jnp.bfloat16)).astype(jnp.float32)

@jax.custom_vjp
def low_back(v):
    return v

def low_keep(v):
    return (low(v), None)

def low_pass(kept, grad):
    return (grad,)

def back_keep(v):
    return (v, None)

def back_low(kept, grad):
    return (low(grad),)
low.defvjp(low_keep, low_pass)
low_back.defvjp(back_keep, back_low)
EPSILON = 1e-05
HIGHEST_PRECISION = lax.Precision.HIGHEST

def norm_rows(values, norm_gain, norm_shift):
    row_mean = lax.optimization_barrier(jnp.mean(values, axis=-1, keepdims=True))
    centred = values - row_mean
    spread = lax.optimization_barrier(jnp.mean(centred * centred, axis=-1, keepdims=True))
    return centred * lax.rsqrt(spread + EPSILON) * norm_gain + norm_shift

def matmul(left, right):
    return jnp.dot(left, right, precision=HIGHEST_PRECISION, preferred_element_type=jnp.float32)

def item_layer(params, item_tokens, item_segments, item_buckets, item_mask):
    query_weight, key_weight, value_weight, output_weight, query_bias, value_bias, output_bias, first_gain, first_shift, mixed_gain, mixed_shift, up_weight, down_weight, up_bias, down_bias, second_gain, second_shift, inner_gain, inner_shift, bias_table, head_scale = params
    factor = float(HD) ** (-0.5)
    normed = low(norm_rows(item_tokens, first_gain, first_shift))
    queries = low_back(low((matmul(normed, query_weight) + query_bias) * factor)).reshape(LEN, HEADS, HD)
    key_rows = low_back(low(matmul(normed, key_weight))).reshape(LEN, HEADS, HD)
    values = low_back(low(matmul(normed, value_weight) + value_bias)).reshape(LEN, HEADS, HD)
    dot_scores = low_back(jnp.einsum('qhd,khd->hqk', queries, key_rows, precision=HIGHEST_PRECISION))
    offset = jnp.mod(item_buckets[None, :] - item_buckets[:, None], NB)
    bucket_index = (item_segments[:, None] * NB + offset).astype(jnp.int32)
    rel_bias = jnp.transpose(bias_table[bucket_index], (2, 0, 1))
    scores = jnp.where(item_mask[None, None, :] > 0, dot_scores + rel_bias, -1e+30)
    row_max = lax.optimization_barrier(jnp.max(scores, axis=-1, keepdims=True))
    exponent = jnp.exp(scores - row_max)
    soft_weights = low(exponent / lax.optimization_barrier(jnp.sum(exponent, axis=-1, keepdims=True)))
    head_rows = low_back(jnp.einsum('hqk,khd->qhd', soft_weights, values, precision=HIGHEST_PRECISION))
    scaled = (head_rows * head_scale[None, :, None]).reshape(LEN, D)
    mixed = low(norm_rows(scaled, mixed_gain, mixed_shift))
    middle = item_tokens + low_back(matmul(mixed, output_weight) + output_bias)
    second = low(norm_rows(middle, second_gain, second_shift))
    pre_act = low_back(matmul(second, up_weight) + up_bias)
    inner = low(norm_rows(jax.nn.gelu(pre_act, approximate=False), inner_gain, inner_shift))
    return middle + low_back(matmul(inner, down_weight) + down_bias)

def reference(tokens, cotangent, segment_ids, bucket_ids, key_mask, query_weight, key_weight, value_weight, output_weight, query_bias, value_bias, output_bias, first_gain, first_shift, mixed_gain, mixed_shift, up_weight, down_weight, up_bias, down_bias, second_gain, second_shift, inner_gain, inner_shift, bias_table, head_scale):
    params = (query_weight, key_weight, value_weight, output_weight, query_bias, value_bias, output_bias, first_gain, first_shift, mixed_gain, mixed_shift, up_weight, down_weight, up_bias, down_bias, second_gain, second_shift, inner_gain, inner_shift, bias_table, head_scale)
    params = tuple((entry.astype(jnp.float32) for entry in params))
    inputs = tokens.astype(jnp.float32)

    def whole(layer_input, layer_params):

        def per_item(packed):
            return item_layer(layer_params, packed[0], packed[1], packed[2], packed[3])
        return lax.map(jax.checkpoint(per_item), (layer_input, segment_ids, bucket_ids, key_mask))
    full, pullback = jax.vjp(whole, inputs, params)
    tokens_grad, grads = pullback(cotangent.astype(jnp.float32))
    query_weight_grad, key_weight_grad, value_weight_grad, output_weight_grad, query_bias_grad, value_bias_grad, output_bias_grad, first_gain_grad, first_shift_grad, mixed_gain_grad, mixed_shift_grad, up_weight_grad, down_weight_grad, up_bias_grad, down_bias_grad, second_gain_grad, second_shift_grad, inner_gain_grad, inner_shift_grad, bias_table_grad, head_scale_grad = grads
    return (full.astype(jnp.bfloat16), tokens_grad, query_weight_grad, key_weight_grad, value_weight_grad, output_weight_grad, query_bias_grad, value_bias_grad, output_bias_grad, first_gain_grad, first_shift_grad, mixed_gain_grad, mixed_shift_grad, up_weight_grad, down_weight_grad, up_bias_grad, down_bias_grad, second_gain_grad, second_shift_grad, inner_gain_grad, inner_shift_grad, bias_table_grad, head_scale_grad)
```

```python
from functools import partial

import jax
import jax.numpy as jnp
from jax import lax
from jax.experimental import pallas as pl
from jax.experimental.pallas import tpu as pltpu
from jax.sharding import PartitionSpec as P

EPSILON = 1e-05
FLOOR_SCORE = -1e30
F32 = jnp.float32
B16 = jnp.bfloat16
NN = (((1,), (0,)), ((), ()))
NT = (((1,), (1,)), ((), ()))
TN = (((0,), (0,)), ((), ()))
VMEM_LIMIT = 58 * 1024 * 1024
SMALL_ROWS = 32
LANES = 128


def dot(a, b, dims, **kw):
    return lax.dot_general(a, b, dims, preferred_element_type=F32, **kw)


def params():
    return pltpu.CompilerParams(vmem_limit_bytes=VMEM_LIMIT)


def cost(flops, nbytes, trans=0):
    return pl.CostEstimate(flops=flops, bytes_accessed=nbytes, transcendentals=trans)


def low_lanes(shape):
    return lax.broadcasted_iota(jnp.int32, shape, 1) < shape[1] // 2


def low_rows(shape):
    return lax.broadcasted_iota(jnp.int32, shape, 0) < shape[0] // 2


def standardise(values):
    mean = jnp.mean(values, axis=-1, keepdims=True)
    centred = values - mean
    spread = jnp.mean(centred * centred, axis=-1, keepdims=True)
    rate = lax.rsqrt(spread + EPSILON)
    return centred * rate, rate


def standard_back(hat_grad, hat, rate):
    first = jnp.mean(hat_grad, axis=-1, keepdims=True)
    second = jnp.mean(hat_grad * hat, axis=-1, keepdims=True)
    return rate * (hat_grad - first - hat * second)


def sums(array):
    return jnp.sum(array, axis=0, keepdims=True)


class Pieces:
    def __init__(self, own, mine, other):
        self.own, self.mine, self.other = own, mine, other

    def arrays(self):
        return [self.own] + list(self.mine) + list(self.other)

    def entries(self, refs, idx_ref):
        count = len(self.mine)
        core = idx_ref[count + 1]
        out = [(refs[0].at[0], idx_ref[0], 0), (refs[0].at[1], idx_ref[0], 1)]
        for j in range(count):
            out.append((refs[1 + j], idx_ref[1 + j], core))
            out.append((refs[1 + count + j], idx_ref[1 + j], 1 - core))
        return out


def place_rows(ref, first, rows, target, shard, half, lane, width, sem):
    start = pl.multiple_of(shard * rows, 16)
    if isinstance(half, int):
        lanes = pl.ds(half * lane[0] + lane[1], width)
    else:
        lanes = pl.ds(pl.multiple_of(half * lane[0] + lane[1], LANES), width)
    pltpu.make_async_copy(
        ref.at[pl.ds(first, rows), :], target.at[pl.ds(start, rows), lanes], sem
    ).start()


def wait_whole(target, sem):
    pltpu.make_async_copy(target, target, sem).wait()


def qkv_kernel(layout, block, a_blocks, idx_ref, x_ref, *refs):
    count, rb, half_width, factor = layout
    n_in = 1 + 2 * count
    pieces = Pieces(None, [None] * count, [None] * count)
    in_refs = refs[:n_in]
    normed_ref, q_ref, kva_ref, kvc_ref, vec_ref = refs[n_in : n_in + 5]
    wq, wk, wv, small, sems = refs[n_in + 5 :]
    step = pl.program_id(0)
    targets = (wq, wk, wv)

    @pl.when(step == 0)
    def _():
        entries = pieces.entries(in_refs, idx_ref)
        for j in range(count + 1):
            ref = in_refs[0].at[0] if j == 0 else in_refs[j]
            pltpu.make_async_copy(
                ref.at[pl.ds(3 * rb, SMALL_ROWS), :], small.at[j], sems.at[3]
            ).start()
        for ref, shard, half in entries:
            for t in range(3):
                place_rows(
                    ref, t * rb, rb, targets[t], shard, half, (half_width, 0), half_width, sems.at[t]
                )
        wait_whole(small, sems.at[3])
        total = jnp.zeros(vec_ref.shape, F32)
        for j in range(count + 1):
            row = lax.broadcasted_iota(jnp.int32, (LANES, vec_ref.shape[1]), 0)
            col = lax.broadcasted_iota(jnp.int32, (LANES, vec_ref.shape[1]), 1)
            spot = jnp.where((row < rb) & (col == row + idx_ref[j] * rb), 1.0, 0.0).astype(B16)
            total = total + dot(small[j, :, 0:LANES], spot, NN)
        vec_ref[...] = total
        for t in range(3):
            wait_whole(targets[t], sems.at[t])

    hat, _ = standardise(x_ref[...].astype(F32))
    normed = (hat * vec_ref[3:4, :] + vec_ref[4:5, :]).astype(B16)
    normed_ref[...] = normed
    q_ref[...] = ((dot(normed, wq[...], NN) + vec_ref[0:1, :]) * factor).astype(B16)
    keys = dot(normed, wk[...], NN).astype(B16)
    values = (dot(normed, wv[...], NN) + vec_ref[1:2, :]).astype(B16)

    @pl.when(step < a_blocks)
    def _():
        kva_ref[0] = keys
        kva_ref[1] = values

    @pl.when(step >= a_blocks)
    def _():
        kvc_ref[0] = keys
        kvc_ref[1] = values


def project(x, pieces, idx, rb, rows_a, block, factor):
    rows, width = x.shape
    count = len(pieces.mine)
    a_blocks = rows_a // block
    layout = (count, rb, width // 2, factor)
    anywhere = pl.BlockSpec(memory_space=pl.ANY)
    rowed = pl.BlockSpec((block, width), lambda i, s: (i, 0))
    return pl.pallas_call(
        partial(qkv_kernel, layout, block, a_blocks),
        grid_spec=pltpu.PrefetchScalarGridSpec(
            num_scalar_prefetch=1,
            grid=(rows // block,),
            in_specs=[rowed] + [anywhere] * len(pieces.arrays()),
            out_specs=[
                rowed,
                rowed,
                pl.BlockSpec((2, block, width), lambda i, s: (0, jnp.minimum(i, a_blocks - 1), 0)),
                pl.BlockSpec((2, block, width), lambda i, s: (0, jnp.maximum(i - a_blocks, 0), 0)),
                pl.BlockSpec((SMALL_ROWS, width), lambda i, s: (0, 0)),
            ],
            scratch_shapes=[pltpu.VMEM((width, width), B16)] * 3
            + [
                pltpu.VMEM((count + 1, SMALL_ROWS, width // 2), B16),
                pltpu.SemaphoreType.DMA((4,)),
            ],
        ),
        out_shape=[
            jax.ShapeDtypeStruct((rows, width), B16),
            jax.ShapeDtypeStruct((rows, width), B16),
            jax.ShapeDtypeStruct((2, rows_a, width), B16),
            jax.ShapeDtypeStruct((2, rows - rows_a, width), B16),
            jax.ShapeDtypeStruct((SMALL_ROWS, width), F32),
        ],
        compiler_params=params(),
        cost_estimate=cost(6 * rows * width * width, 20 * rows * width),
        name="project",
    )(idx, x, *pieces.arrays())


def project_back_kernel(layout, idx_ref, x_ref, dq_ref, dkv_ref, mid_ref, vec_ref, *refs):
    count, rb, half_width, factor = layout
    n_in = 1 + 2 * count
    pieces = Pieces(None, [None] * count, [None] * count)
    in_refs = refs[:n_in]
    out_ref, acc_ref = refs[n_in : n_in + 2]
    wq, wk, wv, sems = refs[n_in + 2 :]
    targets = (wq, wk, wv)
    step = pl.program_id(0)

    @pl.when(step == 0)
    def _():
        for ref, shard, half in pieces.entries(in_refs, idx_ref):
            for t in range(3):
                place_rows(
                    ref, t * rb, rb, targets[t], shard, half, (half_width, 0), half_width, sems.at[t]
                )
        acc_ref[...] = jnp.zeros_like(acc_ref)
        for t in range(3):
            wait_whole(targets[t], sems.at[t])

    dq, dk, dv = dq_ref[...], dkv_ref[0], dkv_ref[1]
    grad = factor * dot(dq, wq[...], NT) + dot(dk, wk[...], NT) + dot(dv, wv[...], NT)
    hat, rate = standardise(x_ref[...].astype(F32))
    out_ref[...] = mid_ref[...] + standard_back(grad * vec_ref[3:4, :], hat, rate)
    acc_ref[0:1, :] += sums(grad * hat)
    acc_ref[1:2, :] += sums(grad)
    acc_ref[2:3, :] += factor * sums(dq.astype(F32))
    acc_ref[3:4, :] += sums(dv.astype(F32))


def project_back(x, dq, dkv, mid, vec, pieces, idx, rb, block, factor):
    rows, width = x.shape
    count = len(pieces.mine)
    layout = (count, rb, width // 2, factor)
    anywhere = pl.BlockSpec(memory_space=pl.ANY)
    rowed = pl.BlockSpec((block, width), lambda i, s: (i, 0))
    return pl.pallas_call(
        partial(project_back_kernel, layout),
        grid_spec=pltpu.PrefetchScalarGridSpec(
            num_scalar_prefetch=1,
            grid=(rows // block,),
            in_specs=[
                rowed,
                rowed,
                pl.BlockSpec((2, block, width), lambda i, s: (0, i, 0)),
                rowed,
                pl.BlockSpec((SMALL_ROWS, width), lambda i, s: (0, 0)),
            ]
            + [anywhere] * len(pieces.arrays()),
            out_specs=[rowed, pl.BlockSpec((8, width), lambda i, s: (0, 0))],
            scratch_shapes=[pltpu.VMEM((width, width), B16)] * 3 + [pltpu.SemaphoreType.DMA((3,))],
        ),
        out_shape=[
            jax.ShapeDtypeStruct((rows, width), F32),
            jax.ShapeDtypeStruct((8, width), F32),
        ],
        compiler_params=params(),
        cost_estimate=cost(6 * rows * width * width, 24 * rows * width),
        name="project_back",
    )(idx, x, dq, dkv, mid, vec, *pieces.arrays())


def score_operands(qp, kp, aux, hot, tab):
    rel = dot(hot, tab, NN).astype(B16)
    lq, lk = low_lanes(qp.shape), low_lanes(kp.shape)
    return (
        (jnp.where(lq, qp, rel), jnp.where(lk, kp, aux)),
        (jnp.where(lq, rel, qp), jnp.where(lk, aux, kp)),
    )


def attend_kernel(n_kv, q_ref, aux_ref, hot_ref, tab_ref, *refs):
    kv_refs = refs[:n_kv]
    o_ref, l_ref = refs[-2:]
    qp = q_ref[...]
    kp = jnp.concatenate([r[0, 0] for r in kv_refs], axis=0)
    vp = jnp.concatenate([r[1, 0] for r in kv_refs], axis=0)
    outs = []
    for h, (qh, kh) in enumerate(score_operands(qp, kp, aux_ref[0], hot_ref[...], tab_ref[...])):
        scores = dot(kh, qh, NT)
        top = jnp.max(scores, axis=0, keepdims=True)
        exponent = jnp.exp(scores - top)
        total = jnp.sum(exponent, axis=0, keepdims=True)
        out = dot(vp, exponent.astype(B16), TN)
        outs.append(out * (1.0 / total))
        l_ref[0, 0, h : h + 1, :] = top + jnp.log(total)
    o_ref[...] = jnp.transpose(jnp.where(low_rows(outs[0].shape), outs[0], outs[1]))


def attend(q, kvs, aux, hot, tab, row_start, q_rows, into):
    rows, width = q.shape
    items, keys = aux.shape[:2]
    pairs = width // LANES
    first = row_start // q_rows
    rowed = pl.BlockSpec((q_rows, LANES), lambda i, p: (first + i, p))
    kv_specs = [pl.BlockSpec((2, 1, kv.shape[2], LANES), lambda i, p: (0, i, 0, p)) for kv in kvs]
    args = [q, aux, hot, tab] + list(kvs)
    specs = [
        rowed,
        pl.BlockSpec((1, keys, LANES), lambda i, p: (i, 0, 0)),
        pl.BlockSpec((q_rows, hot.shape[1]), lambda i, p: (first + i, 0)),
        pl.BlockSpec((tab.shape[0], LANES), lambda i, p: (0, p)),
    ] + kv_specs
    aliases = {}
    if into is not None:
        aliases = {len(args): 0}
        args.append(into)
        specs.append(pl.BlockSpec(memory_space=pl.ANY))
    return pl.pallas_call(
        partial(attend_kernel, len(kvs)),
        grid=(items, pairs),
        in_specs=specs,
        out_specs=[rowed, pl.BlockSpec((1, 1, 8, q_rows), lambda i, p: (i, p, 0, 0))],
        out_shape=[
            jax.ShapeDtypeStruct((rows, width), F32),
            jax.ShapeDtypeStruct((items, pairs, 8, q_rows), F32),
        ],
        input_output_aliases=aliases,
        compiler_params=params(),
        cost_estimate=cost(
            4 * items * q_rows * keys * width * 2,
            items * (q_rows * width * 6 + keys * width * 4),
            items * q_rows * keys * 2 * pairs,
        ),
        name="attend",
    )(*args)


def attend_back_kernel(n_kv, q_ref, aux_ref, hot_ref, tab_ref, do_ref, o_ref, l_ref, *refs):
    kv_refs = refs[:n_kv]
    dq_ref, own_ref, other_ref, g_ref = refs[-4:]
    qp, dop, hot = q_ref[...], do_ref[...], hot_ref[...]
    kp = jnp.concatenate([r[0, 0] for r in kv_refs], axis=0)
    vp = jnp.concatenate([r[1, 0] for r in kv_refs], axis=0)
    lk = low_lanes(kp.shape)
    zero = jnp.zeros_like(vp)
    product = dop.astype(F32) * o_ref[...]
    row = lax.broadcasted_iota(jnp.int32, (8, LANES), 0)
    pick = jnp.where(low_lanes((8, LANES)) == (row == 0), 1.0, 0.0)
    row_dot = dot(pick, product, NT, precision=lax.Precision.HIGHEST)
    dvs, dks, dqs = [], [], []
    operands = score_operands(qp, kp, aux_ref[0], hot, tab_ref[...])
    for h, (qh, kh) in enumerate(operands):
        vh = jnp.where(lk, vp, zero) if h == 0 else jnp.where(lk, zero, vp)
        probs = jnp.exp(dot(kh, qh, NT) - l_ref[0, 0, h : h + 1, :])
        score_grad = (probs * (dot(vh, dop, NT) - row_dot[h : h + 1, :])).astype(B16)
        dvs.append(dot(probs.astype(B16), dop, NN))
        dks.append(dot(score_grad, qp, NN))
        dqs.append(dot(kh, score_grad, TN))
    dk = jnp.where(lk, dks[0], dks[1]).astype(B16)
    dv = jnp.where(lk, dvs[0], dvs[1]).astype(B16)
    half = own_ref.shape[2]
    own_ref[0, 0], own_ref[1, 0] = dk[:half], dv[:half]
    other_ref[0, 0], other_ref[1, 0] = dk[half:], dv[half:]
    lr = low_rows(dqs[0].shape)
    dq_ref[...] = jnp.transpose(jnp.where(lr, dqs[0], dqs[1])).astype(B16)
    levels = jnp.where(lr, dqs[1], dqs[0])
    upper = levels.astype(B16)
    lower = (levels - upper.astype(F32)).astype(B16)
    g_ref[0, 0] = dot(upper, hot, NN) + dot(lower, hot, NN)


def attend_back(q, kvs, aux, hot, tab, head_grad, head_rows, logs, row_start, q_rows, into):
    rows, width = q.shape
    items, keys = aux.shape[:2]
    pairs = width // LANES
    first = row_start // q_rows
    rowed = pl.BlockSpec((q_rows, LANES), lambda i, p: (first + i, p))
    kv_specs = [pl.BlockSpec((2, 1, kv.shape[2], LANES), lambda i, p: (0, i, 0, p)) for kv in kvs]
    args = [q, aux, hot, tab, head_grad, head_rows, logs] + list(kvs)
    specs = [
        rowed,
        pl.BlockSpec((1, keys, LANES), lambda i, p: (i, 0, 0)),
        pl.BlockSpec((q_rows, hot.shape[1]), lambda i, p: (first + i, 0)),
        pl.BlockSpec((tab.shape[0], LANES), lambda i, p: (0, p)),
        rowed,
        rowed,
        pl.BlockSpec((1, 1, 8, q_rows), lambda i, p: (i, p, 0, 0)),
    ] + kv_specs
    aliases = {}
    if into is not None:
        aliases = {len(args): 0}
        args.append(into)
        specs.append(pl.BlockSpec(memory_space=pl.ANY))
    half = pl.BlockSpec((2, 1, keys // 2, LANES), lambda i, p: (0, i, 0, p))
    half_shape = jax.ShapeDtypeStruct((2, items, keys // 2, width), B16)
    return pl.pallas_call(
        partial(attend_back_kernel, len(kvs)),
        grid=(items, pairs),
        in_specs=specs,
        out_specs=[
            rowed,
            half,
            half,
            pl.BlockSpec((1, 1, LANES, hot.shape[1]), lambda i, p: (i, p, 0, 0)),
        ],
        out_shape=[
            jax.ShapeDtypeStruct((rows, width), B16),
            half_shape,
            half_shape,
            jax.ShapeDtypeStruct((items, pairs, LANES, hot.shape[1]), F32),
        ],
        input_output_aliases=aliases,
        compiler_params=params(),
        cost_estimate=cost(
            10 * items * q_rows * keys * width * 2,
            items * (q_rows * width * 10 + keys * width * 8),
            items * q_rows * keys * 2 * pairs,
        ),
        name="attend_back",
    )(*args)


def gelu_parts(v):
    scaled = jnp.abs(v) * 0.7071067811865476
    ratio = 1.0 / (1.0 + 0.3275911 * scaled)
    bell = jnp.exp(v * v * -0.5)
    series = ratio * (
        0.254829592 * 0.5
        + ratio
        * (
            -0.284496736 * 0.5
            + ratio * (1.421413741 * 0.5 + ratio * (-1.453152027 * 0.5 + ratio * (1.061405429 * 0.5)))
        )
    )
    tail = series * bell
    mass = jnp.where(v < 0.0, tail, 1.0 - tail)
    return v * mass, mass + v * bell * 0.3989422804014327


def up_kernel(layout, idx_ref, x_ref, o_ref, vec_ref, ff_ref, scale_ref, *refs):
    count, rb, half_width, blocks = layout
    n_in = 1 + 2 * count
    pieces = Pieces(None, [None] * count, [None] * count)
    in_refs = refs[:n_in]
    mixed_ref, middle_ref, second_ref, inner_ref, hat_ref, slope_ref, rate_ref = refs[n_in : n_in + 7]
    wo, wu, sems = refs[n_in + 7 :]
    step = pl.program_id(0)

    @pl.when(step == 0)
    def _():
        load_output_up(pieces.entries(in_refs, idx_ref), wo, wu, sems, rb, half_width, blocks)

    hat, _ = standardise(o_ref[...] * scale_ref[0:1, :])
    mixed = (hat * vec_ref[5:6, :] + vec_ref[6:7, :]).astype(B16)
    mixed_ref[...] = mixed

    @pl.when(step == 0)
    def _():
        wait_whole(wo, sems.at[0])

    middle = x_ref[...].astype(F32) + dot(mixed, wo[...], NN) + vec_ref[2:3, :]
    middle_ref[...] = middle
    hat, _ = standardise(middle)
    second = (hat * vec_ref[7:8, :] + vec_ref[8:9, :]).astype(B16)
    second_ref[...] = second

    @pl.when(step == 0)
    def _():
        wait_whole(wu, sems.at[1])

    pre = dot(second, wu[...], NN) + ff_ref[0:1, :]
    active, slope = gelu_parts(pre)
    slope_ref[...] = slope.astype(B16)
    hat, rate = standardise(active)
    hat_ref[...] = hat.astype(B16)
    inner_ref[...] = (hat * ff_ref[1:2, :] + ff_ref[2:3, :]).astype(B16)
    rate_ref[...] = jnp.broadcast_to(rate, rate_ref.shape)


def load_output_up(entries, wo, wu, sems, rb, half_width, blocks):
    for ref, shard, half in entries:
        place_rows(ref, 0, rb, wo, shard, half, (half_width, 0), half_width, sems.at[0])
    for ref, shard, half in entries:
        for b in range(blocks):
            place_rows(
                ref,
                (1 + b) * rb,
                rb,
                wu,
                shard,
                half,
                (blocks * half_width, b * half_width),
                half_width,
                sems.at[1],
            )


def feed_up(x, head_rows, vec, ff, scale, pieces, idx, rb, block):
    rows, width = x.shape
    inner = ff.shape[1]
    count = len(pieces.mine)
    layout = (count, rb, width // 2, inner // width)
    anywhere = pl.BlockSpec(memory_space=pl.ANY)

    def rowed(n):
        return pl.BlockSpec((block, n), lambda i, s: (i, 0))

    def fixed(shape):
        return pl.BlockSpec(shape, lambda i, s: (0, 0))

    return pl.pallas_call(
        partial(up_kernel, layout),
        grid_spec=pltpu.PrefetchScalarGridSpec(
            num_scalar_prefetch=1,
            grid=(rows // block,),
            in_specs=[rowed(width), rowed(width), fixed(vec.shape), fixed(ff.shape), fixed(scale.shape)]
            + [anywhere] * len(pieces.arrays()),
            out_specs=[
                rowed(width),
                rowed(width),
                rowed(width),
                rowed(inner),
                rowed(inner),
                rowed(inner),
                rowed(LANES),
            ],
            scratch_shapes=[
                pltpu.VMEM((width, width), B16),
                pltpu.VMEM((width, inner), B16),
                pltpu.SemaphoreType.DMA((2,)),
            ],
        ),
        out_shape=[
            jax.ShapeDtypeStruct((rows, width), B16),
            jax.ShapeDtypeStruct((rows, width), F32),
            jax.ShapeDtypeStruct((rows, width), B16),
            jax.ShapeDtypeStruct((rows, inner), B16),
            jax.ShapeDtypeStruct((rows, inner), B16),
            jax.ShapeDtypeStruct((rows, inner), B16),
            jax.ShapeDtypeStruct((rows, LANES), F32),
        ],
        compiler_params=params(),
        cost_estimate=cost(2 * rows * width * (width + inner), rows * (inner * 6 + width * 14)),
        name="feed_up",
    )(idx, x, head_rows, vec, ff, scale, *pieces.arrays())


def down_kernel(
    layout,
    idx_ref,
    cot_ref,
    middle_ref,
    inner_ref,
    hat_ref,
    slope_ref,
    rate_ref,
    o_ref,
    vec_ref,
    ff_ref,
    scale_ref,
    *refs,
):
    count, rb, half_width, blocks = layout
    n_in = 1 + 2 * count
    pieces = Pieces(None, [None] * count, [None] * count)
    up_refs, down_refs = refs[:n_in], refs[n_in : 2 * n_in]
    result_ref, pre_ref, mid_ref, branch_ref, head_ref, acc_ref, ffacc_ref = refs[2 * n_in : 2 * n_in + 7]
    wo, wu, wd, sems = refs[2 * n_in + 7 :]
    step = pl.program_id(0)

    @pl.when(step == 0)
    def _():
        for ref, shard, half in pieces.entries(down_refs, idx_ref):
            place_rows(ref, 0, blocks * rb, wd, shard, half, (half_width, 0), half_width, sems.at[2])
        load_output_up(pieces.entries(up_refs, idx_ref), wo, wu, sems, rb, half_width, blocks)
        acc_ref[...] = jnp.zeros_like(acc_ref)
        ffacc_ref[...] = jnp.zeros_like(ffacc_ref)
        wait_whole(wd, sems.at[2])

    cot = cot_ref[...]
    middle = middle_ref[...]
    result_ref[...] = (middle + dot(inner_ref[...], wd[...], NN) + vec_ref[9:10, :]).astype(B16)
    grad = dot(cot, wd[...], NT)
    hat = hat_ref[...].astype(F32)
    ffacc_ref[1:2, :] += sums(grad * hat)
    ffacc_ref[2:3, :] += sums(grad)
    pre = (
        standard_back(grad * ff_ref[1:2, :], hat, rate_ref[:, 0:1]) * slope_ref[...].astype(F32)
    ).astype(B16)
    pre_ref[...] = pre
    ffacc_ref[0:1, :] += sums(pre.astype(F32))

    @pl.when(step == 0)
    def _():
        wait_whole(wu, sems.at[1])

    grad = dot(pre, wu[...], NT)
    hat, rate = standardise(middle)
    acc_ref[0:1, :] += sums(grad * hat)
    acc_ref[1:2, :] += sums(grad)
    cot = cot.astype(F32)
    acc_ref[3:4, :] += sums(cot)
    mid = cot + standard_back(grad * vec_ref[7:8, :], hat, rate)
    mid_ref[...] = mid
    branch = mid.astype(B16)
    branch_ref[...] = branch
    acc_ref[2:3, :] += sums(branch.astype(F32))

    @pl.when(step == 0)
    def _():
        wait_whole(wo, sems.at[0])

    grad = dot(branch, wo[...], NT)
    heads = o_ref[...]
    hat, rate = standardise(heads * scale_ref[0:1, :])
    acc_ref[4:5, :] += sums(grad * hat)
    acc_ref[5:6, :] += sums(grad)
    scaled = standard_back(grad * vec_ref[5:6, :], hat, rate)
    acc_ref[6:7, :] += sums(scaled * heads)
    head_ref[...] = (scaled * scale_ref[0:1, :]).astype(B16)


def feed_down(cot, middle, inner, hat, slope, rate, head_rows, vec, ff, scale, ups, downs, idx, rb, block):
    rows, width = cot.shape
    wide = ff.shape[1]
    count = len(ups.mine)
    layout = (count, rb, width // 2, wide // width)
    anywhere = pl.BlockSpec(memory_space=pl.ANY)

    def rowed(n):
        return pl.BlockSpec((block, n), lambda i, s: (i, 0))

    def fixed(shape):
        return pl.BlockSpec(shape, lambda i, s: (0, 0))

    return pl.pallas_call(
        partial(down_kernel, layout),
        grid_spec=pltpu.PrefetchScalarGridSpec(
            num_scalar_prefetch=1,
            grid=(rows // block,),
            in_specs=[
                rowed(width),
                rowed(width),
                rowed(wide),
                rowed(wide),
                rowed(wide),
                rowed(LANES),
                rowed(width),
                fixed(vec.shape),
                fixed(ff.shape),
                fixed(scale.shape),
            ]
            + [anywhere] * (len(ups.arrays()) + len(downs.arrays())),
            out_specs=[
                rowed(width),
                rowed(wide),
                rowed(width),
                rowed(width),
                rowed(width),
                fixed((8, width)),
                fixed((8, wide)),
            ],
            scratch_shapes=[
                pltpu.VMEM((width, width), B16),
                pltpu.VMEM((width, wide), B16),
                pltpu.VMEM((wide, width), B16),
                pltpu.SemaphoreType.DMA((3,)),
            ],
        ),
        out_shape=[
            jax.ShapeDtypeStruct((rows, width), B16),
            jax.ShapeDtypeStruct((rows, wide), B16),
            jax.ShapeDtypeStruct((rows, width), F32),
            jax.ShapeDtypeStruct((rows, width), B16),
            jax.ShapeDtypeStruct((rows, width), B16),
            jax.ShapeDtypeStruct((8, width), F32),
            jax.ShapeDtypeStruct((8, wide), F32),
        ],
        compiler_params=params(),
        cost_estimate=cost(2 * rows * width * (width + 3 * wide), rows * (wide * 8 + width * 20)),
        name="feed_down",
    )(idx, cot, middle, inner, hat, slope, rate, head_rows, vec, ff, scale, *ups.arrays(), *downs.arrays())


def side_kernel(groups, n_left, n_right, shards, rb, scales, *refs):
    lefts, rights = refs[:n_left], refs[n_left : n_left + n_right]
    out_ref = refs[n_left + n_right]
    turned = refs[n_left + n_right + 1 :]
    half, block = pl.program_id(0), pl.program_id(1)

    @pl.when((half == 0) & (block == 0))
    def _():
        for ref, turn in zip(lefts, turned):
            turn[...] = jnp.transpose(ref[...])

    start = 0
    for g, (left, blocks) in enumerate(groups):

        @pl.when((block >= start) & (block < start + blocks))
        def _(g=g, left=left):
            right = rights[g]
            right = right[0] if len(right.shape) == 3 else right[...]
            out = dot(turned[left][...], right, NN)
            if scales[g] != 1.0:
                out = out * scales[g]
            out_ref[0, :, 0] = out.astype(B16).reshape(shards, rb, out.shape[1])

        start += blocks


def side_grads(lefts, rights, shards, rb, name):
    rows, width = lefts[0].shape
    half_width = width // 2
    specs = [pl.BlockSpec((rows, width), lambda h, b: (0, 0)) for _ in lefts]
    groups, args, scales, start = [], list(lefts), [], 0
    for array, lead, left, scale in rights:
        blocks = array.shape[-1] // width

        def at(h, b, start=start, blocks=blocks):
            return h * blocks + jnp.clip(b - start, 0, blocks - 1)

        if lead is None:
            specs.append(pl.BlockSpec((rows, half_width), lambda h, b, at=at: (0, at(h, b))))
        else:
            specs.append(
                pl.BlockSpec((1, rows, half_width), lambda h, b, at=at, lead=lead: (lead, 0, at(h, b)))
            )
        args.append(array)
        groups.append((left, blocks))
        scales.append(scale)
        start += blocks
    return pl.pallas_call(
        partial(side_kernel, groups, len(lefts), len(rights), shards, rb, scales),
        grid=(2, start),
        in_specs=specs,
        out_specs=pl.BlockSpec((1, shards, 1, rb, half_width), lambda h, b: (h, 0, b, 0, 0)),
        out_shape=jax.ShapeDtypeStruct((2, shards, start, rb, half_width), B16),
        scratch_shapes=[pltpu.VMEM((width, rows), B16) for _ in lefts],
        compiler_params=params(),
        cost_estimate=cost(
            2 * rows * width * width * start, 2 * width * (rows * (len(lefts) + start) + width * start)
        ),
        name=name,
    )(*args)


def down_side_kernel(group, blocks, rb, left_ref, right_ref, out_ref):
    turned = jnp.transpose(left_ref[...])
    half_width = out_ref.shape[-1]
    for half in range(2):
        out = dot(turned, right_ref[:, half * half_width : (half + 1) * half_width], NN)
        out_ref[half] = out.astype(B16).reshape(group, blocks, rb, half_width)


def down_side_grads(inner, cot, shards, rb):
    rows, wide = inner.shape
    width = cot.shape[1]
    half_width = width // 2
    blocks = wide // width
    group = width // (blocks * rb)
    return pl.pallas_call(
        partial(down_side_kernel, group, blocks, rb),
        grid=(blocks,),
        in_specs=[
            pl.BlockSpec((rows, width), lambda g: (0, g)),
            pl.BlockSpec((rows, width), lambda g: (0, 0)),
        ],
        out_specs=pl.BlockSpec((2, group, blocks, rb, half_width), lambda g: (0, g, 0, 0, 0)),
        out_shape=jax.ShapeDtypeStruct((2, shards, blocks, rb, half_width), B16),
        compiler_params=params(),
        cost_estimate=cost(2 * rows * width * wide, 2 * (rows * (wide + width) + width * wide)),
        name="down_side",
    )(inner, cot)


class Places:
    def __init__(self):
        self.n = lax.axis_size("dp")
        self.chips = lax.axis_size("seq") // 2
        evens = list(range(0, self.n, 2))
        odds = [i for i in range(self.n) if i % 2]
        self.ring = evens + odds[::-1]
        self.inverse = [self.ring.index(i) for i in range(self.n)]
        me = lax.axis_index("dp")
        self.shard = me
        self.spot = jnp.array(self.inverse, jnp.int32)[me]
        seq = lax.axis_index("seq")
        self.core = lax.rem(seq, 2)
        self.chip = lax.div(seq, 2)

    def at(self, offset):
        table = jnp.array(self.ring * 3, jnp.int32)
        return table[self.spot + (offset + self.n)]

    def round(self, x, way):
        ring, n = self.ring, self.n
        return lax.ppermute(x, "dp", [(ring[i], ring[(i + way) % n]) for i in range(n)])

    def swap(self, x):
        return lax.ppermute(x, "seq", [(i, i ^ 1) for i in range(2 * self.chips)])

    def chip_turn(self, x, by):
        n = self.chips
        perm = [(2 * i + c, 2 * ((i + by) % n) + c) for i in range(n) for c in range(2)]
        return lax.ppermute(x, "seq", perm)

    def chip_pair(self, x, bit):
        n = self.chips
        perm = [(2 * i + c, 2 * (i ^ bit) + c) for i in range(n) for c in range(2)]
        return lax.ppermute(x, "seq", perm)

    def half(self, both, which):
        return lax.dynamic_index_in_dim(both, which, 0, keepdims=False)

    def gather(self, both):
        own = self.half(both, self.core)
        pieces = []
        forward = backward = own
        forwards, backwards = [], []
        for k in range(1, self.n // 2 + 1):
            forward = self.round(forward, 1)
            forwards.append(forward)
            if k <= (self.n - 1) // 2:
                backward = self.round(backward, -1)
                backwards.append(backward)
        pieces = forwards + backwards
        return Pieces(both, pieces, [self.swap(piece) for piece in pieces])

    def shard_order(self):
        order = [self.at(0)]
        order += [self.at(-k) for k in range(1, self.n // 2 + 1)]
        order += [self.at(k) for k in range(1, (self.n - 1) // 2 + 1)]
        return jnp.stack(order + [self.core]).astype(jnp.int32)

    def scatter(self, terms):
        theirs = self.swap(self.half(terms, 1 - self.core))
        mine = self.half(terms, self.core)

        def local(shard):
            return lax.dynamic_index_in_dim(mine, shard, 0, keepdims=False).astype(
                F32
            ) + lax.dynamic_index_in_dim(theirs, shard, 0, keepdims=False).astype(F32)

        forward = backward = None
        for k in range(self.n // 2, 0, -1):
            term = local(self.at(k))
            if forward is not None:
                term = term + forward.astype(F32)
            forward = self.round(term.astype(B16), 1)
            if k <= (self.n - 1) // 2:
                term = local(self.at(-k))
                if backward is not None:
                    term = term + backward.astype(F32)
                backward = self.round(term.astype(B16), -1)
        total = local(self.shard) + forward.astype(F32)
        if backward is not None:
            total = total + backward.astype(F32)
        bit = 1
        while bit < self.chips:
            low = total.astype(B16)
            total = low.astype(F32) + self.chip_pair(low, bit).astype(F32)
            bit *= 2
        other = self.swap(total)
        first = self.core == 0
        return jnp.stack([jnp.where(first, total, other), jnp.where(first, other, total)])

    def total(self, x):
        bit = 1
        while bit < self.n:
            x = x + lax.ppermute(x, "dp", [(i, i ^ bit) for i in range(self.n)])
            bit *= 2
        bit = 1
        while bit < self.chips:
            x = x + self.chip_pair(x, bit)
            bit *= 2
        return x + self.swap(x)


def halves_of(weight, width):
    rows = weight.shape[0]
    half = width // 2
    return jnp.transpose(weight.reshape(rows, 2, -1, half), (1, 2, 0, 3)).reshape(2, -1, half)


def local(
    tokens,
    cotangent,
    segment_ids,
    bucket_ids,
    key_mask,
    query_weight,
    key_weight,
    value_weight,
    output_weight,
    query_bias,
    value_bias,
    output_bias,
    first_gain,
    first_shift,
    mixed_gain,
    mixed_shift,
    up_weight,
    down_weight,
    up_bias,
    down_bias,
    second_gain,
    second_shift,
    inner_gain,
    inner_shift,
    bias_table,
    head_scale,
):
    items, own_rows, width = tokens.shape
    heads = head_scale.shape[0]
    head_width = width // heads
    groups = bias_table.shape[0] // 2
    factor = float(head_width) ** (-0.5)
    wide = up_weight.shape[1]
    rb = query_weight.shape[0]
    here = Places()
    n, chips = here.n, here.chips
    whole = items // chips
    left = items - whole * chips
    rows_a = whole * chips * own_rows
    rows_c = left * own_rows
    block = 256

    smalls = [
        query_bias,
        value_bias,
        output_bias,
        first_gain,
        first_shift,
        mixed_gain,
        mixed_shift,
        second_gain,
        second_shift,
        down_bias,
    ]
    wides = [up_bias, inner_gain, inner_shift]
    small = jnp.concatenate([v.reshape(1, rb) for v in smalls] + [v.reshape(-1, rb) for v in wides])
    small = jnp.pad(small, ((0, SMALL_ROWS - small.shape[0]), (0, width // 2 - rb)))
    bundle = jnp.concatenate(
        [halves_of(w, width) for w in (query_weight, key_weight, value_weight)]
        + [jnp.broadcast_to(small, (2,) + small.shape)],
        axis=1,
    )
    qkv_pieces = here.gather(bundle)
    idx = here.shard_order()
    bundle = jnp.concatenate([halves_of(output_weight, width), halves_of(up_weight, width)], axis=1)
    up_pieces = here.gather(bundle)
    down_pieces = here.gather(halves_of(down_weight, width))

    def take(array, by):
        mine = [
            lax.dynamic_index_in_dim(array, k * chips + lax.rem(here.chip + by, chips), 0, keepdims=False)
            for k in range(whole)
        ]
        return jnp.stack(mine)

    def collect(array):
        parts = [take(array, 0)]
        for by in range(1, chips):
            parts.append(here.chip_turn(take(array, by), by))
        return jnp.concatenate(parts, axis=1)

    def join(array):
        a = collect(array).reshape(rows_a, width)
        return jnp.concatenate([a, array[whole * chips :].reshape(rows_c, width)], axis=0)

    x = join(tokens)
    cot = join(cotangent)

    codes = bucket_ids + groups * segment_ids + 2 * groups * (key_mask > 0).astype(jnp.int32)
    turned = [codes] + [here.chip_turn(codes, by) for by in range(1, chips)]
    a_codes = jnp.concatenate([take(c, 0) for c in turned], axis=1)
    c_codes = jnp.concatenate([c[whole * chips :] for c in turned], axis=1)
    both = jnp.concatenate([a_codes, c_codes], axis=0)
    both = jnp.concatenate([both, here.swap(both)], axis=1)

    level = lax.broadcasted_iota(jnp.int32, (1, 1, LANES), 2) % (2 * groups)
    bucket = (both % groups)[:, :, None]
    hidden = (both // (2 * groups) == 0)[:, :, None]
    aux = jnp.where(
        level < groups,
        (bucket == level).astype(F32),
        jnp.where((level == groups) & hidden, FLOOR_SCORE, 0.0),
    ).astype(B16)
    aux_a, aux_c = aux[:whole], aux[whole:]
    own_codes = jnp.concatenate(
        [a_codes.reshape(rows_a), codes[whole * chips :].reshape(rows_c)], axis=0
    )
    hot = (
        (own_codes % (2 * groups))[:, None]
        == lax.broadcasted_iota(jnp.int32, (1, 2 * groups), 1)
    ).astype(B16)
    shifted = jnp.stack(
        [jnp.roll(bias_table.reshape(2, groups, heads), b, axis=1) for b in range(groups)], axis=1
    )
    shifted = shifted.reshape(2 * groups, groups, heads)
    tab = jnp.concatenate(
        [
            shifted,
            jnp.ones((2 * groups, 1, heads), B16),
            jnp.zeros((2 * groups, groups - 1, heads), B16),
        ],
        axis=1,
    )
    tab = tab.reshape(2 * groups, 2 * groups, heads // 2, 2)[:, :, :, ::-1]
    tab = jnp.transpose(tab, (0, 2, 3, 1)).reshape(2 * groups, width)

    normed, q, kv_a, kv_c, vec = project(x, qkv_pieces, idx, rb, rows_a, block, factor)
    ff = vec[len(smalls) : len(smalls) + 3 * (wide // width)]
    ff = ff.reshape(3, wide // width, n, rb).transpose(0, 2, 1, 3).reshape(3, wide)
    ff = jnp.pad(ff, ((0, 5), (0, 0)))
    scale = jnp.broadcast_to(jnp.repeat(head_scale.astype(F32), head_width)[None], (8, width))

    kv_c = kv_c.reshape(2, left, own_rows, width)
    kvs_c = [kv_c] + [here.chip_turn(kv_c, by) for by in range(1, chips)]
    kv_a = kv_a.reshape(2, whole, chips * own_rows, width)
    kvs_a = [kv_a, here.swap(kv_a)]
    kvs_c = kvs_c + [here.swap(kv) for kv in kvs_c]

    head_rows, logs_a = attend(q, kvs_a, aux_a, hot, tab, 0, chips * own_rows, None)
    head_rows, logs_c = attend(q, kvs_c, aux_c, hot, tab, rows_a, own_rows, head_rows)

    mixed, middle, second, inner, hat, slope, rate = feed_up(
        x, head_rows, vec, ff, scale, up_pieces, idx, rb, block
    )
    down_terms = down_side_grads(inner, cot, n, rb)
    result, pre, mid, branch, head_grad, acc, ff_acc = feed_down(
        cot,
        middle,
        inner,
        hat,
        slope,
        rate,
        head_rows,
        vec,
        ff,
        scale,
        up_pieces,
        down_pieces,
        idx,
        rb,
        block,
    )
    up_terms = side_grads([mixed, second], [(branch, None, 0, 1.0), (pre, None, 1, 1.0)], n, rb, "up_side")

    dq, own_c, other_c, g_c = attend_back(
        q, kvs_c, aux_c, hot, tab, head_grad, head_rows, logs_c, rows_a, own_rows, None
    )
    dq, own_a, other_a, g_a = attend_back(
        q, kvs_a, aux_a, hot, tab, head_grad, head_rows, logs_a, 0, chips * own_rows, dq
    )

    def add(*parts):
        return sum(p.astype(F32) for p in parts)

    dkv_a = add(own_a, here.swap(other_a)).astype(B16).reshape(2, rows_a, width)
    near = add(own_c, here.swap(other_c)).astype(B16).reshape(2, left, chips, own_rows, width)
    parts = [near[:, :, 0]] + [here.chip_turn(near[:, :, by], -by) for by in range(1, chips)]
    dkv_c = add(*parts).astype(B16).reshape(2, rows_c, width)
    dkv = jnp.concatenate([dkv_a, dkv_c], axis=1)

    qkv_terms = side_grads(
        [normed], [(dq, None, 0, factor), (dkv, 0, 0, 1.0), (dkv, 1, 0, 1.0)], n, rb, "qkv_side"
    )
    grad_rows, late = project_back(x, dq, dkv, mid, vec, qkv_pieces, idx, rb, block, factor)

    down_sum = here.scatter(down_terms)
    up_sum = here.scatter(up_terms)
    qkv_sum = here.scatter(qkv_terms)

    def whole_rows(pair):
        return jnp.transpose(pair, (2, 0, 1, 3)).reshape(rb, -1)

    down_weight_grad = jnp.transpose(down_sum, (1, 2, 0, 3)).reshape(-1, width)
    output_weight_grad = whole_rows(up_sum[:, :1])
    up_weight_grad = whole_rows(up_sum[:, 1:])
    query_weight_grad, key_weight_grad, value_weight_grad = [
        whole_rows(qkv_sum[:, t : t + 1]) for t in range(3)
    ]

    g = jnp.sum(g_c, axis=0) + jnp.sum(g_a, axis=0)
    g = g.reshape(heads // 2, 2, 2 * groups, 2 * groups)[:, ::-1, :groups]
    g = g.reshape(heads, groups, 2, groups)
    offset = jnp.arange(groups)
    spread = (
        (offset[:, None, None] - offset[None, :, None]) % groups == offset[None, None, :]
    ).astype(F32)
    table = jnp.einsum("hcsb,cbo->soh", g, spread, precision=lax.Precision.HIGHEST)
    summed = here.total(
        jnp.concatenate(
            [
                acc[:7],
                late[:4],
                ff_acc[:3].reshape(-1, width),
                table.reshape(-1, width),
                jnp.zeros((1, width), F32),
            ]
        )
    )
    mine = lax.dynamic_slice_in_dim(summed[:11], here.shard * rb, rb, axis=1)
    wide_rows = wide // width
    ff_sums = summed[11 : 11 + 3 * wide_rows].reshape(3, wide)
    ff_mine = lax.dynamic_slice_in_dim(ff_sums, here.shard * (wide // n), wide // n, axis=1)
    table_grad = summed[11 + 3 * wide_rows].reshape(2 * groups, heads)
    scale_grad = jnp.sum(summed[6].reshape(heads, head_width), axis=1)

    def home(array, kind):
        a = array[:rows_a].reshape(whole, chips, own_rows, width)
        parts = [a[:, 0].astype(array.dtype)]
        for by in range(1, chips):
            parts.append(here.chip_turn(a[:, by].astype(B16), -by).astype(array.dtype))
        parts = jnp.stack(parts)
        order = lax.rem(jnp.arange(chips) - here.chip + chips, chips)
        parts = jnp.take(parts, order, axis=0)
        out = jnp.transpose(parts, (1, 0, 2, 3)).reshape(whole * chips, own_rows, width)
        return jnp.concatenate([out, array[rows_a:].reshape(left, own_rows, width)], axis=0)

    return (
        home(result, B16),
        home(grad_rows, F32),
        query_weight_grad,
        key_weight_grad,
        value_weight_grad,
        output_weight_grad,
        mine[9],
        mine[10],
        mine[2],
        mine[7],
        mine[8],
        mine[4],
        mine[5],
        up_weight_grad,
        down_weight_grad,
        ff_mine[0],
        mine[3],
        mine[0],
        mine[1],
        ff_mine[1],
        ff_mine[2],
        table_grad,
        scale_grad,
    )


def solution(mesh):
    rowed, shard, vector, whole = P("dp", "seq", None), P("dp", None), P("dp"), P()
    flat = P("dp", "seq")
    placed = (rowed,) * 2 + (flat,) * 3 + (shard,) * 4 + (vector,) * 7 + (shard,) * 2 + (vector,) * 6
    placed = placed + (whole,) * 2
    outs = (rowed,) * 2 + (shard,) * 4 + (vector,) * 7 + (shard,) * 2 + (vector,) * 6 + (whole,) * 2
    return jax.shard_map(local, mesh=mesh, in_specs=placed, out_specs=outs, check_vma=False)
```

```python
from functools import partial

import jax
import jax.numpy as jnp
from jax import lax
from jax.experimental import pallas as pl
from jax.experimental.pallas import tpu as pltpu
from jax.sharding import PartitionSpec as P

EPSILON = 1e-05
FLOOR_SCORE = -1e30
F32 = jnp.float32
B16 = jnp.bfloat16
NN = (((1,), (0,)), ((), ()))
NT = (((1,), (1,)), ((), ()))
TN = (((0,), (0,)), ((), ()))
VMEM_LIMIT = 58 * 1024 * 1024
SMALL_ROWS = 32
LANES = 128


def dot(a, b, dims, **kw):
    return lax.dot_general(a, b, dims, preferred_element_type=F32, **kw)


def params():
    return pltpu.CompilerParams(vmem_limit_bytes=VMEM_LIMIT)


def cost(micros):
    return pl.CostEstimate(flops=int(micros * 1.1e9), bytes_accessed=0, transcendentals=0)


def low_lanes(shape):
    return lax.broadcasted_iota(jnp.int32, shape, 1) < shape[1] // 2


def low_rows(shape):
    return lax.broadcasted_iota(jnp.int32, shape, 0) < shape[0] // 2


def standardise(values):
    mean = jnp.mean(values, axis=-1, keepdims=True)
    centred = values - mean
    spread = jnp.mean(centred * centred, axis=-1, keepdims=True)
    rate = lax.rsqrt(spread + EPSILON)
    return centred * rate, rate


def standard_back(hat_grad, hat, rate):
    first = jnp.mean(hat_grad, axis=-1, keepdims=True)
    second = jnp.mean(hat_grad * hat, axis=-1, keepdims=True)
    return rate * (hat_grad - first - hat * second)


def add(*parts):
    return sum(p.astype(F32) for p in parts)


def sums(array):
    return jnp.sum(array, axis=0, keepdims=True)


SPOT, CORE, CHIP, SHARD, GROUP = range(5)
GROUPS = 4


def ring_at(spot, n):
    spot = lax.rem(spot + 2 * n, n)
    return jnp.where(spot < (n + 1) // 2, 2 * spot, 2 * n - 1 - 2 * spot)


def piece_shards(ids, n):
    spot = ids[SPOT]
    out = [ids[SHARD]]
    out += [ring_at(spot - k, n) for k in range(1, n // 2 + 1)]
    out += [ring_at(spot + k, n) for k in range(1, (n - 1) // 2 + 1)]
    return out


def wait_whole(target, sem):
    pltpu.make_async_copy(target, target, sem).wait()


ANYWHERE = pl.BlockSpec(memory_space=pl.ANY)


def pack_near_kernel(ids_ref, q_ref, k_ref, v_ref, small_ref, near_ref):
    rb = q_ref.shape[0]
    for t, ref in enumerate((q_ref, k_ref, v_ref)):
        near_ref[t * rb : (t + 1) * rb, :] = ref[...]
    near_ref[3 * rb :, :] = jnp.zeros((SMALL_ROWS, near_ref.shape[1]), B16)
    near_ref[3 * rb :, 0:LANES] = small_ref[...]


def pack_near(ids, qkv, small):
    rb, width = qkv[0].shape
    half = width // 2
    return pl.pallas_call(
        pack_near_kernel,
        grid_spec=pltpu.PrefetchScalarGridSpec(
            num_scalar_prefetch=1,
            grid=(1,),
            in_specs=[pl.BlockSpec((rb, half), lambda i, s: (0, s[CORE]))] * 3
            + [pl.BlockSpec(small.shape, lambda i, s: (0, 0))],
            out_specs=pl.BlockSpec((3 * rb + SMALL_ROWS, half), lambda i, s: (0, 0)),
        ),
        out_shape=jax.ShapeDtypeStruct((3 * rb + SMALL_ROWS, half), B16),
        compiler_params=params(),
        cost_estimate=cost(2),
        name="pack_near",
    )(ids, *qkv, small)


def pack_far_kernel(ids_ref, up_ref, down_ref, o_ref, first_ref, second_ref):
    part = up_ref.shape[1]
    first_ref[:, 0:part] = up_ref[...]
    first_ref[:, part:] = o_ref[...]
    second_ref[...] = down_ref[...]


def output_lanes(width):
    return 2 * LANES if width % (2 * LANES) == 0 else LANES


def pack_far(ids, up, down, out):
    rb, width = out.shape
    part = up.shape[1] // GROUPS
    lanes = output_lanes(width)
    last = width // lanes - 1
    return pl.pallas_call(
        pack_far_kernel,
        grid_spec=pltpu.PrefetchScalarGridSpec(
            num_scalar_prefetch=1,
            grid=(1,),
            in_specs=[
                pl.BlockSpec((rb, part), lambda i, s: (0, s[GROUP])),
                pl.BlockSpec((rb, width), lambda i, s: (s[GROUP], 0)),
                pl.BlockSpec((rb, lanes), lambda i, s: (0, jnp.minimum(s[GROUP], last))),
            ],
            out_specs=[
                pl.BlockSpec((rb, part + lanes), lambda i, s: (0, 0)),
                pl.BlockSpec((rb, width), lambda i, s: (0, 0)),
            ],
        ),
        out_shape=[
            jax.ShapeDtypeStruct((rb, part + lanes), B16),
            jax.ShapeDtypeStruct((rb, width), B16),
        ],
        compiler_params=params(),
        cost_estimate=cost(2),
        name="pack_far",
    )(ids, up, down, out)


def prep_kernel(chips, whole, left, ids_ref, *refs):
    code_refs = refs[: 2 * chips]
    table_ref, scale_in_ref = refs[2 * chips : 2 * chips + 2]
    aux_ref, hot_ref, tab_ref, scale_ref = refs[2 * chips + 2 :]
    rows = code_refs[0].shape[1]
    levels = tab_ref.shape[0] // 2
    width = tab_ref.shape[1]
    chip = ids_ref[CHIP]

    def column(item, source):
        code = code_refs[source][pl.ds(item, 1), :]
        level = lax.broadcasted_iota(jnp.int32, (LANES, rows), 0) % (2 * levels)
        hit = jnp.where(level == code % levels, 1.0, 0.0)
        floor = jnp.where((level == levels) & (code < 2 * levels), FLOOR_SCORE, 0.0)
        return jnp.transpose(jnp.where(level < levels, hit, floor)).astype(B16)

    def own(item, source):
        code = code_refs[source][pl.ds(item, 1), :]
        level = lax.broadcasted_iota(jnp.int32, (LANES, rows), 0)
        hit = jnp.where(level == code % (2 * levels), 1.0, 0.0)
        return jnp.transpose(hit).astype(B16)[:, : 2 * levels]

    for item in range(whole + left):
        row = item * chips + chip if item < whole else whole * chips + item - whole
        for source in range(2 * chips):
            aux_ref[item, source * rows : (source + 1) * rows, :] = column(row, source)
    for k in range(whole):
        for source in range(chips):
            start = (k * chips + source) * rows
            hot_ref[start : start + rows, :] = own(k * chips + chip, source)
    for k in range(left):
        start = (whole * chips + k) * rows
        hot_ref[start : start + rows, :] = own(whole * chips + k, 0)

    head = lax.broadcasted_iota(jnp.int32, (LANES, width), 0)
    lane = lax.broadcasted_iota(jnp.int32, (LANES, width), 1)
    owner = lane // LANES * 2 + 1 - lane % LANES // (LANES // 2)
    spread = jnp.where(head == owner, 1.0, 0.0).astype(B16)
    by_lane = dot(table_ref[...], spread, NN)
    lane = lax.broadcasted_iota(jnp.int32, (levels, width), 1) % (2 * levels)
    bucket = lax.broadcasted_iota(jnp.int32, (levels, width), 0)
    turn = jnp.where(lane < levels, (lane - bucket) & (levels - 1), -1)
    for segment in range(2):
        out = jnp.where(lane == levels, 1.0, 0.0)
        for o in range(levels):
            line = by_lane[segment * levels + o : segment * levels + o + 1, :]
            out = jnp.where(turn == o, line, out)
        tab_ref[segment * levels : (segment + 1) * levels, :] = out.astype(B16)
    lane = lax.broadcasted_iota(jnp.int32, (LANES, width), 1)
    spread = jnp.where(head == lane // (LANES // 2), 1.0, 0.0).astype(B16)
    scale_ref[...] = dot(scale_in_ref[...], spread, NN)


def prep(ids, codes, table, head_scale, chips, whole, left, width):
    rows = codes[0].shape[1]
    table = jnp.pad(table, ((0, 0), (0, LANES - table.shape[1])))
    scale = jnp.pad(head_scale[None], ((0, 15), (0, LANES - head_scale.shape[0])))
    levels = table.shape[0]
    q_rows = (whole * chips + left) * rows

    def fixed(shape):
        return pl.BlockSpec(shape, lambda i, s: (0,) * len(shape))

    outs = [(whole + left, 2 * chips * rows, LANES), (q_rows, levels), (levels, width), (16, width)]
    return pl.pallas_call(
        partial(prep_kernel, chips, whole, left),
        grid_spec=pltpu.PrefetchScalarGridSpec(
            num_scalar_prefetch=1,
            grid=(1,),
            in_specs=[fixed(c.shape) for c in codes] + [fixed(table.shape), fixed(scale.shape)],
            out_specs=[fixed(o) for o in outs],
        ),
        out_shape=[
            jax.ShapeDtypeStruct(outs[0], B16),
            jax.ShapeDtypeStruct(outs[1], B16),
            jax.ShapeDtypeStruct(outs[2], B16),
            jax.ShapeDtypeStruct(outs[3], F32),
        ],
        compiler_params=params(),
        cost_estimate=cost(3),
        name="prep",
    )(ids, *codes, table, scale)


def load_qkv(ids_ref, n, rb, half, own, mine, other, targets, sems):
    shards = piece_shards(ids_ref, n)
    core = ids_ref[CORE]
    starts = [pl.multiple_of(shard * rb, 16) for shard in shards]
    here = pl.multiple_of(core * half, LANES)
    there = pl.multiple_of((1 - core) * half, LANES)
    for t, target in enumerate(targets):
        pltpu.make_async_copy(own[t], target.at[pl.ds(starts[0], rb), :], sems.at[t]).start()
        for j in range(n - 1):
            rows = pl.ds(starts[j + 1], rb)
            part = pl.ds(t * rb, rb)
            pltpu.make_async_copy(
                mine[j].at[part, :], target.at[rows, pl.ds(here, half)], sems.at[t]
            ).start()
            pltpu.make_async_copy(
                other[j].at[part, :], target.at[rows, pl.ds(there, half)], sems.at[t]
            ).start()


def project_kernel(n, chips, chunks_a, factor, ids_ref, x_ref, *refs):
    recv = refs[: chips - 1]
    refs = refs[chips - 1 :]
    own, own_small = refs[:3], refs[3]
    mine, other = refs[4 : 4 + n - 1], refs[4 + n - 1 : 4 + 2 * (n - 1)]
    refs = refs[4 + 2 * (n - 1) :]
    x_out, normed_ref, q_ref, kva_ref, kvc_ref, vec_ref = refs[:6]
    wq, wk, wv, small, sems = refs[6:]
    rb = own[0].shape[0]
    half = wq.shape[1] // 2
    step = pl.program_id(0)

    @pl.when(step == 0)
    def _():
        pltpu.make_async_copy(own_small, small.at[0], sems.at[3]).start()
        for j in range(n - 1):
            pltpu.make_async_copy(
                mine[j].at[pl.ds(3 * rb, SMALL_ROWS), pl.ds(0, LANES)], small.at[j + 1], sems.at[3]
            ).start()
        load_qkv(ids_ref, n, rb, half, own, mine, other, (wq, wk, wv), sems)
        wait_whole(small, sems.at[3])
        total = jnp.zeros(vec_ref.shape, F32)
        row = lax.broadcasted_iota(jnp.int32, (LANES, wq.shape[1]), 0)
        col = lax.broadcasted_iota(jnp.int32, (LANES, wq.shape[1]), 1)
        for j, shard in enumerate(piece_shards(ids_ref, n)):
            spot = jnp.where((row < rb) & (col == row + shard * rb), 1.0, 0.0).astype(B16)
            total = total + dot(small[j], spot, NN)
        vec_ref[...] = total
        for t, target in enumerate((wq, wk, wv)):
            wait_whole(target, sems.at[t])

    x = x_ref[0]
    for s in range(1, chips):
        x = jnp.where((step < chunks_a) & (lax.rem(step, chips) == s), recv[s - 1][0], x)
    x_out[...] = x
    hat, _ = standardise(x.astype(F32))
    normed = (hat * vec_ref[3:4, :] + vec_ref[4:5, :]).astype(B16)
    normed_ref[...] = normed
    q_ref[...] = ((dot(normed, wq[...], NN) + vec_ref[0:1, :]) * factor).astype(B16)
    keys = dot(normed, wk[...], NN).astype(B16)
    values = (dot(normed, wv[...], NN) + vec_ref[1:2, :]).astype(B16)

    @pl.when(step < chunks_a)
    def _():
        kva_ref[0] = keys
        kva_ref[1] = values

    @pl.when(step >= chunks_a)
    def _():
        kvc_ref[0] = keys
        kvc_ref[1] = values


def project(ids, tokens, recv, own, small, mine, other, n, chips, whole, factor):
    items, rows, width = tokens.shape
    chunks_a = whole * chips
    rowed = pl.BlockSpec((rows, width), lambda i, s: (i, 0))

    def item(i, s):
        own_item = jnp.minimum(i, chunks_a - 1) // chips * chips + s[CHIP]
        return (jnp.where(i < chunks_a, own_item, i), 0, 0)

    received = pl.BlockSpec((1, rows, width), lambda i, s: (jnp.minimum(i, chunks_a - 1) // chips, 0, 0))
    total = items * rows
    return pl.pallas_call(
        partial(project_kernel, n, chips, chunks_a, factor),
        grid_spec=pltpu.PrefetchScalarGridSpec(
            num_scalar_prefetch=1,
            grid=(items,),
            in_specs=[pl.BlockSpec((1, rows, width), item)]
            + [received] * len(recv)
            + [ANYWHERE] * (4 + 2 * (n - 1)),
            out_specs=[
                rowed,
                rowed,
                rowed,
                pl.BlockSpec((2, rows, width), lambda i, s: (0, jnp.minimum(i, chunks_a - 1), 0)),
                pl.BlockSpec((2, rows, width), lambda i, s: (0, jnp.maximum(i - chunks_a, 0), 0)),
                pl.BlockSpec((SMALL_ROWS, width), lambda i, s: (0, 0)),
            ],
            scratch_shapes=[pltpu.VMEM((width, width), B16)] * 3
            + [pltpu.VMEM((n,) + small.shape, B16), pltpu.SemaphoreType.DMA((4,))],
        ),
        out_shape=[
            jax.ShapeDtypeStruct((total, width), B16),
            jax.ShapeDtypeStruct((total, width), B16),
            jax.ShapeDtypeStruct((total, width), B16),
            jax.ShapeDtypeStruct((2, chunks_a * rows, width), B16),
            jax.ShapeDtypeStruct((2, total - chunks_a * rows, width), B16),
            jax.ShapeDtypeStruct((SMALL_ROWS, width), F32),
        ],
        compiler_params=params(),
        cost_estimate=cost(10),
        name="project",
    )(ids, tokens, *recv, *own, small, *mine, *other)


def home_index(chips, chunks_a):
    def at(i, s):
        k, by = i // chips, lax.rem(i, chips)
        return (jnp.where(i < chunks_a, k * chips + lax.rem(s[CHIP] + by, chips), i), 0, 0)

    return at


def away_spec(rows, width, chips, chunks_a):
    return pl.BlockSpec((1, rows, width), lambda i, s: (jnp.minimum(i, chunks_a - 1) // chips, 0, 0))


def write_away(refs, step, chips, chunks_a, value):
    for s, ref in enumerate(refs, 1):

        @pl.when((step < chunks_a) & (lax.rem(step, chips) == s))
        def _(ref=ref):
            ref[0] = value.astype(ref.dtype)


def project_back_kernel(n, chips, chunks_a, first, fresh, parts, factor, ids_ref, x_ref, dq_ref, mid_ref, vec_ref, *refs):
    dkv_refs, refs = refs[:parts], refs[parts:]
    own = refs[:3]
    mine, other = refs[3 : 3 + n - 1], refs[3 + n - 1 : 3 + 2 * (n - 1)]
    refs = refs[3 + 2 * (n - 1) :]
    if not fresh:
        refs = refs[1:]
    out_ref, acc_ref = refs[:2]
    away = refs[2:-4]
    wq, wk, wv, sems = refs[-4:]
    rb, half = own[0].shape[0], wq.shape[1] // 2
    step = pl.program_id(0) + first

    @pl.when(step == first)
    def _():
        load_qkv(ids_ref, n, rb, half, own, mine, other, (wq, wk, wv), sems)
        acc_ref[...] = jnp.zeros_like(acc_ref)
        for t, target in enumerate((wq, wk, wv)):
            wait_whole(target, sems.at[t])

    dq = dq_ref[...]
    dk, dv = [add(*[r[t] for r in dkv_refs]).astype(B16) for t in range(2)]
    grad = factor * dot(dq, wq[...], NT) + dot(dk, wk[...], NT) + dot(dv, wv[...], NT)
    hat, rate = standardise(x_ref[...].astype(F32))
    out = mid_ref[...] + standard_back(grad * vec_ref[3:4, :], hat, rate)
    out_ref[0] = out
    if first < chunks_a:
        write_away(away, step, chips, chunks_a, out)
    acc_ref[0:1, :] += sums(grad * hat)
    acc_ref[1:2, :] += sums(grad)
    acc_ref[2:3, :] += factor * sums(dq.astype(F32))
    acc_ref[3:4, :] += sums(dv.astype(F32))


def project_back(ids, x, dq, dkvs, mid, vec, own, mine, other, n, chips, whole, rows, factor, span, into):
    total, width = x.shape
    items, chunks_a = total // rows, whole * chips
    first, count = span
    rowed = pl.BlockSpec((rows, width), lambda i, s: (first + i, 0))
    at = home_index(chips, chunks_a)
    fresh = into is None
    away = chips - 1 if first < chunks_a else 0
    n_args = 5 + len(dkvs) + 3 + 2 * (n - 1)
    return pl.pallas_call(
        partial(project_back_kernel, n, chips, chunks_a, first, fresh, len(dkvs), factor),
        grid_spec=pltpu.PrefetchScalarGridSpec(
            num_scalar_prefetch=1,
            grid=(count,),
            in_specs=[
                rowed,
                rowed,
                rowed,
                pl.BlockSpec(vec.shape, lambda i, s: (0, 0)),
            ]
            + [pl.BlockSpec((2, rows, width), lambda i, s: (0, i, 0))] * len(dkvs)
            + [ANYWHERE] * (3 + 2 * (n - 1) + (0 if fresh else 1)),
            out_specs=[
                pl.BlockSpec((1, rows, width), lambda i, s: at(first + i, s)),
                pl.BlockSpec((8, width), lambda i, s: (0, 0)),
            ]
            + [away_spec(rows, width, chips, chunks_a)] * away,
            scratch_shapes=[pltpu.VMEM((width, width), B16)] * 3 + [pltpu.SemaphoreType.DMA((3,))],
        ),
        out_shape=[
            jax.ShapeDtypeStruct((items, rows, width), F32),
            jax.ShapeDtypeStruct((8, width), F32),
        ]
        + [jax.ShapeDtypeStruct((whole, rows, width), B16)] * away,
        input_output_aliases={} if fresh else {n_args: 0},
        compiler_params=params(),
        cost_estimate=cost(8),
        name="project_back",
    )(ids, x, dq, mid, vec, *dkvs, *own, *mine, *other, *([] if fresh else [into]))


def score_operands(qp, kp, aux, hot, tab):
    rel = dot(hot, tab, NN).astype(B16)
    lq, lk = low_lanes(qp.shape), low_lanes(kp.shape)
    return (
        (jnp.where(lq, qp, rel), jnp.where(lk, kp, aux)),
        (jnp.where(lq, rel, qp), jnp.where(lk, aux, kp)),
    )


def attend_kernel(n_kv, q_ref, aux_ref, hot_ref, tab_ref, *refs):
    kv_refs = refs[:n_kv]
    o_ref, l_ref = refs[-2:]
    qp = q_ref[...]
    kp = jnp.concatenate([r[0, 0] for r in kv_refs], axis=0)
    vp = jnp.concatenate([r[1, 0] for r in kv_refs], axis=0)
    outs = []
    for h, (qh, kh) in enumerate(score_operands(qp, kp, aux_ref[0], hot_ref[...], tab_ref[...])):
        scores = dot(kh, qh, NT)
        top = jnp.max(scores, axis=0, keepdims=True)
        exponent = jnp.exp(scores - top)
        total = jnp.sum(exponent, axis=0, keepdims=True)
        out = dot(vp, exponent.astype(B16), TN)
        outs.append(out * (1.0 / total))
        l_ref[0, 0, h : h + 1, :] = top + jnp.log(total)
    o_ref[...] = jnp.transpose(jnp.where(low_rows(outs[0].shape), outs[0], outs[1]))


def attend(q, kvs, aux, hot, tab, item_start, row_start, q_rows, items, into):
    rows, width = q.shape
    keys = aux.shape[1]
    pairs = width // LANES
    first = row_start // q_rows
    rowed = pl.BlockSpec((q_rows, LANES), lambda i, p: (first + i, p))
    args = [q, aux, hot, tab] + list(kvs)
    specs = [
        rowed,
        pl.BlockSpec((1, keys, LANES), lambda i, p: (item_start + i, 0, 0)),
        pl.BlockSpec((q_rows, hot.shape[1]), lambda i, p: (first + i, 0)),
        pl.BlockSpec((tab.shape[0], LANES), lambda i, p: (0, p)),
    ] + [pl.BlockSpec((2, 1, kv.shape[2], LANES), lambda i, p: (0, i, 0, p)) for kv in kvs]
    aliases = {}
    if into is not None:
        aliases = {len(args): 0}
        args.append(into)
        specs.append(ANYWHERE)
    return pl.pallas_call(
        partial(attend_kernel, len(kvs)),
        grid=(items, pairs),
        in_specs=specs,
        out_specs=[rowed, pl.BlockSpec((1, 1, 8, q_rows), lambda i, p: (i, p, 0, 0))],
        out_shape=[
            jax.ShapeDtypeStruct((rows, width), F32),
            jax.ShapeDtypeStruct((items, pairs, 8, q_rows), F32),
        ],
        input_output_aliases=aliases,
        compiler_params=params(),
        cost_estimate=cost(14),
        name="attend",
    )(*args)


def attend_back_kernel(n_kv, q_ref, aux_ref, hot_ref, tab_ref, do_ref, o_ref, l_ref, *refs):
    kv_refs = refs[:n_kv]
    dq_ref, own_ref, other_ref, g_ref = refs[-4:]
    qp, dop, hot = q_ref[...], do_ref[...], hot_ref[...]
    kp = jnp.concatenate([r[0, 0] for r in kv_refs], axis=0)
    vp = jnp.concatenate([r[1, 0] for r in kv_refs], axis=0)
    lk = low_lanes(kp.shape)
    zero = jnp.zeros_like(vp)
    product = dop.astype(F32) * o_ref[...]
    row = lax.broadcasted_iota(jnp.int32, (8, LANES), 0)
    pick = jnp.where(low_lanes((8, LANES)) == (row == 0), 1.0, 0.0)
    row_dot = dot(pick, product, NT, precision=lax.Precision.HIGHEST)
    dvs, dks, dqs = [], [], []
    operands = score_operands(qp, kp, aux_ref[0], hot, tab_ref[...])
    for h, (qh, kh) in enumerate(operands):
        vh = jnp.where(lk, vp, zero) if h == 0 else jnp.where(lk, zero, vp)
        probs = jnp.exp(dot(kh, qh, NT) - l_ref[0, 0, h : h + 1, :])
        score_grad = (probs * (dot(vh, dop, NT) - row_dot[h : h + 1, :])).astype(B16)
        dvs.append(dot(probs.astype(B16), dop, NN))
        dks.append(dot(score_grad, qp, NN))
        dqs.append(dot(kh, score_grad, TN))
    dk = jnp.where(lk, dks[0], dks[1]).astype(B16)
    dv = jnp.where(lk, dvs[0], dvs[1]).astype(B16)
    half = own_ref.shape[2]
    own_ref[0, 0], own_ref[1, 0] = dk[:half], dv[:half]
    other_ref[0, 0], other_ref[1, 0] = dk[half:], dv[half:]
    lr = low_rows(dqs[0].shape)
    dq_ref[...] = jnp.transpose(jnp.where(lr, dqs[0], dqs[1])).astype(B16)
    levels = jnp.where(lr, dqs[1], dqs[0])
    upper = levels.astype(B16)
    lower = (levels - upper.astype(F32)).astype(B16)
    g_ref[0, 0] = dot(upper, hot, NN) + dot(lower, hot, NN)


def attend_back(
    q, kvs, aux, hot, tab, head_grad, head_rows, logs, item_start, row_start, q_rows, items, span, into
):
    rows, width = q.shape
    keys = aux.shape[1]
    p0, pairs = span
    first = row_start // q_rows
    rowed = pl.BlockSpec((q_rows, LANES), lambda i, p: (first + i, p0 + p))
    args = [q, aux, hot, tab, head_grad, head_rows, logs] + list(kvs)
    specs = [
        rowed,
        pl.BlockSpec((1, keys, LANES), lambda i, p: (item_start + i, 0, 0)),
        pl.BlockSpec((q_rows, hot.shape[1]), lambda i, p: (first + i, 0)),
        pl.BlockSpec((tab.shape[0], LANES), lambda i, p: (0, p0 + p)),
        rowed,
        rowed,
        pl.BlockSpec((1, 1, 8, q_rows), lambda i, p: (i, p0 + p, 0, 0)),
    ] + [pl.BlockSpec((2, 1, kv.shape[2], LANES), lambda i, p: (0, i, 0, p0 + p)) for kv in kvs]
    aliases = {}
    if into is not None:
        aliases = {len(args): 0}
        args.append(into)
        specs.append(ANYWHERE)
    half = pl.BlockSpec((2, 1, keys // 2, LANES), lambda i, p: (0, i, 0, p))
    half_shape = jax.ShapeDtypeStruct((2, items, keys // 2, pairs * LANES), B16)
    return pl.pallas_call(
        partial(attend_back_kernel, len(kvs)),
        grid=(items, pairs),
        in_specs=specs,
        out_specs=[
            rowed,
            half,
            half,
            pl.BlockSpec((1, 1, LANES, hot.shape[1]), lambda i, p: (i, p, 0, 0)),
        ],
        out_shape=[
            jax.ShapeDtypeStruct((rows, width), B16),
            half_shape,
            half_shape,
            jax.ShapeDtypeStruct((items, pairs, LANES, hot.shape[1]), F32),
        ],
        input_output_aliases=aliases,
        compiler_params=params(),
        cost_estimate=cost(8),
        name="attend_back",
    )(*args)


CHUNK = 64


def gelu_parts(v):
    mass = 0.5 + 0.5 * lax.erf(v * 0.7071067811865476)
    bell = jnp.exp2(v * v * -0.7213475204444817)
    return v * mass, mass + v * (bell * 0.3989422804014327)


def tiles(width):
    return [slice(k, k + LANES) for k in range(0, width, LANES)]


def row_mean(stat, width):
    mean = jnp.sum(stat[...], axis=1, keepdims=True) * (1.0 / width)
    return jnp.broadcast_to(mean, stat.shape)


def chunk_rows(c):
    return pl.ds(pl.multiple_of(c * CHUNK, CHUNK), CHUNK)


def load_up(far, n, rb, wo, wu, sems):
    group = far.shape[0] // n
    width = wo.shape[0]
    part = wu.shape[1] // GROUPS
    lanes = output_lanes(width)
    for shard in range(n):
        rows = pl.ds(shard * rb, rb)
        for g in range(width // lanes):
            pltpu.make_async_copy(
                far.at[shard * group + g, :, pl.ds(part, lanes)],
                wo.at[rows, pl.ds(g * lanes, lanes)],
                sems.at[0],
            ).start()
        for g in range(GROUPS):
            pltpu.make_async_copy(
                far.at[shard * group + g, :, pl.ds(0, part)],
                wu.at[rows, pl.ds(g * part, part)],
                sems.at[1],
            ).start()


def load_down(far, n, rb, wd, sem):
    group = far.shape[0] // n
    for shard in range(n):
        for g in range(GROUPS):
            pltpu.make_async_copy(
                far.at[shard * group + g], wd.at[pl.ds((shard * GROUPS + g) * rb, rb), :], sem
            ).start()


def up_kernel(n, x_ref, o_ref, vec_ref, ff_ref, scale_ref, far_ref, *refs):
    mixed_ref, middle_ref, second_ref, inner_ref, hat_ref, slope_ref, rate_ref = refs[:7]
    wo, wu, pre, stat, means, sems = refs[7:]
    rb = far_ref.shape[1]
    step = pl.program_id(0)

    @pl.when(step == 0)
    def _():
        load_up(far_ref, n, rb, wo, wu, sems)

    hat, _ = standardise(o_ref[...] * scale_ref[0:1, :])
    mixed = (hat * vec_ref[5:6, :] + vec_ref[6:7, :]).astype(B16)
    mixed_ref[...] = mixed

    @pl.when(step == 0)
    def _():
        wait_whole(wo, sems.at[0])

    middle = x_ref[...].astype(F32) + dot(mixed, wo[...], NN) + vec_ref[2:3, :]
    middle_ref[...] = middle
    hat, _ = standardise(middle)
    second = (hat * vec_ref[7:8, :] + vec_ref[8:9, :]).astype(B16)
    second_ref[...] = second

    @pl.when(step == 0)
    def _():
        wait_whole(wu, sems.at[1])

    pre[...] = dot(second, wu[...], NN)

    chunks, wide = pre.shape[0] // CHUNK, pre.shape[1]

    @pl.loop(0, chunks)
    def _(c):
        rows = chunk_rows(c)
        total = jnp.zeros((CHUNK, LANES), F32)
        for lanes in tiles(wide):
            active, slope = gelu_parts(pre[rows, lanes] + ff_ref[0:1, lanes])
            slope_ref[rows, lanes] = slope.astype(B16)
            pre[rows, lanes] = active
            total = total + active
        stat[rows, :] = total

    means[...] = row_mean(stat, wide)

    @pl.loop(0, chunks)
    def _(c):
        rows = chunk_rows(c)
        mean = means[rows, :]
        total = jnp.zeros((CHUNK, LANES), F32)
        for lanes in tiles(wide):
            centred = pre[rows, lanes] - mean
            total = total + centred * centred
        stat[rows, :] = total

    rate_ref[...] = lax.rsqrt(row_mean(stat, wide) + EPSILON)

    @pl.loop(0, chunks)
    def _(c):
        rows = chunk_rows(c)
        mean, rate = means[rows, :], rate_ref[rows, :]
        for lanes in tiles(wide):
            hat = (pre[rows, lanes] - mean) * rate
            hat_ref[rows, lanes] = hat.astype(B16)
            inner_ref[rows, lanes] = (hat * ff_ref[1:2, lanes] + ff_ref[2:3, lanes]).astype(B16)


def feed_up(x, head_rows, vec, ff, scale, far, n, block):
    rows, width = x.shape
    wide = ff.shape[1]

    def rowed(lanes):
        return pl.BlockSpec((block, lanes), lambda i: (i, 0))

    def fixed(shape):
        return pl.BlockSpec(shape, lambda i: (0, 0))

    lanes = [width, width, width, wide, wide, wide, LANES]
    kinds = [B16, F32, B16, B16, B16, B16, F32]
    return pl.pallas_call(
        partial(up_kernel, n),
        grid=(rows // block,),
        in_specs=[rowed(width), rowed(width), fixed(vec.shape), fixed(ff.shape), fixed(scale.shape), ANYWHERE],
        out_specs=[rowed(k) for k in lanes],
        scratch_shapes=[
            pltpu.VMEM((width, width), B16),
            pltpu.VMEM((width, wide), B16),
            pltpu.VMEM((block, wide), F32),
            pltpu.VMEM((block, LANES), F32),
            pltpu.VMEM((block, LANES), F32),
            pltpu.SemaphoreType.DMA((2,)),
        ],
        out_shape=[jax.ShapeDtypeStruct((rows, k), kind) for k, kind in zip(lanes, kinds)],
        compiler_params=params(),
        cost_estimate=cost(22),
        name="feed_up",
    )(x, head_rows, vec, ff, scale, far)


def down_kernel(
    n,
    chips,
    chunks_a,
    ids_ref,
    cot_ref,
    middle_ref,
    inner_ref,
    hat_ref,
    slope_ref,
    rate_ref,
    o_ref,
    vec_ref,
    ff_ref,
    scale_ref,
    far_ref,
    far_down_ref,
    *refs,
):
    result_ref, pre_ref, mid_ref, branch_ref, head_ref, acc_ref, ffacc_ref = refs[:7]
    away = refs[7 : 7 + chips - 1]
    wo, wu, wd, wide_grad, partial_sums, stat, means, sems = refs[7 + chips - 1 :]
    step = pl.program_id(0)
    rb = far_ref.shape[1]

    @pl.when(step == 0)
    def _():
        load_down(far_down_ref, n, rb, wd, sems.at[2])
        load_up(far_ref, n, rb, wo, wu, sems)
        acc_ref[...] = jnp.zeros_like(acc_ref)
        partial_sums[...] = jnp.zeros_like(partial_sums)
        wait_whole(wd, sems.at[2])

    cot = cot_ref[...]
    wide_grad[...] = dot(cot, wd[...], NT)

    chunks, wide = wide_grad.shape[0] // CHUNK, wide_grad.shape[1]

    def fold(value):
        out = value[:8]
        for k in range(8, CHUNK, 8):
            out = out + value[k : k + 8]
        return out

    @pl.loop(0, chunks)
    def _(c):
        rows = chunk_rows(c)
        first = jnp.zeros((CHUNK, LANES), F32)
        second = jnp.zeros((CHUNK, LANES), F32)
        for lanes in tiles(wide):
            grad = wide_grad[rows, lanes]
            product = grad * hat_ref[rows, lanes].astype(F32)
            partial_sums[1, :, lanes] += fold(product)
            partial_sums[2, :, lanes] += fold(grad)
            gain = ff_ref[1:2, lanes]
            first = first + grad * gain
            second = second + product * gain
        stat[rows, :] = first
        means[rows, :] = second

    stat[...] = row_mean(stat, wide)
    means[...] = row_mean(means, wide)

    @pl.loop(0, chunks)
    def _(c):
        rows = chunk_rows(c)
        first, second, rate = stat[rows, :], means[rows, :], rate_ref[rows, :]
        for lanes in tiles(wide):
            scaled = wide_grad[rows, lanes] * ff_ref[1:2, lanes]
            grad = rate * (scaled - first - hat_ref[rows, lanes].astype(F32) * second)
            pre = (grad * slope_ref[rows, lanes].astype(F32)).astype(B16)
            pre_ref[rows, lanes] = pre
            partial_sums[0, :, lanes] += fold(pre.astype(F32))

    middle = middle_ref[...]
    result = (middle + dot(inner_ref[...], wd[...], NN) + vec_ref[9:10, :]).astype(B16)
    result_ref[0] = result
    write_away(away, step, chips, chunks_a, result)

    @pl.when(step == 0)
    def _():
        wait_whole(wu, sems.at[1])

    grad = dot(pre_ref[...], wu[...], NT)
    hat, rate = standardise(middle)
    acc_ref[0:1, :] += sums(grad * hat)
    acc_ref[1:2, :] += sums(grad)
    cot = cot.astype(F32)
    acc_ref[3:4, :] += sums(cot)
    mid = cot + standard_back(grad * vec_ref[7:8, :], hat, rate)
    mid_ref[...] = mid
    branch = mid.astype(B16)
    branch_ref[...] = branch
    acc_ref[2:3, :] += sums(branch.astype(F32))

    @pl.when(step == 0)
    def _():
        wait_whole(wo, sems.at[0])

    grad = dot(branch, wo[...], NT)
    heads = o_ref[...]
    hat, rate = standardise(heads * scale_ref[0:1, :])
    acc_ref[4:5, :] += sums(grad * hat)
    acc_ref[5:6, :] += sums(grad)
    scaled = standard_back(grad * vec_ref[5:6, :], hat, rate)
    acc_ref[6:7, :] += sums(scaled * heads)
    head_ref[...] = (scaled * scale_ref[0:1, :]).astype(B16)

    @pl.when(step == pl.num_programs(0) - 1)
    def _():
        for k in range(3):
            ffacc_ref[k : k + 1, :] = sums(partial_sums[k])
        ffacc_ref[3:, :] = jnp.zeros((ffacc_ref.shape[0] - 3, ffacc_ref.shape[1]), F32)


def feed_down(ids, cot, middle, inner, hat, slope, rate, head_rows, vec, ff, scale, far, far_down, n, chips, whole, block):
    rows, width = cot.shape
    wide = ff.shape[1]
    chunks_a = whole * chips

    def rowed(lanes):
        return pl.BlockSpec((block, lanes), lambda i, s: (i, 0))

    def fixed(shape):
        return pl.BlockSpec(shape, lambda i, s: (0, 0))

    lanes = [width, width, wide, wide, wide, LANES, width]
    return pl.pallas_call(
        partial(down_kernel, n, chips, chunks_a),
        grid_spec=pltpu.PrefetchScalarGridSpec(
            num_scalar_prefetch=1,
            grid=(rows // block,),
            in_specs=[rowed(k) for k in lanes]
            + [fixed(vec.shape), fixed(ff.shape), fixed(scale.shape), ANYWHERE, ANYWHERE],
            out_specs=[
                pl.BlockSpec((1, block, width), home_index(chips, chunks_a)),
                rowed(wide),
                rowed(width),
                rowed(width),
                rowed(width),
                fixed((8, width)),
                fixed((8, wide)),
            ]
            + [away_spec(block, width, chips, chunks_a)] * (chips - 1),
            scratch_shapes=[
                pltpu.VMEM((width, width), B16),
                pltpu.VMEM((width, wide), B16),
                pltpu.VMEM((wide, width), B16),
                pltpu.VMEM((block, wide), F32),
                pltpu.VMEM((3, 8, wide), F32),
                pltpu.VMEM((block, LANES), F32),
                pltpu.VMEM((block, LANES), F32),
                pltpu.SemaphoreType.DMA((3,)),
            ],
        ),
        out_shape=[
            jax.ShapeDtypeStruct((rows // block, block, width), B16),
            jax.ShapeDtypeStruct((rows, wide), B16),
            jax.ShapeDtypeStruct((rows, width), F32),
            jax.ShapeDtypeStruct((rows, width), B16),
            jax.ShapeDtypeStruct((rows, width), B16),
            jax.ShapeDtypeStruct((8, width), F32),
            jax.ShapeDtypeStruct((8, wide), F32),
        ]
        + [jax.ShapeDtypeStruct((whole, block, width), B16)] * (chips - 1),
        compiler_params=params(),
        cost_estimate=cost(35),
        name="feed_down",
    )(ids, cot, middle, inner, hat, slope, rate, head_rows, vec, ff, scale, far, far_down)


def side_kernel(groups, n_left, scales, shards, rb, ids_ref, *refs):
    lefts, refs, out_ref = refs[:n_left], refs[n_left:-1], refs[-1]
    block = pl.program_id(0)
    start = at = 0
    for (left, blocks, segments), scale in zip(groups, scales):
        mine = refs[at : at + sum(segments)]
        at += sum(segments)

        @pl.when((block >= start) & (block < start + blocks))
        def _(left=left, segments=segments, mine=mine, scale=scale):
            rows, k = [], 0
            for count in segments:
                values = [r[0] if len(r.shape) == 3 else r[...] for r in mine[k : k + count]]
                k += count
                rows.append(values[0] if count == 1 else add(*values).astype(B16))
            right = rows[0] if len(rows) == 1 else jnp.concatenate(rows, axis=0)
            out = dot(lefts[left][...], right, TN)
            if scale != 1.0:
                out = out * scale
            out_ref[:, 0] = out.astype(B16).reshape(shards, rb, out.shape[1])

        start += blocks


def side_grads(ids, own, lefts, rights, shards, rb, name, into=None):
    width = lefts[0].shape[1]
    half_width = width // 2
    specs = [pl.BlockSpec(x.shape, lambda b, s: (0, 0)) for x in lefts]
    groups, args, scales, start = [], list(lefts), [], 0
    for segments, lead, left, scale in rights:
        blocks = segments[0][0].shape[-1] // width

        def at(b, s, start=start, blocks=blocks):
            half = s[CORE] if own else 1 - s[CORE]
            return half * blocks + jnp.clip(b - start, 0, blocks - 1)

        for array in [a for segment in segments for a in segment]:
            if lead is None:
                specs.append(pl.BlockSpec((array.shape[0], half_width), lambda b, s, at=at: (0, at(b, s))))
            else:
                specs.append(
                    pl.BlockSpec(
                        (1, array.shape[1], half_width), lambda b, s, at=at, lead=lead: (lead, 0, at(b, s))
                    )
                )
            args.append(array)
        groups.append((left, blocks, [len(segment) for segment in segments]))
        scales.append(scale)
        start += blocks
    first, aliases = 0, {}
    if into is not None:
        first = into.shape[1] - start
        aliases = {1 + len(args): 0}
        args.append(into)
        specs.append(ANYWHERE)
    return pl.pallas_call(
        partial(side_kernel, groups, len(lefts), scales, shards, rb),
        grid_spec=pltpu.PrefetchScalarGridSpec(
            num_scalar_prefetch=1,
            grid=(start,),
            in_specs=specs,
            out_specs=pl.BlockSpec((shards, 1, rb, half_width), lambda b, s: (0, first + b, 0, 0)),
        ),
        out_shape=jax.ShapeDtypeStruct((shards, first + start, rb, half_width), B16),
        input_output_aliases=aliases,
        compiler_params=params(),
        cost_estimate=cost(8),
        name=name,
    )(ids, *args)


def down_side_kernel(ids_ref, left_ref, right_ref, out_ref):
    out = dot(left_ref[...], right_ref[...], TN)
    out_ref[...] = out.astype(B16).reshape(out_ref.shape)


def down_side(ids, own, inner, cot, shards, rb, more):
    rows, wide = inner.shape
    width = cot.shape[1]
    half = width // 2
    blocks = wide // width
    group = width // (blocks * rb)
    return pl.pallas_call(
        down_side_kernel,
        grid_spec=pltpu.PrefetchScalarGridSpec(
            num_scalar_prefetch=1,
            grid=(blocks,),
            in_specs=[
                pl.BlockSpec((rows, width), lambda g, s: (0, g)),
                pl.BlockSpec((rows, half), lambda g, s: (0, s[CORE] if own else 1 - s[CORE])),
            ],
            out_specs=pl.BlockSpec((group, blocks, rb, half), lambda g, s: (g, 0, 0, 0)),
        ),
        out_shape=jax.ShapeDtypeStruct((shards, blocks + more, rb, half), B16),
        compiler_params=params(),
        cost_estimate=cost(7),
        name="down_side",
    )(ids, inner, cot)


def terms_kernel(offsets, counts, ids_ref, keep_ref, theirs_ref, *refs):
    outs = refs[-len(counts) :]
    n, at = keep_ref.shape[0], 0
    for out, offset, count in zip(outs, offsets, counts):
        shard = ring_at(ids_ref[SPOT] + offset, n)
        total = keep_ref[shard].astype(F32) + theirs_ref[shard].astype(F32)
        for ref in refs[at : at + count]:
            total = total + ref[...].astype(F32)
        out[...] = total.astype(B16)
        at += count


def ring_terms(ids, keep, theirs, jobs):
    piece = keep.shape[1:]
    args = [keep, theirs] + [x for _, arrived in jobs for x in arrived]
    near = pl.BlockSpec(memory_space=pltpu.VMEM)
    return pl.pallas_call(
        partial(terms_kernel, [offset for offset, _ in jobs], [len(arrived) for _, arrived in jobs]),
        in_specs=[pl.BlockSpec(memory_space=pltpu.SMEM)] + [near] * len(args),
        out_specs=[near] * len(jobs),
        out_shape=[jax.ShapeDtypeStruct(piece, B16)] * len(jobs),
        compiler_params=pltpu.CompilerParams(vmem_limit_bytes=4 * 1024 * 1024),
        cost_estimate=cost(2),
        name="ring_terms",
    )(ids, *args)


def finish_kernel(jobs, count, ids_ref, *refs):
    mine, other = refs[:count], refs[count : 2 * count]
    outs = refs[2 * count :]
    half = mine[0].shape[2]
    core = ids_ref[CORE]
    for group, own in ((mine, True), (other, False)):
        for which in range(2):

            @pl.when((core == which) == own)
            def _(group=group, which=which):
                for out, (first, blocks, stacked) in zip(outs, jobs):
                    for b in range(blocks):
                        value = add(*[r[first + b] for r in group])
                        rb = value.shape[0]
                        if stacked:
                            out[b * rb : (b + 1) * rb, which * half : (which + 1) * half] = value
                        else:
                            at = (which * blocks + b) * half
                            out[:, at : at + half] = value


def finish(ids, mine, other, jobs):
    rb, half = mine[0].shape[1:]
    shapes = [
        (blocks * rb, 2 * half) if stacked else (rb, 2 * blocks * half) for _, blocks, stacked in jobs
    ]
    near = pl.BlockSpec(memory_space=pltpu.VMEM)
    return pl.pallas_call(
        partial(finish_kernel, jobs, len(mine)),
        in_specs=[pl.BlockSpec(memory_space=pltpu.SMEM)] + [near] * (2 * len(mine)),
        out_specs=[near] * len(jobs),
        out_shape=[jax.ShapeDtypeStruct(shape, F32) for shape in shapes],
        compiler_params=pltpu.CompilerParams(vmem_limit_bytes=4 * 1024 * 1024),
        cost_estimate=cost(2),
        name="finish",
    )(ids, *mine, *other)


def tie(x, *others):
    return lax.optimization_barrier((x,) + others)[0]


class Places:
    def __init__(self):
        self.n = n = lax.axis_size("dp")
        self.seq = lax.axis_size("seq")
        self.chips = self.seq // 2
        self.ring = list(range(0, n, 2)) + [i for i in range(n) if i % 2][::-1]
        self.shard = shard = lax.axis_index("dp")
        seq = lax.axis_index("seq")
        self.core, self.chip = seq & 1, seq >> 1
        self.spot = jnp.where((shard & 1) == 0, shard >> 1, n - 1 - (shard >> 1))
        lane = lax.broadcasted_iota(jnp.int32, (8,), 0)
        ids = jnp.zeros((8,), jnp.int32)
        values = (self.spot, self.core, self.chip, shard, lax.rem(seq, GROUPS))
        for k, value in enumerate(values):
            ids = jnp.where(lane == k, value, ids)
        self.ids = ids

    def at(self, offset):
        return ring_at(self.spot + offset, self.n)

    def round(self, x, way):
        ring, n = self.ring, self.n
        return lax.ppermute(x, "dp", [(ring[i], ring[(i + way) % n]) for i in range(n)])

    def swap(self, x):
        return lax.ppermute(x, "seq", [(i, i ^ 1) for i in range(self.seq)])

    def chip_turn(self, x, by):
        n = self.chips
        perm = [(2 * i + c, 2 * ((i + by) % n) + c) for i in range(n) for c in range(2)]
        return lax.ppermute(x, "seq", perm)

    def chip_pair(self, x, bit):
        n = self.chips
        perm = [(2 * i + c, 2 * (i ^ bit) + c) for i in range(n) for c in range(2)]
        return lax.ppermute(x, "seq", perm)

    def gather(self, own, beside):
        forward = backward = own
        forwards, backwards, others, gains = [], [], [], []
        last = self.n // 2
        for k in range(1, last + 1):
            both = k <= (self.n - 1) // 2
            sent = [forward, backward] if both else [forward]
            moved = [self.round(x, way) for x, way in zip(sent, (1, -1))]
            gain = beside[k - 1](forward) if k <= len(beside) else []
            if k < last:
                out = lax.optimization_barrier(tuple(moved) + tuple(gain))
                moved, gain = list(out[: len(moved)]), list(out[len(moved) :])
            gains.append(gain)
            forward = moved[0]
            forwards.append(forward)
            if both:
                backward = moved[1]
                backwards.append(backward)
        pieces = forwards + backwards
        return pieces, [self.swap(piece) for piece in pieces], gains


    def seq_sums(self, total):
        bit, mine = 1, [total]
        while bit < self.chips:
            low = mine[0] if len(mine) == 1 else add(*mine).astype(B16)
            mine = [low, self.chip_pair(low, bit)]
            bit *= 2
        return mine, [self.swap(x) for x in mine]

    def total_steps(self):
        steps = []
        bit = 1
        while bit < self.n:
            perm = [(i, i ^ bit) for i in range(self.n)]
            steps.append(lambda x, perm=perm: x + lax.ppermute(x, "dp", perm))
            bit *= 2
        bit = 1
        while bit < self.chips:
            steps.append(lambda x, bit=bit: x + self.chip_pair(x, bit))
            bit *= 2
        steps.append(lambda x: x + self.swap(x))
        return steps


class RingSum:
    def __init__(self, here, keep, theirs):
        self.here, self.keep, self.theirs = here, keep, theirs
        self.k = here.n // 2
        self.forward = self.backward = None

    def after(self, *values):
        if self.forward is not None:
            self.forward = tie(self.forward, *values)
        if self.backward is not None:
            self.backward = tie(self.backward, *values)

    def jobs(self, ahead, behind):
        forward = [] if self.forward is None else [self.forward]
        backward = [] if self.backward is None else [self.backward]
        return [(ahead, forward)] + ([] if behind is None else [(behind, backward)])

    def round(self):
        both = self.k <= (self.here.n - 1) // 2
        terms = ring_terms(
            self.here.ids, self.keep, self.theirs, self.jobs(self.k, -self.k if both else None)
        )
        self.forward = self.here.round(terms[0], 1)
        if both:
            self.backward = self.here.round(terms[1], -1)
        self.k -= 1
        return terms[0]

    def done(self):
        arrived = [x for x in (self.forward, self.backward) if x is not None]
        return ring_terms(self.here.ids, self.keep, self.theirs, [(0, arrived)])[0]


def local(
    tokens,
    cotangent,
    segment_ids,
    bucket_ids,
    key_mask,
    query_weight,
    key_weight,
    value_weight,
    output_weight,
    query_bias,
    value_bias,
    output_bias,
    first_gain,
    first_shift,
    mixed_gain,
    mixed_shift,
    up_weight,
    down_weight,
    up_bias,
    down_bias,
    second_gain,
    second_shift,
    inner_gain,
    inner_shift,
    bias_table,
    head_scale,
):
    items, own_rows, width = tokens.shape
    heads = head_scale.shape[0]
    head_width = width // heads
    groups = bias_table.shape[0] // 2
    factor = float(head_width) ** (-0.5)
    wide = up_weight.shape[1]
    wide_rows = wide // width
    rb = query_weight.shape[0]
    here = Places()
    n, chips, ids = here.n, here.chips, here.ids
    whole = items // chips
    left = items - whole * chips
    rows_a = whole * chips * own_rows
    rows_c = left * own_rows

    first_far, second_far = pack_far(ids, up_weight, down_weight, output_weight)
    first_far = lax.all_gather(first_far, ("dp", "seq"), axis=0, tiled=False)
    smalls = [
        query_bias,
        value_bias,
        output_bias,
        first_gain,
        first_shift,
        mixed_gain,
        mixed_shift,
        second_gain,
        second_shift,
        down_bias,
    ]
    wides = [up_bias, inner_gain, inner_shift]
    small = jnp.concatenate([v.reshape(1, rb) for v in smalls] + [v.reshape(-1, rb) for v in wides])
    small = jnp.pad(small, ((0, SMALL_ROWS - small.shape[0]), (0, LANES - rb)))
    own = (query_weight, key_weight, value_weight)
    near = pack_near(ids, own, small)

    def take(array, by):
        mine = [
            lax.dynamic_index_in_dim(array, k * chips + lax.rem(here.chip + by, chips), 0, keepdims=False)
            for k in range(whole)
        ]
        return jnp.stack(mine)

    codes = bucket_ids + groups * segment_ids + 2 * groups * (key_mask > 0).astype(jnp.int32)
    tokens_away = [take(tokens, by) for by in range(1, chips)]
    cot_away = [take(cotangent, by) for by in range(1, chips)]

    def first_round(sent):
        turned = [codes] + [here.chip_turn(tie(codes, sent), by) for by in range(1, chips)]
        return [here.chip_turn(tie(x, sent), by) for by, x in enumerate(tokens_away, 1)] + turned

    def second_round(sent):
        return [here.chip_turn(tie(x, sent), by) for by, x in enumerate(cot_away, 1)]

    mine, other, gains = here.gather(near, [first_round, second_round])
    recv, turned = gains[0][: chips - 1], gains[0][chips - 1 :]
    turned = turned + [here.swap(c) for c in turned]
    second_far = lax.all_gather(tie(second_far, mine[1]), ("dp", "seq"), axis=0, tiled=False)
    aux, hot, tab, scale = prep(ids, turned, bias_table, head_scale, chips, whole, left, width)
    cot = jnp.concatenate([take(cotangent, 0)] + gains[1], axis=1).reshape(rows_a, width)
    cot = jnp.concatenate([cot, cotangent[whole * chips :].reshape(rows_c, width)], axis=0)

    x, normed, q, kv_a, kv_c, vec = project(
        tie(ids, aux, cot), tokens, recv, own, small, mine, other, n, chips, whole, factor
    )
    kv_c = kv_c.reshape(2, left, own_rows, width)
    kvs_c = [here.chip_turn(kv_c, by) for by in range(1, chips)]
    kv_a = kv_a.reshape(2, whole, chips * own_rows, width)
    kvs_a = [kv_a, here.swap(kv_a)]
    own_c = [kv_c, here.swap(kv_c)]
    q_a, q_c = chips * own_rows, own_rows
    ff = vec[len(smalls) : len(smalls) + 3 * wide_rows]
    ff = ff.reshape(3, wide_rows, n, rb).transpose(0, 2, 1, 3).reshape(3, wide)
    ff = jnp.pad(ff, ((0, 5), (0, 0)))

    head_rows, logs_a = attend(q, kvs_a, tie(aux, ff), hot, tab, 0, 0, q_a, whole, None)
    kvs_c = [tie(kv, logs_a) for kv in kvs_c]
    kvs_c = own_c[:1] + kvs_c + own_c[1:] + [here.swap(kv) for kv in kvs_c]
    head_rows, logs_c = attend(q, kvs_c, aux, hot, tab, whole, rows_a, q_c, left, head_rows)

    mixed, middle, second, inner, hat, slope, rate = feed_up(
        x, head_rows, vec, ff, scale, first_far, n, own_rows
    )
    more = 1 + wide_rows
    far_send = down_side(ids, False, inner, cot, n, rb, more)
    far_keep = down_side(ids, True, inner, tie(cot, far_send), n, rb, more)
    outs = feed_down(
        ids,
        cot,
        tie(middle, far_keep),
        inner,
        hat,
        slope,
        rate,
        head_rows,
        vec,
        ff,
        scale,
        first_far,
        second_far,
        n,
        chips,
        whole,
        own_rows,
    )
    result, pre, mid, branch, head_grad, acc, ff_acc = outs[:7]
    result_away = [here.chip_turn(part, -by) for by, part in enumerate(outs[7:], 1)]

    def up_side(own, mixed, into):
        rights = [([[branch]], None, 0, 1.0), ([[pre]], None, 1, 1.0)]
        return side_grads(ids, own, [mixed, second], rights, n, rb, "up_side", into)

    far_send = up_side(False, mixed, far_send)
    far_theirs = here.swap(far_send)
    far_keep = up_side(True, tie(mixed, far_send), far_keep)
    far_terms = add(far_keep, far_theirs).astype(B16)
    far_total = lax.psum_scatter(far_terms, "dp", scatter_dimension=0, tiled=False)

    pairs = heads // 2
    third = pairs // 3

    def back_c(span, aux, into):
        return attend_back(
            q, kvs_c, aux, hot, tab, head_grad, head_rows, logs_c, whole, rows_a, q_c, left, span, into
        )

    def back_a(span, aux, into):
        return attend_back(
            q, kvs_a, aux, hot, tab, head_grad, head_rows, logs_a, 0, 0, q_a, whole, span, into
        )

    dq, own_c, other_c, g_c = back_c((0, pairs), tie(aux, far_terms), None)
    other_c = here.swap(other_c)
    dq, own_a0, other_a0, g_a0 = back_a((0, third), aux, dq)
    other_a0 = here.swap(other_a0)
    near_c = add(own_c, tie(other_c, dq)).astype(B16).reshape(2, left, chips, own_rows, -1)
    parts_c = [near_c[:, :, 0]] + [here.chip_turn(near_c[:, :, by], -by) for by in range(1, chips)]
    dq, own_a1, other_a1, g_a1 = back_a((third, pairs - third), tie(aux, near_c, *result_away), dq)
    other_a1 = here.swap(other_a1)
    dkv_c = add(*[tie(p, dq) for p in parts_c]).astype(B16).reshape(2, rows_c, width)
    chunks_a = whole * chips

    def rows_back(span, x, dkvs, into):
        return project_back(
            ids, x, dq, dkvs, mid, vec, own, mine, other, n, chips, whole, own_rows, factor, span, into
        )

    grad_rows, late_c = rows_back((chunks_a, left), x, [dkv_c], None)
    own_a = jnp.concatenate([own_a0, own_a1], axis=-1).reshape(2, rows_a, width)
    other_a = jnp.concatenate([other_a0, tie(other_a1, late_c)], axis=-1).reshape(2, rows_a, width)

    def qkv_side(own, normed):
        rights = [([[dq]], None, 0, factor)]
        rights += [([[own_a, other_a], [dkv_c]], t, 0, 1.0) for t in range(2)]
        return side_grads(ids, own, [normed], rights, n, rb, "qkv_side")

    qkv_send = qkv_side(False, normed)
    qkv_keep = qkv_side(True, tie(normed, qkv_send))
    qkv_ring = RingSum(here, qkv_keep, here.swap(qkv_send))
    sent = qkv_ring.round()
    grad_rows, late_a, *grad_away = rows_back((0, chunks_a), tie(x, sent), [own_a, other_a], grad_rows)

    g_a = jnp.concatenate([g_a0, g_a1], axis=1)
    g = jnp.sum(g_c, axis=0) + jnp.sum(g_a, axis=0)
    g = g.reshape(pairs, 2, 2 * groups, 2 * groups)[:, ::-1, :groups]
    g = g.reshape(heads, groups, 2, groups)
    offset = jnp.arange(groups)
    spread = (
        (offset[:, None, None] - offset[None, :, None]) % groups == offset[None, None, :]
    ).astype(F32)
    table = jnp.einsum("hcsb,cbo->soh", g, spread, precision=lax.Precision.HIGHEST)
    summed = jnp.concatenate(
        [
            acc[:7],
            (late_a + late_c)[:4],
            ff_acc[:3].reshape(-1, width),
            table.reshape(-1, width),
            jnp.zeros((1, width), F32),
        ]
    )

    steps = here.total_steps()
    qkv_ring.after(late_a)
    qkv_ring.round()
    grad_away = [here.chip_turn(part, -by) for by, part in enumerate(grad_away, 1)]
    summed = steps.pop(0)(summed)
    qkv_ring.after(summed)
    qkv_ring.round()
    summed = steps.pop(0)(summed)
    far_sums = here.seq_sums(tie(far_total, summed))
    while qkv_ring.k > 0:
        qkv_ring.after(summed, *grad_away)
        grad_away = [tie(part, summed) for part in grad_away]
        qkv_ring.round()
        if steps:
            summed = steps.pop(0)(summed)
    qkv_total = qkv_ring.done()
    while steps:
        summed = steps.pop(0)(summed)

    query_weight_grad, key_weight_grad, value_weight_grad = finish(
        ids, *here.seq_sums(qkv_total), [(0, 1, False), (1, 1, False), (2, 1, False)]
    )
    down_weight_grad, output_weight_grad, up_weight_grad = finish(
        ids, *far_sums, [(0, wide_rows, True), (wide_rows, 1, False), (wide_rows + 1, wide_rows, False)]
    )
    mine = lax.dynamic_slice_in_dim(summed[:11], here.shard * rb, rb, axis=1)
    ff_sums = summed[11 : 11 + 3 * wide_rows].reshape(3, wide)
    ff_mine = lax.dynamic_slice_in_dim(ff_sums, here.shard * (wide // n), wide // n, axis=1)
    table_grad = summed[11 + 3 * wide_rows].reshape(2 * groups, heads)
    scale_grad = jnp.sum(summed[6].reshape(heads, head_width), axis=1)

    def home(array, away):
        for by, part in enumerate(away, 1):
            part = part.astype(array.dtype)
            for k in range(whole):
                item = k * chips + lax.rem(here.chip + by, chips)
                array = lax.dynamic_update_index_in_dim(array, part[k], item, 0)
        return array

    return (
        home(result, result_away),
        home(grad_rows, grad_away),
        query_weight_grad,
        key_weight_grad,
        value_weight_grad,
        output_weight_grad,
        mine[9],
        mine[10],
        mine[2],
        mine[7],
        mine[8],
        mine[4],
        mine[5],
        up_weight_grad,
        down_weight_grad,
        ff_mine[0],
        mine[3],
        mine[0],
        mine[1],
        ff_mine[1],
        ff_mine[2],
        table_grad,
        scale_grad,
    )


def solution(mesh):
    rowed, shard, vector, whole = P("dp", "seq", None), P("dp", None), P("dp"), P()
    flat = P("dp", "seq")
    placed = (rowed,) * 2 + (flat,) * 3 + (shard,) * 4 + (vector,) * 7 + (shard,) * 2 + (vector,) * 6
    placed = placed + (whole,) * 2
    outs = (rowed,) * 2 + (shard,) * 4 + (vector,) * 7 + (shard,) * 2 + (vector,) * 6 + (whole,) * 2
    return jax.shard_map(local, mesh=mesh, in_specs=placed, out_specs=outs, check_vma=False)
```

```python
from functools import partial

import jax
import jax.numpy as jnp
from jax import lax
from jax.experimental import pallas as pl
from jax.experimental.pallas import tpu as pltpu
from jax.sharding import PartitionSpec as P

EPSILON = 1e-05
FLOOR_SCORE = -1e30
F32 = jnp.float32
B16 = jnp.bfloat16
NN = (((1,), (0,)), ((), ()))
NT = (((1,), (1,)), ((), ()))
TN = (((0,), (0,)), ((), ()))
VMEM_LIMIT = 60 * 1024 * 1024
SMALL_ROWS = 32
LANES = 128


def dot(a, b, dims, **kw):
    return lax.dot_general(a, b, dims, preferred_element_type=F32, **kw)


def params():
    return pltpu.CompilerParams(vmem_limit_bytes=VMEM_LIMIT)


def cost(micros):
    return pl.CostEstimate(flops=int(micros * 1.1e9), bytes_accessed=0, transcendentals=0)


def low_lanes(shape):
    return lax.broadcasted_iota(jnp.int32, shape, 1) < shape[1] // 2


def low_rows(shape):
    return lax.broadcasted_iota(jnp.int32, shape, 0) < shape[0] // 2


def standardise(values):
    mean = jnp.mean(values, axis=-1, keepdims=True)
    centred = values - mean
    spread = jnp.mean(centred * centred, axis=-1, keepdims=True)
    rate = lax.rsqrt(spread + EPSILON)
    return centred * rate, rate


def standard_back(hat_grad, hat, rate):
    first = jnp.mean(hat_grad, axis=-1, keepdims=True)
    second = jnp.mean(hat_grad * hat, axis=-1, keepdims=True)
    return rate * (hat_grad - first - hat * second)


def add(*parts):
    return sum(p.astype(F32) for p in parts)


def sums(array):
    return jnp.sum(array, axis=0, keepdims=True)


SPOT, CORE, CHIP, SHARD, GROUP = range(5)
GROUPS = 4


def ring_at(spot, n):
    spot = lax.rem(spot + 2 * n, n)
    return jnp.where(spot < (n + 1) // 2, 2 * spot, 2 * n - 1 - 2 * spot)


def piece_shards(ids, n):
    spot = ids[SPOT]
    out = [ids[SHARD]]
    out += [ring_at(spot - k, n) for k in range(1, n // 2 + 1)]
    out += [ring_at(spot + k, n) for k in range(1, (n - 1) // 2 + 1)]
    return out


def wait_whole(target, sem):
    pltpu.make_async_copy(target, target, sem).wait()


ANYWHERE = pl.BlockSpec(memory_space=pl.ANY)


def pack_near_kernel(ids_ref, q_ref, k_ref, v_ref, o_ref, small_ref, near_ref):
    rb = q_ref.shape[0]
    for t, ref in enumerate((q_ref, k_ref, v_ref, o_ref)):
        near_ref[t * rb : (t + 1) * rb, :] = ref[...]
    near_ref[4 * rb :, :] = jnp.zeros((SMALL_ROWS, near_ref.shape[1]), B16)
    near_ref[4 * rb :, 0:LANES] = small_ref[...]


def pack_near(ids, weights, small):
    rb, width = weights[0].shape
    half = width // 2
    return pl.pallas_call(
        pack_near_kernel,
        grid_spec=pltpu.PrefetchScalarGridSpec(
            num_scalar_prefetch=1,
            grid=(1,),
            in_specs=[pl.BlockSpec((rb, half), lambda i, s: (0, s[CORE]))] * 4
            + [pl.BlockSpec(small.shape, lambda i, s: (0, 0))],
            out_specs=pl.BlockSpec((4 * rb + SMALL_ROWS, half), lambda i, s: (0, 0)),
        ),
        out_shape=jax.ShapeDtypeStruct((4 * rb + SMALL_ROWS, half), B16),
        compiler_params=params(),
        cost_estimate=cost(2),
        name="pack_near",
    )(ids, *weights, small)


def pack_far_kernel(ids_ref, up_ref, down_ref, far_ref):
    part = up_ref.shape[1]
    far_ref[:, :part] = up_ref[...]
    far_ref[:, part:] = down_ref[...]


def pack_far(ids, up, down):
    rb, wide = up.shape
    width = down.shape[1]
    part = wide // GROUPS
    return pl.pallas_call(
        pack_far_kernel,
        grid_spec=pltpu.PrefetchScalarGridSpec(
            num_scalar_prefetch=1,
            grid=(1,),
            in_specs=[
                pl.BlockSpec((rb, part), lambda i, s: (0, s[GROUP])),
                pl.BlockSpec((rb, width), lambda i, s: (s[GROUP], 0)),
            ],
            out_specs=pl.BlockSpec((rb, part + width), lambda i, s: (0, 0)),
        ),
        out_shape=jax.ShapeDtypeStruct((rb, part + width), B16),
        compiler_params=params(),
        cost_estimate=cost(2),
        name="pack_far",
    )(ids, up, down)


def prep_kernel(chips, whole, left, ids_ref, *refs):
    code_refs = refs[: 2 * chips]
    table_ref, scale_in_ref = refs[2 * chips : 2 * chips + 2]
    aux_ref, hot_ref, tab_ref, scale_ref = refs[2 * chips + 2 :]
    rows = code_refs[0].shape[1]
    levels = tab_ref.shape[0] // 2
    width = tab_ref.shape[1]
    chip = ids_ref[CHIP]

    def column(item, source):
        code = code_refs[source][pl.ds(item, 1), :]
        level = lax.broadcasted_iota(jnp.int32, (LANES, rows), 0) % (2 * levels)
        hit = jnp.where(level == code % levels, 1.0, 0.0)
        floor = jnp.where((level == levels) & (code < 2 * levels), FLOOR_SCORE, 0.0)
        return jnp.transpose(jnp.where(level < levels, hit, floor)).astype(B16)

    def own(item, source):
        code = code_refs[source][pl.ds(item, 1), :]
        level = lax.broadcasted_iota(jnp.int32, (LANES, rows), 0)
        hit = jnp.where(level == code % (2 * levels), 1.0, 0.0)
        return jnp.transpose(hit).astype(B16)[:, : 2 * levels]

    for item in range(whole + left):
        row = item * chips + chip if item < whole else whole * chips + item - whole
        for source in range(2 * chips):
            aux_ref[item, source * rows : (source + 1) * rows, :] = column(row, source)
    for k in range(whole):
        for source in range(chips):
            start = (k * chips + source) * rows
            hot_ref[start : start + rows, :] = own(k * chips + chip, source)
    for k in range(left):
        start = (whole * chips + k) * rows
        hot_ref[start : start + rows, :] = own(whole * chips + k, 0)

    head = lax.broadcasted_iota(jnp.int32, (LANES, width), 0)
    lane = lax.broadcasted_iota(jnp.int32, (LANES, width), 1)
    owner = lane // LANES * 2 + 1 - lane % LANES // (LANES // 2)
    spread = jnp.where(head == owner, 1.0, 0.0).astype(B16)
    by_lane = dot(table_ref[...], spread, NN)
    lane = lax.broadcasted_iota(jnp.int32, (levels, width), 1) % (2 * levels)
    bucket = lax.broadcasted_iota(jnp.int32, (levels, width), 0)
    turn = jnp.where(lane < levels, (lane - bucket) & (levels - 1), -1)
    for segment in range(2):
        out = jnp.where(lane == levels, 1.0, 0.0)
        for o in range(levels):
            line = by_lane[segment * levels + o : segment * levels + o + 1, :]
            out = jnp.where(turn == o, line, out)
        tab_ref[segment * levels : (segment + 1) * levels, :] = out.astype(B16)
    lane = lax.broadcasted_iota(jnp.int32, (LANES, width), 1)
    spread = jnp.where(head == lane // (LANES // 2), 1.0, 0.0).astype(B16)
    scale_ref[...] = dot(scale_in_ref[...], spread, NN)


def prep(ids, codes, table, head_scale, chips, whole, left, width):
    rows = codes[0].shape[1]
    table = jnp.pad(table, ((0, 0), (0, LANES - table.shape[1])))
    scale = jnp.pad(head_scale[None], ((0, 15), (0, LANES - head_scale.shape[0])))
    levels = table.shape[0]
    q_rows = (whole * chips + left) * rows

    def fixed(shape):
        return pl.BlockSpec(shape, lambda i, s: (0,) * len(shape))

    outs = [(whole + left, 2 * chips * rows, LANES), (q_rows, levels), (levels, width), (16, width)]
    return pl.pallas_call(
        partial(prep_kernel, chips, whole, left),
        grid_spec=pltpu.PrefetchScalarGridSpec(
            num_scalar_prefetch=1,
            grid=(1,),
            in_specs=[fixed(c.shape) for c in codes] + [fixed(table.shape), fixed(scale.shape)],
            out_specs=[fixed(o) for o in outs],
        ),
        out_shape=[
            jax.ShapeDtypeStruct(outs[0], B16),
            jax.ShapeDtypeStruct(outs[1], B16),
            jax.ShapeDtypeStruct(outs[2], B16),
            jax.ShapeDtypeStruct(outs[3], F32),
        ],
        compiler_params=params(),
        cost_estimate=cost(3),
        name="prep",
    )(ids, *codes, table, scale)


def load_qkv(ids_ref, n, rb, half, own, mine, other, targets, sems):
    shards = piece_shards(ids_ref, n)
    core = ids_ref[CORE]
    starts = [pl.multiple_of(shard * rb, 16) for shard in shards]
    here = pl.multiple_of(core * half, LANES)
    there = pl.multiple_of((1 - core) * half, LANES)
    for t, target in enumerate(targets):
        pltpu.make_async_copy(own[t], target.at[pl.ds(starts[0], rb), :], sems.at[t]).start()
        for j in range(n - 1):
            rows = pl.ds(starts[j + 1], rb)
            part = pl.ds(t * rb, rb)
            pltpu.make_async_copy(
                mine[j].at[part, :], target.at[rows, pl.ds(here, half)], sems.at[t]
            ).start()
            pltpu.make_async_copy(
                other[j].at[part, :], target.at[rows, pl.ds(there, half)], sems.at[t]
            ).start()


def project_kernel(n, chips, chunks_a, factor, ids_ref, x_ref, *refs):
    recv = refs[: chips - 1]
    refs = refs[chips - 1 :]
    own, own_small = refs[:3], refs[3]
    mine, other = refs[4 : 4 + n - 1], refs[4 + n - 1 : 4 + 2 * (n - 1)]
    refs = refs[4 + 2 * (n - 1) :]
    x_out, normed_ref, q_ref, kva_ref, kvc_ref, vec_ref = refs[:6]
    wq, wk, wv, small, sems = refs[6:]
    rb = own[0].shape[0]
    half = wq.shape[1] // 2
    step = pl.program_id(0)

    @pl.when(step == 0)
    def _():
        pltpu.make_async_copy(own_small, small.at[0], sems.at[3]).start()
        for j in range(n - 1):
            pltpu.make_async_copy(
                mine[j].at[pl.ds(4 * rb, SMALL_ROWS), pl.ds(0, LANES)], small.at[j + 1], sems.at[3]
            ).start()
        load_qkv(ids_ref, n, rb, half, own, mine, other, (wq, wk, wv), sems)
        wait_whole(small, sems.at[3])
        total = jnp.zeros(vec_ref.shape, F32)
        row = lax.broadcasted_iota(jnp.int32, (LANES, wq.shape[1]), 0)
        col = lax.broadcasted_iota(jnp.int32, (LANES, wq.shape[1]), 1)
        for j, shard in enumerate(piece_shards(ids_ref, n)):
            spot = jnp.where((row < rb) & (col == row + shard * rb), 1.0, 0.0).astype(B16)
            total = total + dot(small[j], spot, NN)
        vec_ref[...] = total
        for t, target in enumerate((wq, wk, wv)):
            wait_whole(target, sems.at[t])

    x = x_ref[0]
    for s in range(1, chips):
        x = jnp.where((step < chunks_a) & (lax.rem(step, chips) == s), recv[s - 1][0], x)
    x_out[...] = x
    hat, _ = standardise(x.astype(F32))
    normed = (hat * vec_ref[3:4, :] + vec_ref[4:5, :]).astype(B16)
    normed_ref[...] = normed
    q_ref[...] = ((dot(normed, wq[...], NN) + vec_ref[0:1, :]) * factor).astype(B16)
    keys = dot(normed, wk[...], NN).astype(B16)
    values = (dot(normed, wv[...], NN) + vec_ref[1:2, :]).astype(B16)

    @pl.when(step < chunks_a)
    def _():
        kva_ref[0] = keys
        kva_ref[1] = values

    @pl.when(step >= chunks_a)
    def _():
        kvc_ref[0] = keys
        kvc_ref[1] = values


def project(ids, tokens, recv, own, small, mine, other, n, chips, whole, factor):
    items, rows, width = tokens.shape
    chunks_a = whole * chips
    rowed = pl.BlockSpec((rows, width), lambda i, s: (i, 0))

    def item(i, s):
        own_item = jnp.minimum(i, chunks_a - 1) // chips * chips + s[CHIP]
        return (jnp.where(i < chunks_a, own_item, i), 0, 0)

    received = pl.BlockSpec((1, rows, width), lambda i, s: (jnp.minimum(i, chunks_a - 1) // chips, 0, 0))
    total = items * rows
    return pl.pallas_call(
        partial(project_kernel, n, chips, chunks_a, factor),
        grid_spec=pltpu.PrefetchScalarGridSpec(
            num_scalar_prefetch=1,
            grid=(items,),
            in_specs=[pl.BlockSpec((1, rows, width), item)]
            + [received] * len(recv)
            + [ANYWHERE] * (4 + 2 * (n - 1)),
            out_specs=[
                rowed,
                rowed,
                rowed,
                pl.BlockSpec((2, rows, width), lambda i, s: (0, jnp.minimum(i, chunks_a - 1), 0)),
                pl.BlockSpec((2, rows, width), lambda i, s: (0, jnp.maximum(i - chunks_a, 0), 0)),
                pl.BlockSpec((SMALL_ROWS, width), lambda i, s: (0, 0)),
            ],
            scratch_shapes=[pltpu.VMEM((width, width), B16)] * 3
            + [pltpu.VMEM((n,) + small.shape, B16), pltpu.SemaphoreType.DMA((4,))],
        ),
        out_shape=[
            jax.ShapeDtypeStruct((total, width), B16),
            jax.ShapeDtypeStruct((total, width), B16),
            jax.ShapeDtypeStruct((total, width), B16),
            jax.ShapeDtypeStruct((2, chunks_a * rows, width), B16),
            jax.ShapeDtypeStruct((2, total - chunks_a * rows, width), B16),
            jax.ShapeDtypeStruct((SMALL_ROWS, width), F32),
        ],
        compiler_params=params(),
        cost_estimate=cost(10),
        name="project",
    )(ids, tokens, *recv, *own, small, *mine, *other)


def home_index(chips, chunks_a):
    def at(i, s):
        k, by = i // chips, lax.rem(i, chips)
        return (jnp.where(i < chunks_a, k * chips + lax.rem(s[CHIP] + by, chips), i), 0, 0)

    return at


def away_spec(rows, width, chips, chunks_a):
    return pl.BlockSpec((1, rows, width), lambda i, s: (jnp.minimum(i, chunks_a - 1) // chips, 0, 0))


def write_away(refs, step, chips, chunks_a, value):
    for s, ref in enumerate(refs, 1):

        @pl.when((step < chunks_a) & (lax.rem(step, chips) == s))
        def _(ref=ref):
            ref[0] = value.astype(ref.dtype)


def project_back_kernel(n, chips, chunks_a, first, fresh, count, factor, ids_ref, x_ref, mid_ref, vec_ref, *refs):
    dq_refs, dkv_refs = refs[:2], (refs[2 : 2 + count], refs[2 + count : 2 + 2 * count])
    refs = refs[2 + 2 * count :]
    own = refs[:3]
    mine, other = refs[3 : 3 + n - 1], refs[3 + n - 1 : 3 + 2 * (n - 1)]
    refs = refs[3 + 2 * (n - 1) :]
    if not fresh:
        refs = refs[1:]
    out_ref, acc_ref = refs[:2]
    away = refs[2:-5]
    wq, wk, wv, joined, sems = refs[-5:]
    rb, half = own[0].shape[0], wq.shape[1] // 2
    step = pl.program_id(0) + first
    core = ids_ref[CORE]

    @pl.when(step == first)
    def _():
        load_qkv(ids_ref, n, rb, half, own, mine, other, (wq, wk, wv), sems)
        acc_ref[...] = jnp.zeros_like(acc_ref)

    for h, place in enumerate((core, 1 - core)):
        lanes = pl.ds(pl.multiple_of(place * half, LANES), half)
        joined[0, :, lanes] = dq_refs[h][...]
        for t in range(2):
            value = dkv_refs[h][0][t] if count == 1 else add(*[r[t] for r in dkv_refs[h]]).astype(B16)
            joined[1 + t, :, lanes] = value

    @pl.when(step == first)
    def _():
        for t, target in enumerate((wq, wk, wv)):
            wait_whole(target, sems.at[t])

    dq, dk, dv = joined[0], joined[1], joined[2]
    grad = factor * dot(dq, wq[...], NT) + dot(dk, wk[...], NT) + dot(dv, wv[...], NT)
    hat, rate = standardise(x_ref[...].astype(F32))
    out = mid_ref[...] + standard_back(grad * vec_ref[3:4, :], hat, rate)
    out_ref[0] = out
    if first < chunks_a:
        write_away(away, step, chips, chunks_a, out)
    acc_ref[0:1, :] += sums(grad * hat)
    acc_ref[1:2, :] += sums(grad)
    acc_ref[2:3, :] += factor * sums(dq.astype(F32))
    acc_ref[3:4, :] += sums(dv.astype(F32))


def project_back(ids, x, dqs, dkvs, mid, vec, own, mine, other, n, chips, whole, rows, factor, span, into):
    total, width = x.shape
    items, chunks_a = total // rows, whole * chips
    first, count = span
    rowed = pl.BlockSpec((rows, width), lambda i, s: (first + i, 0))
    at = home_index(chips, chunks_a)
    fresh = into is None
    away = chips - 1 if first < chunks_a else 0
    flat = list(dqs) + [d for group in dkvs for d in group]
    n_args = 4 + len(flat) + 3 + 2 * (n - 1)
    return pl.pallas_call(
        partial(project_back_kernel, n, chips, chunks_a, first, fresh, len(dkvs[0]), factor),
        grid_spec=pltpu.PrefetchScalarGridSpec(
            num_scalar_prefetch=1,
            grid=(count,),
            in_specs=[rowed, rowed, pl.BlockSpec(vec.shape, lambda i, s: (0, 0))]
            + [pl.BlockSpec((rows, width // 2), lambda i, s: (i, 0))] * 2
            + [pl.BlockSpec((2, rows, width // 2), lambda i, s: (0, i, 0))] * (len(flat) - 2)
            + [ANYWHERE] * (3 + 2 * (n - 1) + (0 if fresh else 1)),
            out_specs=[
                pl.BlockSpec((1, rows, width), lambda i, s: at(first + i, s)),
                pl.BlockSpec((8, width), lambda i, s: (0, 0)),
            ]
            + [away_spec(rows, width, chips, chunks_a)] * away,
            scratch_shapes=[pltpu.VMEM((width, width), B16)] * 3
            + [pltpu.VMEM((3, rows, width), B16), pltpu.SemaphoreType.DMA((3,))],
        ),
        out_shape=[
            jax.ShapeDtypeStruct((items, rows, width), F32),
            jax.ShapeDtypeStruct((8, width), F32),
        ]
        + [jax.ShapeDtypeStruct((whole, rows, width), B16)] * away,
        input_output_aliases={} if fresh else {n_args: 0},
        compiler_params=params(),
        cost_estimate=cost(8),
        name="project_back",
    )(ids, x, mid, vec, *flat, *own, *mine, *other, *([] if fresh else [into]))


def score_operands(qp, kp, aux, hot, tab):
    rel = dot(hot, tab, NN).astype(B16)
    lq, lk = low_lanes(qp.shape), low_lanes(kp.shape)
    return (
        (jnp.where(lq, qp, rel), jnp.where(lk, kp, aux)),
        (jnp.where(lq, rel, qp), jnp.where(lk, aux, kp)),
    )


def attend_kernel(n_kv, q_ref, aux_ref, hot_ref, tab_ref, *refs):
    kv_refs = refs[:n_kv]
    o_ref, l_ref = refs[-2:]
    qp = q_ref[...]
    kp = jnp.concatenate([r[0, 0] for r in kv_refs], axis=0)
    vp = jnp.concatenate([r[1, 0] for r in kv_refs], axis=0)
    outs = []
    for h, (qh, kh) in enumerate(score_operands(qp, kp, aux_ref[0], hot_ref[...], tab_ref[...])):
        scores = dot(kh, qh, NT)
        top = jnp.max(scores, axis=0, keepdims=True)
        exponent = jnp.exp(scores - top)
        total = jnp.sum(exponent, axis=0, keepdims=True)
        out = dot(vp, exponent.astype(B16), TN)
        outs.append(out * (1.0 / total))
        l_ref[0, 0, h : h + 1, :] = top + jnp.log(total)
    o_ref[...] = jnp.transpose(jnp.where(low_rows(outs[0].shape), outs[0], outs[1]))


def attend(q, kvs, aux, hot, tab, item_start, row_start, q_rows, items, into):
    rows, width = q.shape
    keys = aux.shape[1]
    pairs = width // LANES
    first = row_start // q_rows
    rowed = pl.BlockSpec((q_rows, LANES), lambda i, p: (first + i, p))
    args = [q, aux, hot, tab] + list(kvs)
    specs = [
        rowed,
        pl.BlockSpec((1, keys, LANES), lambda i, p: (item_start + i, 0, 0)),
        pl.BlockSpec((q_rows, hot.shape[1]), lambda i, p: (first + i, 0)),
        pl.BlockSpec((tab.shape[0], LANES), lambda i, p: (0, p)),
    ] + [pl.BlockSpec((2, 1, kv.shape[2], LANES), lambda i, p: (0, i, 0, p)) for kv in kvs]
    aliases = {}
    if into is not None:
        aliases = {len(args): 0}
        args.append(into)
        specs.append(ANYWHERE)
    return pl.pallas_call(
        partial(attend_kernel, len(kvs)),
        grid=(items, pairs),
        in_specs=specs,
        out_specs=[rowed, pl.BlockSpec((1, 1, 8, q_rows), lambda i, p: (i, p, 0, 0))],
        out_shape=[
            jax.ShapeDtypeStruct((rows, width), F32),
            jax.ShapeDtypeStruct((items, pairs, 8, q_rows), F32),
        ],
        input_output_aliases=aliases,
        compiler_params=params(),
        cost_estimate=cost(14),
        name="attend",
    )(*args)


def attend_back_kernel(n_kv, ids_ref, q_ref, aux_ref, hot_ref, tab_ref, do_ref, o_ref, l_ref, *refs):
    kv_refs = refs[:n_kv]
    dq_ref, own_ref, other_ref, g_ref = refs[-4:]
    qp, dop, hot = q_ref[...], do_ref[...], hot_ref[...]
    kp = jnp.concatenate([r[0, 0] for r in kv_refs], axis=0)
    vp = jnp.concatenate([r[1, 0] for r in kv_refs], axis=0)
    lk = low_lanes(kp.shape)
    zero = jnp.zeros_like(vp)
    product = dop.astype(F32) * o_ref[...]
    row = lax.broadcasted_iota(jnp.int32, (8, LANES), 0)
    pick = jnp.where(low_lanes((8, LANES)) == (row == 0), 1.0, 0.0)
    row_dot = dot(pick, product, NT, precision=lax.Precision.HIGHEST)
    dvs, dks, dqs = [], [], []
    operands = score_operands(qp, kp, aux_ref[0], hot, tab_ref[...])
    for h, (qh, kh) in enumerate(operands):
        vh = jnp.where(lk, vp, zero) if h == 0 else jnp.where(lk, zero, vp)
        probs = jnp.exp(dot(kh, qh, NT) - l_ref[0, 0, h : h + 1, :])
        score_grad = (probs * (dot(vh, dop, NT) - row_dot[h : h + 1, :])).astype(B16)
        dvs.append(dot(probs.astype(B16), dop, NN))
        dks.append(dot(score_grad, qp, NN))
        dqs.append(dot(kh, score_grad, TN))
    dk = jnp.where(lk, dks[0], dks[1]).astype(B16)
    dv = jnp.where(lk, dvs[0], dvs[1]).astype(B16)
    half = own_ref.shape[2]
    own_ref[0, 0], own_ref[1, 0] = dk[:half], dv[:half]
    other_ref[0, 0], other_ref[1, 0] = dk[half:], dv[half:]
    lr = low_rows(dqs[0].shape)
    dq_ref[...] = jnp.transpose(jnp.where(lr, dqs[0], dqs[1])).astype(B16)
    count = g_ref.shape[2] // 2
    middle = LANES // 2
    levels = jnp.concatenate([dqs[0][middle : middle + count], dqs[1][:count]], axis=0)
    upper = levels.astype(B16)
    lower = (levels - upper.astype(F32)).astype(B16)
    g_ref[0, 0] = dot(upper, hot, NN) + dot(lower, hot, NN)


def attend_back(ids, q, kvs, aux, hot, tab, head_grad, head_rows, logs, item_start, row_start, q_rows, items, own):
    width = q.shape[1]
    keys = aux.shape[1]
    pairs = width // LANES // 2
    first = row_start // q_rows

    def pair(p, s):
        return (s[CORE] if own else 1 - s[CORE]) * pairs + p

    rowed = pl.BlockSpec((q_rows, LANES), lambda i, p, s: (first + i, pair(p, s)))
    half = pl.BlockSpec((2, 1, keys // 2, LANES), lambda i, p, s: (0, i, 0, p))
    half_shape = jax.ShapeDtypeStruct((2, items, keys // 2, width // 2), B16)
    return pl.pallas_call(
        partial(attend_back_kernel, len(kvs)),
        grid_spec=pltpu.PrefetchScalarGridSpec(
            num_scalar_prefetch=1,
            grid=(items, pairs),
            in_specs=[
                rowed,
                pl.BlockSpec((1, keys, LANES), lambda i, p, s: (item_start + i, 0, 0)),
                pl.BlockSpec((q_rows, hot.shape[1]), lambda i, p, s: (first + i, 0)),
                pl.BlockSpec((tab.shape[0], LANES), lambda i, p, s: (0, pair(p, s))),
                rowed,
                rowed,
                pl.BlockSpec((1, 1, 8, q_rows), lambda i, p, s: (i, pair(p, s), 0, 0)),
            ]
            + [
                pl.BlockSpec((2, 1, kv.shape[2], LANES), lambda i, p, s: (0, i, 0, pair(p, s)))
                for kv in kvs
            ],
            out_specs=[
                pl.BlockSpec((q_rows, LANES), lambda i, p, s: (i, p)),
                half,
                half,
                pl.BlockSpec((1, 1, hot.shape[1], hot.shape[1]), lambda i, p, s: (i, p, 0, 0)),
            ],
        ),
        out_shape=[
            jax.ShapeDtypeStruct((items * q_rows, width // 2), B16),
            half_shape,
            half_shape,
            jax.ShapeDtypeStruct((items, pairs, hot.shape[1], hot.shape[1]), F32),
        ],
        compiler_params=params(),
        cost_estimate=cost(8),
        name="attend_back",
    )(ids, q, aux, hot, tab, head_grad, head_rows, logs, *kvs)


CHUNK = 32


def gelu_parts(v):
    mass = 0.5 + 0.5 * lax.erf(v * 0.7071067811865476)
    bell = jnp.exp2(v * v * -0.7213475204444817)
    return v * mass, mass + v * (bell * 0.3989422804014327)


def tiles(width):
    return [slice(k, k + LANES) for k in range(0, width, LANES)]


def row_mean(stat, width):
    mean = jnp.sum(stat[...], axis=1, keepdims=True) * (1.0 / width)
    return jnp.broadcast_to(mean, stat.shape)


def chunk_rows(c):
    return pl.ds(pl.multiple_of(c * CHUNK, CHUNK), CHUNK)


def load_output(ids_ref, n, own, mine, other, wo, sem):
    shards = piece_shards(ids_ref, n)
    core = ids_ref[CORE]
    rb, width = own.shape
    half = width // 2
    starts = [pl.multiple_of(shard * rb, 16) for shard in shards]
    pltpu.make_async_copy(own, wo.at[pl.ds(starts[0], rb), :], sem).start()
    for j in range(n - 1):
        for piece, place in ((mine[j], core), (other[j], 1 - core)):
            pltpu.make_async_copy(
                piece.at[pl.ds(3 * rb, rb), :],
                wo.at[pl.ds(starts[j + 1], rb), pl.ds(pl.multiple_of(place * half, LANES), half)],
                sem,
            ).start()


def load_far(far, n, rb, wu, wd, sems):
    group = far.shape[0] // n
    width = wu.shape[0]
    part = wu.shape[1] // GROUPS
    for shard in range(n):
        for g in range(GROUPS):
            pltpu.make_async_copy(
                far.at[shard * group + g, :, pl.ds(0, part)],
                wu.at[pl.ds(shard * rb, rb), pl.ds(g * part, part)],
                sems.at[1],
            ).start()
    for shard in range(n):
        for g in range(GROUPS):
            pltpu.make_async_copy(
                far.at[shard * group + g, :, pl.ds(part, width)],
                wd.at[pl.ds((shard * GROUPS + g) * rb, rb), :],
                sems.at[2],
            ).start()


PARTS = 2


def feed_kernel(n, chips, chunks_a, ids_ref, x_ref, cot_ref, o_ref, vec_ref, ff_ref, scale_ref, far_ref, *refs):
    own, mine, other = refs[0], refs[1:n], refs[n : 2 * n - 1]
    refs = refs[2 * n - 1 :]
    mixed_ref, second_ref, inner_ref, pre_keep, pre_send, branch_keep, branch_send = refs[:7]
    result_ref, mid_ref, head_ref, acc_ref, ffacc_ref = refs[7:12]
    away = refs[12 : 12 + chips - 1]
    wo, wu, wd, act, grads, hats, slopes, pre_grad, total_ref, fold_sums = refs[12 + chips - 1 : -4]
    stat, means, rates, sems = refs[-4:]
    step = pl.program_id(0)
    core = ids_ref[CORE]
    block, wide = act.shape
    width = wo.shape[0]
    share = block // PARTS
    lines = min(CHUNK, share)

    def at_start(action):
        pl.when(step == 0)(action)

    @pl.when(step == 0)
    def _():
        load_output(ids_ref, n, own, mine, other, wo, sems.at[0])
        load_far(far_ref, n, far_ref.shape[1], wu, wd, sems)
        acc_ref[...] = jnp.zeros_like(acc_ref)
        fold_sums[...] = jnp.zeros_like(fold_sums)

    def row_chunks(part):
        for k in range(share // lines):
            yield pl.ds(pl.multiple_of(part * share + k * lines, lines), lines)

    def fold(value):
        out = value[:8]
        for k in range(8, value.shape[0], 8):
            out = out + value[k : k + 8]
        return out

    heads = o_ref[...]
    hat, _ = standardise(heads * scale_ref[0:1, :])
    mixed = (hat * vec_ref[5:6, :] + vec_ref[6:7, :]).astype(B16)
    mixed_ref[...] = mixed
    at_start(lambda: wait_whole(wo, sems.at[0]))
    middle = x_ref[...].astype(F32) + dot(mixed, wo[...], NN) + vec_ref[2:3, :]
    hat, _ = standardise(middle)
    second = (hat * vec_ref[7:8, :] + vec_ref[8:9, :]).astype(B16)
    second_ref[...] = second
    mid_ref[...] = middle
    at_start(lambda: wait_whole(wu, sems.at[1]))
    act[...] = dot(second, wu[...], NN)
    at_start(lambda: wait_whole(wd, sems.at[2]))

    span = wide // PARTS

    @pl.loop(0, PARTS)
    def _(part):
        columns = pl.ds(pl.multiple_of(part * span, LANES), span)
        grads[:, columns] = dot(cot_ref[...], wd[columns, :], NT)
        for rows in row_chunks(part):
            total = jnp.zeros((lines, LANES), F32)
            for lanes in tiles(wide):
                active, slope = gelu_parts(act[rows, lanes] + ff_ref[0:1, lanes])
                slopes[rows, lanes] = slope.astype(B16)
                act[rows, lanes] = active
                total = total + active
            stat[rows, :] = total

    means[...] = row_mean(stat, wide)

    @pl.loop(0, PARTS)
    def _(part):
        for rows in row_chunks(part):
            mean = means[rows, :]
            total = jnp.zeros((lines, LANES), F32)
            for lanes in tiles(wide):
                centred = act[rows, lanes] - mean
                total = total + centred * centred
            stat[rows, :] = total

    rates[...] = lax.rsqrt(row_mean(stat, wide) + EPSILON)

    @pl.loop(0, PARTS)
    def _(part):
        for rows in row_chunks(part):
            mean, rate = means[rows, :], rates[rows, :]
            first = jnp.zeros((lines, LANES), F32)
            other = jnp.zeros((lines, LANES), F32)
            for lanes in tiles(wide):
                gain = ff_ref[1:2, lanes]
                hat = (act[rows, lanes] - mean) * rate
                hats[rows, lanes] = hat.astype(B16)
                inner_ref[rows, lanes] = (hat * gain + ff_ref[2:3, lanes]).astype(B16)
                grad = grads[rows, lanes]
                product = grad * hat
                fold_sums[1, :, lanes] += fold(product)
                fold_sums[2, :, lanes] += fold(grad)
                first = first + grad * gain
                other = other + product * gain
            stat[rows, :] = first
            means[rows, :] = other

    stat[...] = row_mean(stat, wide)
    means[...] = row_mean(means, wide)
    total_ref[...] = mid_ref[...] + vec_ref[9:10, :]

    @pl.loop(0, PARTS)
    def _(part):
        columns = pl.ds(pl.multiple_of(part * span, LANES), span)
        total_ref[...] += dot(inner_ref[:, columns], wd[columns, :], NN)
        for rows in row_chunks(part):
            first, other, rate = stat[rows, :], means[rows, :], rates[rows, :]
            for lanes in tiles(wide):
                scaled = grads[rows, lanes] * ff_ref[1:2, lanes]
                grad = rate * (scaled - first - hats[rows, lanes].astype(F32) * other)
                pre = (grad * slopes[rows, lanes].astype(F32)).astype(B16)
                pre_grad[rows, lanes] = pre
                fold_sums[0, :, lanes] += fold(pre.astype(F32))

    result = total_ref[...].astype(B16)
    result_ref[0] = result
    write_away(away, step, chips, chunks_a, result)
    for which in range(2):

        @pl.when(core == which)
        def _(which=which):
            pre_keep[...] = pre_grad[:, which * wide // 2 : (which + 1) * wide // 2]
            pre_send[...] = pre_grad[:, (1 - which) * wide // 2 : (2 - which) * wide // 2]

    grad = dot(pre_grad[...], wu[...], NT)
    hat, rate = standardise(mid_ref[...])
    acc_ref[0:1, :] += sums(grad * hat)
    acc_ref[1:2, :] += sums(grad)
    cot = cot_ref[...].astype(F32)
    acc_ref[3:4, :] += sums(cot)
    mid = cot + standard_back(grad * vec_ref[7:8, :], hat, rate)
    mid_ref[...] = mid
    branch = mid.astype(B16)
    acc_ref[2:3, :] += sums(branch.astype(F32))
    for which in range(2):

        @pl.when(core == which)
        def _(which=which):
            branch_keep[...] = branch[:, which * width // 2 : (which + 1) * width // 2]
            branch_send[...] = branch[:, (1 - which) * width // 2 : (2 - which) * width // 2]

    grad = dot(branch, wo[...], NT)
    heads = o_ref[...]
    hat, rate = standardise(heads * scale_ref[0:1, :])
    acc_ref[4:5, :] += sums(grad * hat)
    acc_ref[5:6, :] += sums(grad)
    scaled = standard_back(grad * vec_ref[5:6, :], hat, rate)
    acc_ref[6:7, :] += sums(scaled * heads)
    head_ref[...] = (scaled * scale_ref[0:1, :]).astype(B16)

    @pl.when(step == pl.num_programs(0) - 1)
    def _():
        for k in range(3):
            ffacc_ref[k : k + 1, :] = sums(fold_sums[k])
        ffacc_ref[3:, :] = jnp.zeros((ffacc_ref.shape[0] - 3, wide), F32)


def feed(ids, x, cot, head_rows, vec, ff, scale, far, own, mine, other, n, chips, whole, block):
    rows, width = x.shape
    wide = ff.shape[1]
    chunks_a = whole * chips

    def rowed(lanes):
        return pl.BlockSpec((block, lanes), lambda i, s: (i, 0))

    def fixed(shape):
        return pl.BlockSpec(shape, lambda i, s: (0, 0))

    lanes = [width, width, wide, wide // 2, wide // 2, width // 2, width // 2]
    scratch = [(width, width), (width, wide), (wide, width)]
    return pl.pallas_call(
        partial(feed_kernel, n, chips, chunks_a),
        grid_spec=pltpu.PrefetchScalarGridSpec(
            num_scalar_prefetch=1,
            grid=(rows // block,),
            in_specs=[rowed(width)] * 3
            + [fixed(vec.shape), fixed(ff.shape), fixed(scale.shape)]
            + [ANYWHERE] * (2 * n),
            out_specs=[rowed(k) for k in lanes]
            + [
                pl.BlockSpec((1, block, width), home_index(chips, chunks_a)),
                rowed(width),
                rowed(width),
                fixed((8, width)),
                fixed((8, wide)),
            ]
            + [away_spec(block, width, chips, chunks_a)] * (chips - 1),
            scratch_shapes=[pltpu.VMEM(shape, B16) for shape in scratch]
            + [pltpu.VMEM((block, wide), F32)] * 2
            + [pltpu.VMEM((block, wide), B16)] * 3
            + [pltpu.VMEM((block, width), F32), pltpu.VMEM((3, 8, wide), F32)]
            + [pltpu.VMEM((block, LANES), F32)] * 3
            + [pltpu.SemaphoreType.DMA((3,))],
        ),
        out_shape=[jax.ShapeDtypeStruct((rows, k), B16) for k in lanes]
        + [
            jax.ShapeDtypeStruct((rows // block, block, width), B16),
            jax.ShapeDtypeStruct((rows, width), F32),
            jax.ShapeDtypeStruct((rows, width), B16),
            jax.ShapeDtypeStruct((8, width), F32),
            jax.ShapeDtypeStruct((8, wide), F32),
        ]
        + [jax.ShapeDtypeStruct((whole, block, width), B16)] * (chips - 1),
        compiler_params=params(),
        cost_estimate=cost(45),
        name="feed",
    )(ids, x, cot, head_rows, vec, ff, scale, far, own, *mine, *other)


def qkv_side_kernel(counts, factor, shards, rb, ids_ref, normed_ref, normed_other_ref, *refs):
    out_ref = refs[-1]
    step = pl.program_id(0)
    dq_refs, refs = refs[:4], refs[4:-1]

    def finish(out):
        out_ref[:, 0] = out.astype(B16).reshape(shards, rb, out.shape[1])

    @pl.when(step == 0)
    def _():
        rights = [jnp.concatenate([dq_refs[k][...], dq_refs[k + 1][...]], axis=0) for k in (0, 2)]
        finish((dot(normed_ref[...], rights[0], TN) + dot(normed_other_ref[...], rights[1], TN)) * factor)

    @pl.when(step > 0)
    def _():
        at, rights = 0, []
        for count in counts:
            first = add(*[r[0] for r in refs[at : at + count]]).astype(B16)
            rights.append(jnp.concatenate([first, refs[at + count][0]], axis=0))
            at += count + 1
        finish(dot(normed_ref[...], rights[0], TN) + dot(normed_other_ref[...], rights[1], TN))


def qkv_side(ids, normed, normed_other, dqs, dkvs, shards, rb, factor):
    rows, width = normed.shape
    half = width // 2
    whole = pl.BlockSpec((rows, width), lambda t, s: (0, 0))
    flat = [d for first, second in dkvs for d in list(first) + [second]]
    return pl.pallas_call(
        partial(qkv_side_kernel, [len(first) for first, _ in dkvs], factor, shards, rb),
        grid_spec=pltpu.PrefetchScalarGridSpec(
            num_scalar_prefetch=1,
            grid=(3,),
            in_specs=[whole, whole]
            + [pl.BlockSpec(d.shape, lambda t, s: (0, 0)) for d in dqs]
            + [pl.BlockSpec((1,) + d.shape[1:], lambda t, s: (jnp.maximum(t - 1, 0), 0, 0)) for d in flat],
            out_specs=pl.BlockSpec((shards, 1, rb, half), lambda t, s: (0, t, 0, 0)),
        ),
        out_shape=jax.ShapeDtypeStruct((shards, 3, rb, half), B16),
        compiler_params=params(),
        cost_estimate=cost(9),
        name="qkv_side",
    )(ids, normed, normed_other, *dqs, *flat)


def pair_kernel(groups, ids_ref, *refs):
    out_ref = refs[-1]
    block = pl.program_id(0)
    start = 0
    for g, blocks in enumerate(groups):
        left, left_other, right, right_other = refs[4 * g : 4 * g + 4]

        @pl.when((block >= start) & (block < start + blocks))
        def _(left=left, left_other=left_other, right=right, right_other=right_other):
            out = dot(left[...], right[...], TN) + dot(left_other[...], right_other[...], TN)
            out_ref[...] = out.astype(B16).reshape(out_ref.shape)

        start += blocks


def up_side_kernel(blocks, before, ids_ref, mixed_ref, branch_ref, second_ref, pre_ref, *refs):
    out_ref = refs[-1]
    step = pl.program_id(0)

    def finish(out):
        if before:
            out = out + refs[0][...].astype(F32).reshape(out.shape)
        out_ref[...] = out.astype(B16).reshape(out_ref.shape)

    @pl.when(step < blocks)
    def _():
        finish(dot(second_ref[...], pre_ref[...], TN))

    @pl.when(step >= blocks)
    def _():
        finish(dot(mixed_ref[...], branch_ref[...], TN))


def down_side(ids, inner, inner_other, cot, cot_other, into, rb):
    shards = into.shape[0]
    rows, wide = inner.shape
    width = cot.shape[1]
    half = width // 2
    blocks = wide // width
    group = width // (blocks * rb)
    left = pl.BlockSpec((rows, width), lambda g, s: (0, g))
    return pl.pallas_call(
        partial(pair_kernel, [blocks]),
        grid_spec=pltpu.PrefetchScalarGridSpec(
            num_scalar_prefetch=1,
            grid=(blocks,),
            in_specs=[
                left,
                left,
                pl.BlockSpec((rows, half), lambda g, s: (0, s[CORE])),
                pl.BlockSpec((rows, half), lambda g, s: (0, 0)),
                ANYWHERE,
            ],
            out_specs=pl.BlockSpec((group, blocks, rb, half), lambda g, s: (g, 0, 0, 0)),
        ),
        out_shape=jax.ShapeDtypeStruct(into.shape, B16),
        input_output_aliases={5: 0},
        compiler_params=params(),
        cost_estimate=cost(12),
        name="down_side",
    )(ids, inner, inner_other, cot, cot_other, into)


def up_side(ids, mixed, branch, second, pre, into, shards, rb):
    rows, width = mixed.shape
    half = width // 2
    blocks = pre.shape[1] // half
    first = blocks
    shape = (shards, 1 + 2 * blocks, rb, half)
    before = [] if into is None else [into]
    whole = pl.BlockSpec((rows, width), lambda b, s: (0, 0))
    out = pl.BlockSpec((shards, 1, rb, half), lambda b, s: (0, first + jnp.where(b < blocks, b + 1, 0), 0, 0))
    return pl.pallas_call(
        partial(up_side_kernel, blocks, into is not None),
        grid_spec=pltpu.PrefetchScalarGridSpec(
            num_scalar_prefetch=1,
            grid=(1 + blocks,),
            in_specs=[
                whole,
                pl.BlockSpec((rows, half), lambda b, s: (0, 0)),
                whole,
                pl.BlockSpec((rows, half), lambda b, s: (0, jnp.minimum(b, blocks - 1))),
            ]
            + [out] * len(before),
            out_specs=out,
        ),
        out_shape=jax.ShapeDtypeStruct(shape, B16),
        input_output_aliases={} if into is None else {5: 0},
        compiler_params=params(),
        cost_estimate=cost(8),
        name="up_side",
    )(ids, mixed, branch, second, pre, *before)


def terms_kernel(offsets, counts, far, ids_ref, *refs):
    outs = refs[-len(counts) :]
    at = 0
    for out, offset, count in zip(outs, offsets, counts):
        if far:
            total = refs[at][0].astype(F32)
            at += 1
        else:
            total = refs[0][ring_at(ids_ref[SPOT] + offset, refs[0].shape[0])].astype(F32)
            at = max(at, 1)
        for ref in refs[at : at + count]:
            total = total + ref[...].astype(F32)
        out[...] = total.astype(B16)
        at += count


def ring_terms(ids, terms, jobs, far):
    n, piece = terms.shape[0], terms.shape[1:]
    near = pl.BlockSpec(memory_space=pltpu.VMEM)
    zeros = (0,) * len(piece)
    args, specs = ([], []) if far else ([terms], [near])
    for offset, arrived in jobs:
        if far:
            args.append(terms)
            specs.append(
                pl.BlockSpec((1,) + piece, lambda i, s, offset=offset: (ring_at(s[SPOT] + offset, n),) + zeros)
            )
        args += list(arrived)
        specs += [near] * len(arrived)
    out_specs = [near] * len(jobs)
    if far:
        grid = dict(
            grid_spec=pltpu.PrefetchScalarGridSpec(
                num_scalar_prefetch=1, grid=(1,), in_specs=specs, out_specs=out_specs
            )
        )
    else:
        grid = dict(in_specs=[pl.BlockSpec(memory_space=pltpu.SMEM)] + specs, out_specs=out_specs)
    return pl.pallas_call(
        partial(terms_kernel, [offset for offset, _ in jobs], [len(arrived) for _, arrived in jobs], far),
        out_shape=[jax.ShapeDtypeStruct(piece, B16)] * len(jobs),
        compiler_params=params() if far else pltpu.CompilerParams(vmem_limit_bytes=10 * 1024 * 1024),
        cost_estimate=cost(2),
        name="ring_terms",
        **grid,
    )(ids, *args)


def small_kernel(ids_ref, acc_ref, first_ref, second_ref, wide_ref, table_ref, table_send_ref, out_ref):
    width = acc_ref.shape[1]
    core = ids_ref[CORE]
    out_ref[...] = jnp.zeros_like(out_ref)
    out_ref[0:8, :] = acc_ref[...]
    out_ref[8:16, :] = first_ref[...] + second_ref[...]
    blocks = wide_ref.shape[1] // width
    for k in range(3):
        for b in range(blocks):
            row = 16 + k * blocks + b
            out_ref[row : row + 1, :] = wide_ref[k : k + 1, b * width : (b + 1) * width]
    first = 16 + 3 * blocks
    count, lanes = table_ref.shape
    for which in range(2):

        @pl.when(core == which)
        def _(which=which):
            for group, at in ((table_ref, which), (table_send_ref, 1 - which)):
                out_ref[first + at * count : first + (at + 1) * count, 0:lanes] = group[...]


def small_sums(ids, acc, first, second, wide, table, table_send):
    width = acc.shape[1]
    rows = 16 + 3 * (wide.shape[1] // width) + 2 * table.shape[0]
    near = pl.BlockSpec(memory_space=pltpu.VMEM)
    return pl.pallas_call(
        small_kernel,
        in_specs=[pl.BlockSpec(memory_space=pltpu.SMEM)] + [near] * 6,
        out_specs=near,
        out_shape=jax.ShapeDtypeStruct((-(-rows // 8) * 8, width), F32),
        compiler_params=pltpu.CompilerParams(vmem_limit_bytes=4 * 1024 * 1024),
        cost_estimate=cost(2),
        name="small_sums",
    )(ids, acc, first, second, wide, table, table_send)


def finish_kernel(jobs, count, ids_ref, *refs):
    mine, other = refs[:count], refs[count : 2 * count]
    outs = refs[2 * count :]
    half = mine[0].shape[2]
    core = ids_ref[CORE]
    for group, own in ((mine, True), (other, False)):
        for which in range(2):

            @pl.when((core == which) == own)
            def _(group=group, which=which):
                for out, (first, blocks, stacked) in zip(outs, jobs):
                    for b in range(blocks):
                        value = add(*[r[first + b] for r in group])
                        rb = value.shape[0]
                        if stacked:
                            out[b * rb : (b + 1) * rb, which * half : (which + 1) * half] = value
                        else:
                            at = (which * blocks + b) * half
                            out[:, at : at + half] = value


def finish(ids, mine, other, jobs):
    rb, half = mine[0].shape[1:]
    shapes = [
        (blocks * rb, 2 * half) if stacked else (rb, 2 * blocks * half) for _, blocks, stacked in jobs
    ]
    near = pl.BlockSpec(memory_space=pltpu.VMEM)
    return pl.pallas_call(
        partial(finish_kernel, jobs, len(mine)),
        in_specs=[pl.BlockSpec(memory_space=pltpu.SMEM)] + [near] * (2 * len(mine)),
        out_specs=[near] * len(jobs),
        out_shape=[jax.ShapeDtypeStruct(shape, F32) for shape in shapes],
        compiler_params=pltpu.CompilerParams(vmem_limit_bytes=4 * 1024 * 1024),
        cost_estimate=cost(2),
        name="finish",
    )(ids, *mine, *other)


def tie(x, *others):
    return lax.optimization_barrier((x,) + others)[0]


class Places:
    def __init__(self):
        self.n = n = lax.axis_size("dp")
        self.seq = lax.axis_size("seq")
        self.chips = self.seq // 2
        self.ring = list(range(0, n, 2)) + [i for i in range(n) if i % 2][::-1]
        self.shard = shard = lax.axis_index("dp")
        seq = lax.axis_index("seq")
        self.core, self.chip = seq & 1, seq >> 1
        self.spot = jnp.where((shard & 1) == 0, shard >> 1, n - 1 - (shard >> 1))
        lane = lax.broadcasted_iota(jnp.int32, (8,), 0)
        ids = jnp.zeros((8,), jnp.int32)
        values = (self.spot, self.core, self.chip, shard, lax.rem(seq, GROUPS))
        for k, value in enumerate(values):
            ids = jnp.where(lane == k, value, ids)
        self.ids = ids

    def at(self, offset):
        return ring_at(self.spot + offset, self.n)

    def round(self, x, way):
        ring, n = self.ring, self.n
        return lax.ppermute(x, "dp", [(ring[i], ring[(i + way) % n]) for i in range(n)])

    def swap(self, x):
        return lax.ppermute(x, "seq", [(i, i ^ 1) for i in range(self.seq)])

    def chip_turn(self, x, by):
        n = self.chips
        perm = [(2 * i + c, 2 * ((i + by) % n) + c) for i in range(n) for c in range(2)]
        return lax.ppermute(x, "seq", perm)

    def chip_pair(self, x, bit):
        n = self.chips
        perm = [(2 * i + c, 2 * (i ^ bit) + c) for i in range(n) for c in range(2)]
        return lax.ppermute(x, "seq", perm)

    def seq_sums(self, total):
        bit, mine = 1, [total]
        while bit < self.chips:
            low = mine[0] if len(mine) == 1 else add(*mine).astype(B16)
            mine = [low, self.chip_pair(low, bit)]
            bit *= 2
        return mine, [self.swap(x) for x in mine]

    def total_steps(self):
        def over(axis, size, low, high):
            def step(x):
                far = {
                    bit: lax.ppermute(x, axis, [(i, i ^ bit) for i in range(size)])
                    for bit in (low, high, low | high)
                    if bit
                }

                def arrived(value):
                    own = tie(x, value)
                    if low == 0 or high == 0:
                        return own + far[low | high]
                    return (own + far[low]) + (far[high] + far[low | high])

                return arrived

            return step

        steps = []
        for axis, size in (("dp", self.n), ("seq", self.seq)):
            bits = [1 << k for k in range(size.bit_length() - 1)]
            while bits:
                high = bits.pop()
                steps.append(over(axis, size, bits.pop() if bits else 0, high))
        return steps


class RingGather:
    def __init__(self, here, own):
        self.here, self.k = here, 0
        self.forwards, self.backwards = [own], [own]

    def round(self):
        self.k += 1
        self.forwards.append(self.here.round(self.forwards[-1], 1))
        if self.k <= (self.here.n - 1) // 2:
            self.backwards.append(self.here.round(self.backwards[-1], -1))

    def settle(self, *values):
        out = lax.optimization_barrier((self.forwards[-1], self.backwards[-1]) + values)
        self.forwards[-1], self.backwards[-1] = out[:2]
        return out[2:]

    def finish(self):
        while self.k < self.here.n // 2:
            self.round()
        pieces = self.forwards[1:] + self.backwards[1:]
        return pieces, [self.here.swap(piece) for piece in pieces]


class RingSum:
    def __init__(self, here, terms, far):
        self.here, self.terms, self.far = here, terms, far
        self.k = here.n // 2
        self.forward = self.backward = None

    def after(self, *values):
        if self.forward is not None:
            self.forward = tie(self.forward, *values)
        if self.backward is not None:
            self.backward = tie(self.backward, *values)

    def jobs(self, ahead, behind):
        forward = [] if self.forward is None else [self.forward]
        backward = [] if self.backward is None else [self.backward]
        return [(ahead, forward)] + ([] if behind is None else [(behind, backward)])

    def round(self):
        both = self.k <= (self.here.n - 1) // 2
        terms = ring_terms(self.here.ids, self.terms, self.jobs(self.k, -self.k if both else None), self.far)
        self.forward = self.here.round(terms[0], 1)
        if both:
            self.backward = self.here.round(terms[1], -1)
        self.k -= 1
        return terms[0]

    def done(self):
        arrived = [x for x in (self.forward, self.backward) if x is not None]
        return ring_terms(self.here.ids, self.terms, [(0, arrived)], self.far)[0]


def local(
    tokens,
    cotangent,
    segment_ids,
    bucket_ids,
    key_mask,
    query_weight,
    key_weight,
    value_weight,
    output_weight,
    query_bias,
    value_bias,
    output_bias,
    first_gain,
    first_shift,
    mixed_gain,
    mixed_shift,
    up_weight,
    down_weight,
    up_bias,
    down_bias,
    second_gain,
    second_shift,
    inner_gain,
    inner_shift,
    bias_table,
    head_scale,
):
    items, own_rows, width = tokens.shape
    heads = head_scale.shape[0]
    head_width = width // heads
    groups = bias_table.shape[0] // 2
    factor = float(head_width) ** (-0.5)
    wide = up_weight.shape[1]
    wide_rows = wide // width
    rb = query_weight.shape[0]
    here = Places()
    n, chips, ids = here.n, here.chips, here.ids
    whole = items // chips
    left = items - whole * chips
    rows_a = whole * chips * own_rows
    rows_c = left * own_rows

    far = pack_far(ids, up_weight, down_weight)
    far = lax.all_gather(far, ("dp", "seq"), axis=0, tiled=False)
    smalls = [
        query_bias,
        value_bias,
        output_bias,
        first_gain,
        first_shift,
        mixed_gain,
        mixed_shift,
        second_gain,
        second_shift,
        down_bias,
    ]
    wides = [up_bias, inner_gain, inner_shift]
    small = jnp.concatenate([v.reshape(1, rb) for v in smalls] + [v.reshape(-1, rb) for v in wides])
    small = jnp.pad(small, ((0, SMALL_ROWS - small.shape[0]), (0, LANES - rb)))
    own = (query_weight, key_weight, value_weight)
    near = pack_near(ids, own + (output_weight,), small)
    near_ring = RingGather(here, near)
    near_ring.round()

    def take(array, by):
        mine = [
            lax.dynamic_index_in_dim(array, k * chips + lax.rem(here.chip + by, chips), 0, keepdims=False)
            for k in range(whole)
        ]
        return jnp.stack(mine)

    codes = bucket_ids + groups * segment_ids + 2 * groups * (key_mask > 0).astype(jnp.int32)
    turned = [codes] + [here.chip_turn(tie(codes, near), by) for by in range(1, chips)]
    recv = [here.chip_turn(tie(take(tokens, by), near), by) for by in range(1, chips)]
    near_ring.settle()
    near_ring.round()
    out = near_ring.settle(*turned, *recv)
    turned, recv = list(out[:chips]), list(out[chips:])
    turned = turned + [here.swap(c) for c in turned]
    near_ring.round()
    aux, hot, tab, scale = prep(ids, turned, bias_table, head_scale, chips, whole, left, width)
    aux, hot, tab, scale = near_ring.settle(aux, hot, tab, scale)
    near_ring.round()
    mine, other = near_ring.finish()

    x, normed, q, kv_a, kv_c, vec = project(
        tie(ids, aux), tokens, recv, own, small, mine, other, n, chips, whole, factor
    )
    kv_c = kv_c.reshape(2, left, own_rows, width)
    kvs_c = [here.chip_turn(kv_c, by) for by in range(1, chips)]
    kv_a = kv_a.reshape(2, whole, chips * own_rows, width)
    kvs_a = [kv_a, here.swap(kv_a)]
    own_c = [kv_c, here.swap(kv_c)]
    normed_other = here.swap(normed)
    q_a, q_c = chips * own_rows, own_rows
    ff = vec[len(smalls) : len(smalls) + 3 * wide_rows]
    ff = ff.reshape(3, wide_rows, n, rb).transpose(0, 2, 1, 3).reshape(3, wide)
    ff = jnp.pad(ff, ((0, 5), (0, 0)))

    head_rows, logs_a = attend(q, kvs_a, tie(aux, ff), hot, tab, 0, 0, q_a, whole, None)
    kvs_c = [tie(kv, logs_a) for kv in kvs_c]
    cot = [take(cotangent, by) for by in range(1, chips)]
    cot = [here.chip_turn(tie(x, *kvs_c), by) for by, x in enumerate(cot, 1)]
    kvs_c = own_c[:1] + kvs_c + own_c[1:] + [here.swap(kv) for kv in kvs_c]
    head_rows, logs_c = attend(q, kvs_c, aux, hot, tab, whole, rows_a, q_c, left, head_rows)
    cot = jnp.concatenate([take(cotangent, 0)] + [tie(x, logs_c) for x in cot], axis=1)
    cot = jnp.concatenate([cot.reshape(rows_a, width), cotangent[whole * chips :].reshape(rows_c, width)])
    cot_half = lax.dynamic_slice_in_dim(cot, (1 - here.core) * (width // 2), width // 2, axis=1)
    cot_other = here.swap(cot_half)

    outs = feed(
        ids, x, cot, head_rows, vec, ff, scale, far, output_weight, mine, other, n, chips, whole, own_rows
    )
    mixed, second, inner, pre, pre_send, branch, branch_send = outs[:7]
    result, mid, head_grad, acc, ff_acc = outs[7:12]
    pre_other, second_other, mixed_other, branch_other = [
        here.swap(part) for part in (pre_send, second, mixed, branch_send)
    ]
    far_terms = up_side(ids, mixed, branch, second, pre, None, n, rb)
    inner_other = here.swap(tie(inner, pre_other, second_other))
    far_terms = up_side(ids, mixed_other, branch_other, second_other, pre_other, far_terms, n, rb)
    far_terms = down_side(ids, inner, inner_other, cot, cot_other, far_terms, rb)
    far_total = lax.psum_scatter(far_terms, "dp", scatter_dimension=0, tiled=False)
    result_away = [here.chip_turn(part, -by) for by, part in enumerate(outs[12:], 1)]

    pairs = heads // 2

    def back(unit, own, aux):
        kvs, logs, item, row, q_rows, count = unit
        return attend_back(
            ids, q, kvs, aux, hot, tab, head_grad, head_rows, logs, item, row, q_rows, count, own
        )

    unit_c = (kvs_c, logs_c, whole, rows_a, q_c, left)
    unit_a = (kvs_a, logs_a, 0, 0, q_a, whole)
    dq_c_send, own_c_send, other_c_send, g_c_send = back(unit_c, False, tie(aux, far_terms))
    dq_c, own_c, other_c, g_c = back(unit_c, True, aux)

    def near_sum(mine, theirs):
        return add(mine, theirs).astype(B16).reshape(2, left, chips, own_rows, -1)

    def far_parts(near):
        return [near[:, :, 0]] + [here.chip_turn(near[:, :, by], -by) for by in range(1, chips)]

    parts_c = far_parts(near_sum(own_c, here.swap(other_c_send)))
    other_c = here.swap(other_c)
    dq_a_send, own_a_send, other_a_send, g_a_send = back(unit_a, False, tie(aux, parts_c[0]))
    parts_c_send = far_parts(near_sum(own_c_send, tie(other_c, dq_a_send)))
    dq_a_other, own_a_other, other_a_other = [here.swap(x) for x in (dq_a_send, own_a_send, other_a_send)]
    dq_a, own_a, other_a, g_a = back(unit_a, True, tie(aux, parts_c_send[0], *result_away))
    mine_a = here.swap(other_a)

    def c_rows(parts):
        return add(*[tie(p, dq_a) for p in parts]).astype(B16).reshape(2, rows_c, -1)

    dkv_c, dkv_c_send = c_rows(parts_c), c_rows(parts_c_send)
    dkv_c_other, dq_c_other = here.swap(dkv_c_send), here.swap(dq_c_send)

    def a_rows(x):
        return x.reshape(2, rows_a, -1)

    qkv_terms = qkv_side(
        ids,
        normed,
        normed_other,
        [dq_a, dq_c, dq_a_other, dq_c_other],
        [
            ([a_rows(own_a), a_rows(other_a_other)], dkv_c),
            ([a_rows(other_a), a_rows(own_a_other)], dkv_c_other),
        ],
        n,
        rb,
        factor,
    )
    qkv_ring = RingSum(here, qkv_terms, False)

    def rows_back(span, x, dqs, dkvs, into):
        return project_back(
            ids, x, dqs, dkvs, mid, vec, own, mine, other, n, chips, whole, own_rows, factor, span, into
        )

    sent = qkv_ring.round()
    chunks_a = whole * chips
    grad_rows, late_c = rows_back(
        (chunks_a, left), tie(x, sent), [dq_c, dq_c_send], [[dkv_c], [dkv_c_send]], None
    )
    qkv_ring.after(late_c)
    sent = qkv_ring.round()
    grad_rows, late_a, *grad_away = rows_back(
        (0, chunks_a),
        tie(x, sent),
        [dq_a, dq_a_send],
        [
            [a_rows(own_a), a_rows(other_a_other)],
            [a_rows(own_a_send), a_rows(mine_a)],
        ],
        grad_rows,
    )

    offset = jnp.arange(groups)
    spread = (
        (offset[:, None, None] - offset[None, :, None]) % groups == offset[None, None, :]
    ).astype(F32)

    def table_of(*parts):
        g = sum(jnp.sum(tie(part, late_c), axis=0) for part in parts)
        g = g.reshape(heads // 2, groups, 2, groups)
        table = jnp.einsum("hcsb,cbo->hso", g, spread, precision=lax.Precision.HIGHEST)
        return table.reshape(heads // 2, 2 * groups)

    summed = small_sums(ids, acc, late_a, late_c, ff_acc, table_of(g_c, g_a), table_of(g_c_send, g_a_send))

    steps = here.total_steps()
    qkv_ring.after(late_a)
    sent = qkv_ring.round()
    grad_away = [here.chip_turn(tie(part, sent), -by) for by, part in enumerate(grad_away, 1)]
    moved = steps.pop(0)(tie(summed, sent))
    while qkv_ring.k > 0:
        sent = qkv_ring.round()
        if steps:
            moved = steps.pop(0)(moved(sent))
    qkv_ring.after(*grad_away)
    qkv_total = qkv_ring.done()
    far_sums = here.seq_sums(tie(far_total, qkv_total))
    while steps:
        moved = steps.pop(0)(moved(qkv_total))
    summed = moved(qkv_total)

    query_weight_grad, key_weight_grad, value_weight_grad = finish(
        ids, *here.seq_sums(qkv_total), [(0, 1, False), (1, 1, False), (2, 1, False)]
    )
    down_weight_grad, output_weight_grad, up_weight_grad = finish(
        ids, *far_sums, [(0, wide_rows, True), (wide_rows, 1, False), (wide_rows + 1, wide_rows, False)]
    )
    mine = lax.dynamic_slice_in_dim(summed[:16], here.shard * rb, rb, axis=1)
    ff_sums = summed[16 : 16 + 3 * wide_rows].reshape(3, wide)
    ff_mine = lax.dynamic_slice_in_dim(ff_sums, here.shard * (wide // n), wide // n, axis=1)
    first = 16 + 3 * wide_rows
    table_grad = jnp.transpose(summed[first : first + heads, : 2 * groups])
    scale_grad = jnp.sum(summed[6].reshape(heads, head_width), axis=1)

    def home(array, away):
        for by, part in enumerate(away, 1):
            part = part.astype(array.dtype)
            for k in range(whole):
                item = k * chips + lax.rem(here.chip + by, chips)
                array = lax.dynamic_update_index_in_dim(array, part[k], item, 0)
        return array

    return (
        home(result, result_away),
        home(grad_rows, grad_away),
        query_weight_grad,
        key_weight_grad,
        value_weight_grad,
        output_weight_grad,
        mine[10],
        mine[11],
        mine[2],
        mine[8],
        mine[9],
        mine[4],
        mine[5],
        up_weight_grad,
        down_weight_grad,
        ff_mine[0],
        mine[3],
        mine[0],
        mine[1],
        ff_mine[1],
        ff_mine[2],
        table_grad,
        scale_grad,
    )


def solution(mesh):
    rowed, shard, vector, whole = P("dp", "seq", None), P("dp", None), P("dp"), P()
    flat = P("dp", "seq")
    placed = (rowed,) * 2 + (flat,) * 3 + (shard,) * 4 + (vector,) * 7 + (shard,) * 2 + (vector,) * 6
    placed = placed + (whole,) * 2
    outs = (rowed,) * 2 + (shard,) * 4 + (vector,) * 7 + (shard,) * 2 + (vector,) * 6 + (whole,) * 2
    return jax.shard_map(local, mesh=mesh, in_specs=placed, out_specs=outs, check_vma=False)
```

```python
from functools import partial

import jax
import jax.numpy as jnp
from jax import lax
from jax.experimental import pallas as pl
from jax.experimental.pallas import tpu as pltpu
from jax.sharding import PartitionSpec as P

EPSILON = 1e-05
FLOOR_SCORE = -1e30
F32 = jnp.float32
B16 = jnp.bfloat16
NN = (((1,), (0,)), ((), ()))
NT = (((1,), (1,)), ((), ()))
TN = (((0,), (0,)), ((), ()))
VMEM_LIMIT = 60 * 1024 * 1024
SMALL_ROWS = 32
LANES = 128


def dot(a, b, dims, **kw):
    return lax.dot_general(a, b, dims, preferred_element_type=F32, **kw)


def params():
    return pltpu.CompilerParams(vmem_limit_bytes=VMEM_LIMIT)


def cost(micros):
    return pl.CostEstimate(flops=int(micros * 1.1e9), bytes_accessed=0, transcendentals=0)


def low_lanes(shape):
    return lax.broadcasted_iota(jnp.int32, shape, 1) < shape[1] // 2


def low_rows(shape):
    return lax.broadcasted_iota(jnp.int32, shape, 0) < shape[0] // 2


def standardise(values):
    mean = jnp.mean(values, axis=-1, keepdims=True)
    centred = values - mean
    spread = jnp.mean(centred * centred, axis=-1, keepdims=True)
    rate = lax.rsqrt(spread + EPSILON)
    return centred * rate, rate


def standard_back(hat_grad, hat, rate):
    first = jnp.mean(hat_grad, axis=-1, keepdims=True)
    second = jnp.mean(hat_grad * hat, axis=-1, keepdims=True)
    return rate * (hat_grad - first - hat * second)


def add(*parts):
    return sum(p.astype(F32) for p in parts)


def sums(array):
    return jnp.sum(array, axis=0, keepdims=True)


SPOT, CORE, CHIP, SHARD, GROUP = range(5)
GROUPS = 4


def ring_at(spot, n):
    spot = lax.rem(spot + 2 * n, n)
    return jnp.where(spot < (n + 1) // 2, 2 * spot, 2 * n - 1 - 2 * spot)


def piece_shards(ids, n):
    spot = ids[SPOT]
    out = [ids[SHARD]]
    out += [ring_at(spot - k, n) for k in range(1, n // 2 + 1)]
    out += [ring_at(spot + k, n) for k in range(1, (n - 1) // 2 + 1)]
    return out


def wait_whole(target, sem):
    pltpu.make_async_copy(target, target, sem).wait()


ANYWHERE = pl.BlockSpec(memory_space=pl.ANY)


def pack_near_kernel(ids_ref, q_ref, k_ref, v_ref, o_ref, small_ref, near_ref):
    rb = q_ref.shape[0]
    for t, ref in enumerate((q_ref, k_ref, v_ref, o_ref)):
        near_ref[t * rb : (t + 1) * rb, :] = ref[...]
    near_ref[4 * rb :, :] = jnp.zeros((SMALL_ROWS, near_ref.shape[1]), B16)
    near_ref[4 * rb :, 0:LANES] = small_ref[...]


def pack_near(ids, weights, small):
    rb, width = weights[0].shape
    half = width // 2
    return pl.pallas_call(
        pack_near_kernel,
        grid_spec=pltpu.PrefetchScalarGridSpec(
            num_scalar_prefetch=1,
            grid=(1,),
            in_specs=[pl.BlockSpec((rb, half), lambda i, s: (0, s[CORE]))] * 4
            + [pl.BlockSpec(small.shape, lambda i, s: (0, 0))],
            out_specs=pl.BlockSpec((4 * rb + SMALL_ROWS, half), lambda i, s: (0, 0)),
        ),
        out_shape=jax.ShapeDtypeStruct((4 * rb + SMALL_ROWS, half), B16),
        compiler_params=params(),
        cost_estimate=cost(2),
        name="pack_near",
    )(ids, *weights, small)


def pack_far_kernel(ids_ref, up_ref, down_ref, far_ref):
    part = up_ref.shape[1]
    far_ref[:, :part] = up_ref[...]
    far_ref[:, part:] = down_ref[...]


def pack_far(ids, up, down):
    rb, wide = up.shape
    width = down.shape[1]
    part = wide // GROUPS
    return pl.pallas_call(
        pack_far_kernel,
        grid_spec=pltpu.PrefetchScalarGridSpec(
            num_scalar_prefetch=1,
            grid=(1,),
            in_specs=[
                pl.BlockSpec((rb, part), lambda i, s: (0, s[GROUP])),
                pl.BlockSpec((rb, width), lambda i, s: (s[GROUP], 0)),
            ],
            out_specs=pl.BlockSpec((rb, part + width), lambda i, s: (0, 0)),
        ),
        out_shape=jax.ShapeDtypeStruct((rb, part + width), B16),
        compiler_params=params(),
        cost_estimate=cost(2),
        name="pack_far",
    )(ids, up, down)


def prep_kernel(chips, whole, left, ids_ref, *refs):
    code_refs = refs[: 2 * chips]
    table_ref, scale_in_ref = refs[2 * chips : 2 * chips + 2]
    aux_ref, hot_ref, tab_ref, scale_ref = refs[2 * chips + 2 :]
    rows = code_refs[0].shape[1]
    levels = tab_ref.shape[0] // 2
    width = tab_ref.shape[1]
    chip = ids_ref[CHIP]

    def column(item, source):
        code = code_refs[source][pl.ds(item, 1), :]
        level = lax.broadcasted_iota(jnp.int32, (LANES, rows), 0) % (2 * levels)
        hit = jnp.where(level == code % levels, 1.0, 0.0)
        floor = jnp.where((level == levels) & (code < 2 * levels), FLOOR_SCORE, 0.0)
        return jnp.transpose(jnp.where(level < levels, hit, floor)).astype(B16)

    def own(item, source):
        code = code_refs[source][pl.ds(item, 1), :]
        level = lax.broadcasted_iota(jnp.int32, (LANES, rows), 0)
        hit = jnp.where(level == code % (2 * levels), 1.0, 0.0)
        return jnp.transpose(hit).astype(B16)[:, : 2 * levels]

    for item in range(whole + left):
        row = item * chips + chip if item < whole else whole * chips + item - whole
        for source in range(2 * chips):
            aux_ref[item, source * rows : (source + 1) * rows, :] = column(row, source)
    for k in range(whole):
        for source in range(chips):
            start = (k * chips + source) * rows
            hot_ref[start : start + rows, :] = own(k * chips + chip, source)
    for k in range(left):
        start = (whole * chips + k) * rows
        hot_ref[start : start + rows, :] = own(whole * chips + k, 0)

    head = lax.broadcasted_iota(jnp.int32, (LANES, width), 0)
    lane = lax.broadcasted_iota(jnp.int32, (LANES, width), 1)
    owner = lane // LANES * 2 + 1 - lane % LANES // (LANES // 2)
    spread = jnp.where(head == owner, 1.0, 0.0).astype(B16)
    by_lane = dot(table_ref[...], spread, NN)
    lane = lax.broadcasted_iota(jnp.int32, (levels, width), 1) % (2 * levels)
    bucket = lax.broadcasted_iota(jnp.int32, (levels, width), 0)
    turn = jnp.where(lane < levels, (lane - bucket) & (levels - 1), -1)
    for segment in range(2):
        out = jnp.where(lane == levels, 1.0, 0.0)
        for o in range(levels):
            line = by_lane[segment * levels + o : segment * levels + o + 1, :]
            out = jnp.where(turn == o, line, out)
        tab_ref[segment * levels : (segment + 1) * levels, :] = out.astype(B16)
    lane = lax.broadcasted_iota(jnp.int32, (LANES, width), 1)
    spread = jnp.where(head == lane // (LANES // 2), 1.0, 0.0).astype(B16)
    scale_ref[...] = dot(scale_in_ref[...], spread, NN)


def prep(ids, codes, table, head_scale, chips, whole, left, width):
    rows = codes[0].shape[1]
    table = jnp.pad(table, ((0, 0), (0, LANES - table.shape[1])))
    scale = jnp.pad(head_scale[None], ((0, 15), (0, LANES - head_scale.shape[0])))
    levels = table.shape[0]
    q_rows = (whole * chips + left) * rows

    def fixed(shape):
        return pl.BlockSpec(shape, lambda i, s: (0,) * len(shape))

    outs = [(whole + left, 2 * chips * rows, LANES), (q_rows, levels), (levels, width), (16, width)]
    return pl.pallas_call(
        partial(prep_kernel, chips, whole, left),
        grid_spec=pltpu.PrefetchScalarGridSpec(
            num_scalar_prefetch=1,
            grid=(1,),
            in_specs=[fixed(c.shape) for c in codes] + [fixed(table.shape), fixed(scale.shape)],
            out_specs=[fixed(o) for o in outs],
        ),
        out_shape=[
            jax.ShapeDtypeStruct(outs[0], B16),
            jax.ShapeDtypeStruct(outs[1], B16),
            jax.ShapeDtypeStruct(outs[2], B16),
            jax.ShapeDtypeStruct(outs[3], F32),
        ],
        compiler_params=params(),
        cost_estimate=cost(3),
        name="prep",
    )(ids, *codes, table, scale)


def load_qkv(ids_ref, n, rb, half, own, mine, other, targets, sems):
    shards = piece_shards(ids_ref, n)
    core = ids_ref[CORE]
    starts = [pl.multiple_of(shard * rb, 16) for shard in shards]
    here = pl.multiple_of(core * half, LANES)
    there = pl.multiple_of((1 - core) * half, LANES)
    for t, target in enumerate(targets):
        pltpu.make_async_copy(own[t], target.at[pl.ds(starts[0], rb), :], sems.at[t]).start()
        for j in range(n - 1):
            rows = pl.ds(starts[j + 1], rb)
            part = pl.ds(t * rb, rb)
            pltpu.make_async_copy(
                mine[j].at[part, :], target.at[rows, pl.ds(here, half)], sems.at[t]
            ).start()
            pltpu.make_async_copy(
                other[j].at[part, :], target.at[rows, pl.ds(there, half)], sems.at[t]
            ).start()


def project_kernel(n, chips, chunks_a, factor, ids_ref, x_ref, *refs):
    recv = refs[: chips - 1]
    refs = refs[chips - 1 :]
    own, own_small = refs[:3], refs[3]
    mine, other = refs[4 : 4 + n - 1], refs[4 + n - 1 : 4 + 2 * (n - 1)]
    refs = refs[4 + 2 * (n - 1) :]
    x_out, normed_ref, q_ref, kva_ref, kvc_ref, vec_ref = refs[:6]
    wq, wk, wv, small, sems = refs[6:]
    rb = own[0].shape[0]
    half = wq.shape[1] // 2
    step = pl.program_id(0)

    @pl.when(step == 0)
    def _():
        pltpu.make_async_copy(own_small, small.at[0], sems.at[3]).start()
        for j in range(n - 1):
            pltpu.make_async_copy(
                mine[j].at[pl.ds(4 * rb, SMALL_ROWS), pl.ds(0, LANES)], small.at[j + 1], sems.at[3]
            ).start()
        load_qkv(ids_ref, n, rb, half, own, mine, other, (wq, wk, wv), sems)
        wait_whole(small, sems.at[3])
        total = jnp.zeros(vec_ref.shape, F32)
        row = lax.broadcasted_iota(jnp.int32, (LANES, wq.shape[1]), 0)
        col = lax.broadcasted_iota(jnp.int32, (LANES, wq.shape[1]), 1)
        for j, shard in enumerate(piece_shards(ids_ref, n)):
            spot = jnp.where((row < rb) & (col == row + shard * rb), 1.0, 0.0).astype(B16)
            total = total + dot(small[j], spot, NN)
        vec_ref[...] = total
        for t, target in enumerate((wq, wk, wv)):
            wait_whole(target, sems.at[t])

    x = x_ref[0]
    for s in range(1, chips):
        x = jnp.where((step < chunks_a) & (lax.rem(step, chips) == s), recv[s - 1][0], x)
    x_out[...] = x
    hat, _ = standardise(x.astype(F32))
    normed = (hat * vec_ref[3:4, :] + vec_ref[4:5, :]).astype(B16)
    normed_ref[...] = normed
    q_ref[...] = ((dot(normed, wq[...], NN) + vec_ref[0:1, :]) * factor).astype(B16)
    keys = dot(normed, wk[...], NN).astype(B16)
    values = (dot(normed, wv[...], NN) + vec_ref[1:2, :]).astype(B16)

    @pl.when(step < chunks_a)
    def _():
        kva_ref[0] = keys
        kva_ref[1] = values

    @pl.when(step >= chunks_a)
    def _():
        kvc_ref[0] = keys
        kvc_ref[1] = values


def project(ids, tokens, recv, own, small, mine, other, n, chips, whole, factor):
    items, rows, width = tokens.shape
    chunks_a = whole * chips
    rowed = pl.BlockSpec((rows, width), lambda i, s: (i, 0))

    def item(i, s):
        own_item = jnp.minimum(i, chunks_a - 1) // chips * chips + s[CHIP]
        return (jnp.where(i < chunks_a, own_item, i), 0, 0)

    received = pl.BlockSpec((1, rows, width), lambda i, s: (jnp.minimum(i, chunks_a - 1) // chips, 0, 0))
    total = items * rows
    return pl.pallas_call(
        partial(project_kernel, n, chips, chunks_a, factor),
        grid_spec=pltpu.PrefetchScalarGridSpec(
            num_scalar_prefetch=1,
            grid=(items,),
            in_specs=[pl.BlockSpec((1, rows, width), item)]
            + [received] * len(recv)
            + [ANYWHERE] * (4 + 2 * (n - 1)),
            out_specs=[
                rowed,
                rowed,
                rowed,
                pl.BlockSpec((2, rows, width), lambda i, s: (0, jnp.minimum(i, chunks_a - 1), 0)),
                pl.BlockSpec((2, rows, width), lambda i, s: (0, jnp.maximum(i - chunks_a, 0), 0)),
                pl.BlockSpec((SMALL_ROWS, width), lambda i, s: (0, 0)),
            ],
            scratch_shapes=[pltpu.VMEM((width, width), B16)] * 3
            + [pltpu.VMEM((n,) + small.shape, B16), pltpu.SemaphoreType.DMA((4,))],
        ),
        out_shape=[
            jax.ShapeDtypeStruct((total, width), B16),
            jax.ShapeDtypeStruct((total, width), B16),
            jax.ShapeDtypeStruct((total, width), B16),
            jax.ShapeDtypeStruct((2, chunks_a * rows, width), B16),
            jax.ShapeDtypeStruct((2, total - chunks_a * rows, width), B16),
            jax.ShapeDtypeStruct((SMALL_ROWS, width), F32),
        ],
        compiler_params=params(),
        cost_estimate=cost(10),
        name="project",
    )(ids, tokens, *recv, *own, small, *mine, *other)


def home_index(chips, chunks_a):
    def at(i, s):
        k, by = i // chips, lax.rem(i, chips)
        return (jnp.where(i < chunks_a, k * chips + lax.rem(s[CHIP] + by, chips), i), 0, 0)

    return at


def away_spec(rows, width, chips, chunks_a):
    return pl.BlockSpec((1, rows, width), lambda i, s: (jnp.minimum(i, chunks_a - 1) // chips, 0, 0))


def write_away(refs, step, chips, chunks_a, value):
    for s, ref in enumerate(refs, 1):

        @pl.when((step < chunks_a) & (lax.rem(step, chips) == s))
        def _(ref=ref):
            ref[0] = value.astype(ref.dtype)


def project_back_kernel(n, chips, chunks_a, first, fresh, count, factor, ids_ref, x_ref, mid_ref, vec_ref, *refs):
    dq_refs, dkv_refs = refs[:2], (refs[2 : 2 + count], refs[2 + count : 2 + 2 * count])
    refs = refs[2 + 2 * count :]
    own = refs[:3]
    mine, other = refs[3 : 3 + n - 1], refs[3 + n - 1 : 3 + 2 * (n - 1)]
    refs = refs[3 + 2 * (n - 1) :]
    if not fresh:
        refs = refs[1:]
    out_ref, acc_ref = refs[:2]
    away = refs[2:-5]
    wq, wk, wv, joined, sems = refs[-5:]
    rb, half = own[0].shape[0], wq.shape[1] // 2
    step = pl.program_id(0) + first
    core = ids_ref[CORE]

    @pl.when(step == first)
    def _():
        load_qkv(ids_ref, n, rb, half, own, mine, other, (wq, wk, wv), sems)
        acc_ref[...] = jnp.zeros_like(acc_ref)

    for h, place in enumerate((core, 1 - core)):
        lanes = pl.ds(pl.multiple_of(place * half, LANES), half)
        joined[0, :, lanes] = dq_refs[h][...]
        for t in range(2):
            value = dkv_refs[h][0][t] if count == 1 else add(*[r[t] for r in dkv_refs[h]]).astype(B16)
            joined[1 + t, :, lanes] = value

    @pl.when(step == first)
    def _():
        for t, target in enumerate((wq, wk, wv)):
            wait_whole(target, sems.at[t])

    dq, dk, dv = joined[0], joined[1], joined[2]
    grad = factor * dot(dq, wq[...], NT) + dot(dk, wk[...], NT) + dot(dv, wv[...], NT)
    hat, rate = standardise(x_ref[...].astype(F32))
    out = mid_ref[...] + standard_back(grad * vec_ref[3:4, :], hat, rate)
    out_ref[0] = out
    if first < chunks_a:
        write_away(away, step, chips, chunks_a, out)
    acc_ref[0:1, :] += sums(grad * hat)
    acc_ref[1:2, :] += sums(grad)
    acc_ref[2:3, :] += factor * sums(dq.astype(F32))
    acc_ref[3:4, :] += sums(dv.astype(F32))


def project_back(ids, x, dqs, dkvs, mid, vec, own, mine, other, n, chips, whole, rows, factor, span, into):
    total, width = x.shape
    items, chunks_a = total // rows, whole * chips
    first, count = span
    rowed = pl.BlockSpec((rows, width), lambda i, s: (first + i, 0))
    at = home_index(chips, chunks_a)
    fresh = into is None
    away = chips - 1 if first < chunks_a else 0
    flat = list(dqs) + [d for group in dkvs for d in group]
    n_args = 4 + len(flat) + 3 + 2 * (n - 1)
    return pl.pallas_call(
        partial(project_back_kernel, n, chips, chunks_a, first, fresh, len(dkvs[0]), factor),
        grid_spec=pltpu.PrefetchScalarGridSpec(
            num_scalar_prefetch=1,
            grid=(count,),
            in_specs=[rowed, rowed, pl.BlockSpec(vec.shape, lambda i, s: (0, 0))]
            + [pl.BlockSpec((rows, width // 2), lambda i, s: (i, 0))] * 2
            + [pl.BlockSpec((2, rows, width // 2), lambda i, s: (0, i, 0))] * (len(flat) - 2)
            + [ANYWHERE] * (3 + 2 * (n - 1) + (0 if fresh else 1)),
            out_specs=[
                pl.BlockSpec((1, rows, width), lambda i, s: at(first + i, s)),
                pl.BlockSpec((8, width), lambda i, s: (0, 0)),
            ]
            + [away_spec(rows, width, chips, chunks_a)] * away,
            scratch_shapes=[pltpu.VMEM((width, width), B16)] * 3
            + [pltpu.VMEM((3, rows, width), B16), pltpu.SemaphoreType.DMA((3,))],
        ),
        out_shape=[
            jax.ShapeDtypeStruct((items, rows, width), F32),
            jax.ShapeDtypeStruct((8, width), F32),
        ]
        + [jax.ShapeDtypeStruct((whole, rows, width), B16)] * away,
        input_output_aliases={} if fresh else {n_args: 0},
        compiler_params=params(),
        cost_estimate=cost(8),
        name="project_back",
    )(ids, x, mid, vec, *flat, *own, *mine, *other, *([] if fresh else [into]))


def score_operands(qp, kp, aux, hot, tab):
    rel = dot(hot, tab, NN).astype(B16)
    lq, lk = low_lanes(qp.shape), low_lanes(kp.shape)
    return (
        (jnp.where(lq, qp, rel), jnp.where(lk, kp, aux)),
        (jnp.where(lq, rel, qp), jnp.where(lk, aux, kp)),
    )


def attend_kernel(n_kv, q_ref, aux_ref, hot_ref, tab_ref, *refs):
    kv_refs = refs[:n_kv]
    o_ref, l_ref = refs[-2:]
    qp = q_ref[...]
    kp = jnp.concatenate([r[0, 0] for r in kv_refs], axis=0)
    vp = jnp.concatenate([r[1, 0] for r in kv_refs], axis=0)
    outs = []
    for h, (qh, kh) in enumerate(score_operands(qp, kp, aux_ref[0], hot_ref[...], tab_ref[...])):
        scores = dot(kh, qh, NT)
        top = jnp.max(scores, axis=0, keepdims=True)
        exponent = jnp.exp(scores - top)
        total = jnp.sum(exponent, axis=0, keepdims=True)
        out = dot(vp, exponent.astype(B16), TN)
        outs.append(out * (1.0 / total))
        l_ref[0, 0, h : h + 1, :] = top + jnp.log(total)
    o_ref[...] = jnp.transpose(jnp.where(low_rows(outs[0].shape), outs[0], outs[1]))


def attend(q, kvs, aux, hot, tab, item_start, row_start, q_rows, items, into):
    rows, width = q.shape
    keys = aux.shape[1]
    pairs = width // LANES
    first = row_start // q_rows
    rowed = pl.BlockSpec((q_rows, LANES), lambda i, p: (first + i, p))
    args = [q, aux, hot, tab] + list(kvs)
    specs = [
        rowed,
        pl.BlockSpec((1, keys, LANES), lambda i, p: (item_start + i, 0, 0)),
        pl.BlockSpec((q_rows, hot.shape[1]), lambda i, p: (first + i, 0)),
        pl.BlockSpec((tab.shape[0], LANES), lambda i, p: (0, p)),
    ] + [pl.BlockSpec((2, 1, kv.shape[2], LANES), lambda i, p: (0, i, 0, p)) for kv in kvs]
    aliases = {}
    if into is not None:
        aliases = {len(args): 0}
        args.append(into)
        specs.append(ANYWHERE)
    return pl.pallas_call(
        partial(attend_kernel, len(kvs)),
        grid=(items, pairs),
        in_specs=specs,
        out_specs=[rowed, pl.BlockSpec((1, 1, 8, q_rows), lambda i, p: (i, p, 0, 0))],
        out_shape=[
            jax.ShapeDtypeStruct((rows, width), F32),
            jax.ShapeDtypeStruct((items, pairs, 8, q_rows), F32),
        ],
        input_output_aliases=aliases,
        compiler_params=params(),
        cost_estimate=cost(14),
        name="attend",
    )(*args)


def attend_back_kernel(n_kv, ids_ref, q_ref, aux_ref, hot_ref, tab_ref, do_ref, o_ref, l_ref, *refs):
    kv_refs = refs[:n_kv]
    dq_ref, own_ref, other_ref, g_ref = refs[-4:]
    qp, dop, hot = q_ref[...], do_ref[...], hot_ref[...]
    kp = jnp.concatenate([r[0, 0] for r in kv_refs], axis=0)
    vp = jnp.concatenate([r[1, 0] for r in kv_refs], axis=0)
    lk = low_lanes(kp.shape)
    zero = jnp.zeros_like(vp)
    product = dop.astype(F32) * o_ref[...]
    row = lax.broadcasted_iota(jnp.int32, (8, LANES), 0)
    pick = jnp.where(low_lanes((8, LANES)) == (row == 0), 1.0, 0.0)
    row_dot = dot(pick, product, NT, precision=lax.Precision.HIGHEST)
    dvs, dks, dqs = [], [], []
    operands = score_operands(qp, kp, aux_ref[0], hot, tab_ref[...])
    for h, (qh, kh) in enumerate(operands):
        vh = jnp.where(lk, vp, zero) if h == 0 else jnp.where(lk, zero, vp)
        probs = jnp.exp(dot(kh, qh, NT) - l_ref[0, 0, h : h + 1, :])
        score_grad = (probs * (dot(vh, dop, NT) - row_dot[h : h + 1, :])).astype(B16)
        dvs.append(dot(probs.astype(B16), dop, NN))
        dks.append(dot(score_grad, qp, NN))
        dqs.append(dot(kh, score_grad, TN))
    dk = jnp.where(lk, dks[0], dks[1]).astype(B16)
    dv = jnp.where(lk, dvs[0], dvs[1]).astype(B16)
    half = own_ref.shape[2]
    own_ref[0, 0], own_ref[1, 0] = dk[:half], dv[:half]
    other_ref[0, 0], other_ref[1, 0] = dk[half:], dv[half:]
    lr = low_rows(dqs[0].shape)
    dq_ref[...] = jnp.transpose(jnp.where(lr, dqs[0], dqs[1])).astype(B16)
    count = g_ref.shape[2] // 2
    middle = LANES // 2
    levels = jnp.concatenate([dqs[0][middle : middle + count], dqs[1][:count]], axis=0)
    upper = levels.astype(B16)
    lower = (levels - upper.astype(F32)).astype(B16)
    g_ref[0, 0] = dot(upper, hot, NN) + dot(lower, hot, NN)


def attend_back(ids, q, kvs, aux, hot, tab, head_grad, head_rows, logs, item_start, row_start, q_rows, items, own):
    width = q.shape[1]
    keys = aux.shape[1]
    pairs = width // LANES // 2
    first = row_start // q_rows

    def pair(p, s):
        return (s[CORE] if own else 1 - s[CORE]) * pairs + p

    rowed = pl.BlockSpec((q_rows, LANES), lambda i, p, s: (first + i, pair(p, s)))
    half = pl.BlockSpec((2, 1, keys // 2, LANES), lambda i, p, s: (0, i, 0, p))
    half_shape = jax.ShapeDtypeStruct((2, items, keys // 2, width // 2), B16)
    return pl.pallas_call(
        partial(attend_back_kernel, len(kvs)),
        grid_spec=pltpu.PrefetchScalarGridSpec(
            num_scalar_prefetch=1,
            grid=(items, pairs),
            in_specs=[
                rowed,
                pl.BlockSpec((1, keys, LANES), lambda i, p, s: (item_start + i, 0, 0)),
                pl.BlockSpec((q_rows, hot.shape[1]), lambda i, p, s: (first + i, 0)),
                pl.BlockSpec((tab.shape[0], LANES), lambda i, p, s: (0, pair(p, s))),
                rowed,
                rowed,
                pl.BlockSpec((1, 1, 8, q_rows), lambda i, p, s: (i, pair(p, s), 0, 0)),
            ]
            + [
                pl.BlockSpec((2, 1, kv.shape[2], LANES), lambda i, p, s: (0, i, 0, pair(p, s)))
                for kv in kvs
            ],
            out_specs=[
                pl.BlockSpec((q_rows, LANES), lambda i, p, s: (i, p)),
                half,
                half,
                pl.BlockSpec((1, 1, hot.shape[1], hot.shape[1]), lambda i, p, s: (i, p, 0, 0)),
            ],
        ),
        out_shape=[
            jax.ShapeDtypeStruct((items * q_rows, width // 2), B16),
            half_shape,
            half_shape,
            jax.ShapeDtypeStruct((items, pairs, hot.shape[1], hot.shape[1]), F32),
        ],
        compiler_params=params(),
        cost_estimate=cost(8),
        name="attend_back",
    )(ids, q, aux, hot, tab, head_grad, head_rows, logs, *kvs)


CHUNK = 32


def gelu_parts(v):
    mass = 0.5 + 0.5 * lax.erf(v * 0.7071067811865476)
    bell = jnp.exp2(v * v * -0.7213475204444817)
    return v * mass, mass + v * (bell * 0.3989422804014327)


def tiles(width):
    return [slice(k, k + LANES) for k in range(0, width, LANES)]


def row_mean(stat, width):
    mean = jnp.sum(stat[...], axis=1, keepdims=True) * (1.0 / width)
    return jnp.broadcast_to(mean, stat.shape)


def chunk_rows(c):
    return pl.ds(pl.multiple_of(c * CHUNK, CHUNK), CHUNK)


def load_output(ids_ref, n, own, mine, other, wo, sem):
    shards = piece_shards(ids_ref, n)
    core = ids_ref[CORE]
    rb, width = own.shape
    half = width // 2
    starts = [pl.multiple_of(shard * rb, 16) for shard in shards]
    pltpu.make_async_copy(own, wo.at[pl.ds(starts[0], rb), :], sem).start()
    for j in range(n - 1):
        for piece, place in ((mine[j], core), (other[j], 1 - core)):
            pltpu.make_async_copy(
                piece.at[pl.ds(3 * rb, rb), :],
                wo.at[pl.ds(starts[j + 1], rb), pl.ds(pl.multiple_of(place * half, LANES), half)],
                sem,
            ).start()


def load_far(far, n, rb, wu, wd, sems):
    group = far.shape[0] // n
    width = wu.shape[0]
    part = wu.shape[1] // GROUPS
    for shard in range(n):
        for g in range(GROUPS):
            pltpu.make_async_copy(
                far.at[shard * group + g, :, pl.ds(0, part)],
                wu.at[pl.ds(shard * rb, rb), pl.ds(g * part, part)],
                sems.at[1],
            ).start()
    for shard in range(n):
        for g in range(GROUPS):
            pltpu.make_async_copy(
                far.at[shard * group + g, :, pl.ds(part, width)],
                wd.at[pl.ds((shard * GROUPS + g) * rb, rb), :],
                sems.at[2],
            ).start()


PARTS = 2


def feed_kernel(n, chips, chunks_a, ids_ref, x_ref, cot_ref, o_ref, vec_ref, ff_ref, scale_ref, far_ref, *refs):
    own, mine, other = refs[0], refs[1:n], refs[n : 2 * n - 1]
    refs = refs[2 * n - 1 :]
    mixed_ref, second_ref, inner_ref, pre_keep, pre_send, branch_keep, branch_send = refs[:7]
    result_ref, mid_ref, head_ref, acc_ref, ffacc_ref = refs[7:12]
    away = refs[12 : 12 + chips - 1]
    wo, wu, wd, act, grads, hats, slopes, pre_grad, total_ref, fold_sums = refs[12 + chips - 1 : -4]
    stat, means, rates, sems = refs[-4:]
    step = pl.program_id(0)
    core = ids_ref[CORE]
    block, wide = act.shape
    width = wo.shape[0]
    share = block // PARTS
    lines = min(CHUNK, share)

    def at_start(action):
        pl.when(step == 0)(action)

    @pl.when(step == 0)
    def _():
        load_output(ids_ref, n, own, mine, other, wo, sems.at[0])
        load_far(far_ref, n, far_ref.shape[1], wu, wd, sems)
        acc_ref[...] = jnp.zeros_like(acc_ref)
        fold_sums[...] = jnp.zeros_like(fold_sums)

    def row_chunks(part):
        for k in range(share // lines):
            yield pl.ds(pl.multiple_of(part * share + k * lines, lines), lines)

    def fold(value):
        out = value[:8]
        for k in range(8, value.shape[0], 8):
            out = out + value[k : k + 8]
        return out

    heads = o_ref[...]
    hat, _ = standardise(heads * scale_ref[0:1, :])
    mixed = (hat * vec_ref[5:6, :] + vec_ref[6:7, :]).astype(B16)
    mixed_ref[...] = mixed
    at_start(lambda: wait_whole(wo, sems.at[0]))
    middle = x_ref[...].astype(F32) + dot(mixed, wo[...], NN) + vec_ref[2:3, :]
    hat, _ = standardise(middle)
    second = (hat * vec_ref[7:8, :] + vec_ref[8:9, :]).astype(B16)
    second_ref[...] = second
    mid_ref[...] = middle
    at_start(lambda: wait_whole(wu, sems.at[1]))
    act[...] = dot(second, wu[...], NN)
    at_start(lambda: wait_whole(wd, sems.at[2]))

    span = wide // PARTS

    @pl.loop(0, PARTS)
    def _(part):
        columns = pl.ds(pl.multiple_of(part * span, LANES), span)
        grads[:, columns] = dot(cot_ref[...], wd[columns, :], NT)
        for rows in row_chunks(part):
            total = jnp.zeros((lines, LANES), F32)
            for lanes in tiles(wide):
                active, slope = gelu_parts(act[rows, lanes] + ff_ref[0:1, lanes])
                slopes[rows, lanes] = slope.astype(B16)
                act[rows, lanes] = active
                total = total + active
            stat[rows, :] = total

    means[...] = row_mean(stat, wide)

    @pl.loop(0, PARTS)
    def _(part):
        for rows in row_chunks(part):
            mean = means[rows, :]
            total = jnp.zeros((lines, LANES), F32)
            for lanes in tiles(wide):
                centred = act[rows, lanes] - mean
                total = total + centred * centred
            stat[rows, :] = total

    rates[...] = lax.rsqrt(row_mean(stat, wide) + EPSILON)

    @pl.loop(0, PARTS)
    def _(part):
        for rows in row_chunks(part):
            mean, rate = means[rows, :], rates[rows, :]
            first = jnp.zeros((lines, LANES), F32)
            other = jnp.zeros((lines, LANES), F32)
            for lanes in tiles(wide):
                gain = ff_ref[1:2, lanes]
                hat = (act[rows, lanes] - mean) * rate
                hats[rows, lanes] = hat.astype(B16)
                inner_ref[rows, lanes] = (hat * gain + ff_ref[2:3, lanes]).astype(B16)
                grad = grads[rows, lanes]
                product = grad * hat
                fold_sums[1, :, lanes] += fold(product)
                fold_sums[2, :, lanes] += fold(grad)
                first = first + grad * gain
                other = other + product * gain
            stat[rows, :] = first
            means[rows, :] = other

    stat[...] = row_mean(stat, wide)
    means[...] = row_mean(means, wide)
    total_ref[...] = mid_ref[...] + vec_ref[9:10, :]

    @pl.loop(0, PARTS)
    def _(part):
        columns = pl.ds(pl.multiple_of(part * span, LANES), span)
        total_ref[...] += dot(inner_ref[:, columns], wd[columns, :], NN)
        for rows in row_chunks(part):
            first, other, rate = stat[rows, :], means[rows, :], rates[rows, :]
            for lanes in tiles(wide):
                scaled = grads[rows, lanes] * ff_ref[1:2, lanes]
                grad = rate * (scaled - first - hats[rows, lanes].astype(F32) * other)
                pre = (grad * slopes[rows, lanes].astype(F32)).astype(B16)
                pre_grad[rows, lanes] = pre
                fold_sums[0, :, lanes] += fold(pre.astype(F32))

    result = total_ref[...].astype(B16)
    result_ref[0] = result
    write_away(away, step, chips, chunks_a, result)
    for which in range(2):

        @pl.when(core == which)
        def _(which=which):
            pre_keep[...] = pre_grad[:, which * wide // 2 : (which + 1) * wide // 2]
            pre_send[...] = pre_grad[:, (1 - which) * wide // 2 : (2 - which) * wide // 2]

    grad = dot(pre_grad[...], wu[...], NT)
    hat, rate = standardise(mid_ref[...])
    acc_ref[0:1, :] += sums(grad * hat)
    acc_ref[1:2, :] += sums(grad)
    cot = cot_ref[...].astype(F32)
    acc_ref[3:4, :] += sums(cot)
    mid = cot + standard_back(grad * vec_ref[7:8, :], hat, rate)
    mid_ref[...] = mid
    branch = mid.astype(B16)
    acc_ref[2:3, :] += sums(branch.astype(F32))
    for which in range(2):

        @pl.when(core == which)
        def _(which=which):
            branch_keep[...] = branch[:, which * width // 2 : (which + 1) * width // 2]
            branch_send[...] = branch[:, (1 - which) * width // 2 : (2 - which) * width // 2]

    grad = dot(branch, wo[...], NT)
    heads = o_ref[...]
    hat, rate = standardise(heads * scale_ref[0:1, :])
    acc_ref[4:5, :] += sums(grad * hat)
    acc_ref[5:6, :] += sums(grad)
    scaled = standard_back(grad * vec_ref[5:6, :], hat, rate)
    acc_ref[6:7, :] += sums(scaled * heads)
    head_ref[...] = (scaled * scale_ref[0:1, :]).astype(B16)

    @pl.when(step == pl.num_programs(0) - 1)
    def _():
        for k in range(3):
            ffacc_ref[k : k + 1, :] = sums(fold_sums[k])
        ffacc_ref[3:, :] = jnp.zeros((ffacc_ref.shape[0] - 3, wide), F32)


def feed(ids, x, cot, head_rows, vec, ff, scale, far, own, mine, other, n, chips, whole, block):
    rows, width = x.shape
    wide = ff.shape[1]
    chunks_a = whole * chips

    def rowed(lanes):
        return pl.BlockSpec((block, lanes), lambda i, s: (i, 0))

    def fixed(shape):
        return pl.BlockSpec(shape, lambda i, s: (0, 0))

    lanes = [width, width, wide, wide // 2, wide // 2, width // 2, width // 2]
    scratch = [(width, width), (width, wide), (wide, width)]
    return pl.pallas_call(
        partial(feed_kernel, n, chips, chunks_a),
        grid_spec=pltpu.PrefetchScalarGridSpec(
            num_scalar_prefetch=1,
            grid=(rows // block,),
            in_specs=[rowed(width)] * 3
            + [fixed(vec.shape), fixed(ff.shape), fixed(scale.shape)]
            + [ANYWHERE] * (2 * n),
            out_specs=[rowed(k) for k in lanes]
            + [
                pl.BlockSpec((1, block, width), home_index(chips, chunks_a)),
                rowed(width),
                rowed(width),
                fixed((8, width)),
                fixed((8, wide)),
            ]
            + [away_spec(block, width, chips, chunks_a)] * (chips - 1),
            scratch_shapes=[pltpu.VMEM(shape, B16) for shape in scratch]
            + [pltpu.VMEM((block, wide), F32)] * 2
            + [pltpu.VMEM((block, wide), B16)] * 3
            + [pltpu.VMEM((block, width), F32), pltpu.VMEM((3, 8, wide), F32)]
            + [pltpu.VMEM((block, LANES), F32)] * 3
            + [pltpu.SemaphoreType.DMA((3,))],
        ),
        out_shape=[jax.ShapeDtypeStruct((rows, k), B16) for k in lanes]
        + [
            jax.ShapeDtypeStruct((rows // block, block, width), B16),
            jax.ShapeDtypeStruct((rows, width), F32),
            jax.ShapeDtypeStruct((rows, width), B16),
            jax.ShapeDtypeStruct((8, width), F32),
            jax.ShapeDtypeStruct((8, wide), F32),
        ]
        + [jax.ShapeDtypeStruct((whole, block, width), B16)] * (chips - 1),
        compiler_params=params(),
        cost_estimate=cost(45),
        name="feed",
    )(ids, x, cot, head_rows, vec, ff, scale, far, own, *mine, *other)


def qkv_side_kernel(counts, factor, shards, rb, ids_ref, normed_ref, normed_other_ref, *refs):
    out_ref = refs[-1]
    step = pl.program_id(0)
    dq_refs, refs = refs[:4], refs[4:-1]

    def finish(out):
        out_ref[:, 0] = out.astype(B16).reshape(shards, rb, out.shape[1])

    @pl.when(step == 0)
    def _():
        rights = [jnp.concatenate([dq_refs[k][...], dq_refs[k + 1][...]], axis=0) for k in (0, 2)]
        finish((dot(normed_ref[...], rights[0], TN) + dot(normed_other_ref[...], rights[1], TN)) * factor)

    @pl.when(step > 0)
    def _():
        at, rights = 0, []
        for count in counts:
            first = add(*[r[0] for r in refs[at : at + count]]).astype(B16)
            rights.append(jnp.concatenate([first, refs[at + count][0]], axis=0))
            at += count + 1
        finish(dot(normed_ref[...], rights[0], TN) + dot(normed_other_ref[...], rights[1], TN))


def qkv_side(ids, normed, normed_other, dqs, dkvs, shards, rb, factor):
    rows, width = normed.shape
    half = width // 2
    whole = pl.BlockSpec((rows, width), lambda t, s: (0, 0))
    flat = [d for first, second in dkvs for d in list(first) + [second]]
    return pl.pallas_call(
        partial(qkv_side_kernel, [len(first) for first, _ in dkvs], factor, shards, rb),
        grid_spec=pltpu.PrefetchScalarGridSpec(
            num_scalar_prefetch=1,
            grid=(3,),
            in_specs=[whole, whole]
            + [pl.BlockSpec(d.shape, lambda t, s: (0, 0)) for d in dqs]
            + [pl.BlockSpec((1,) + d.shape[1:], lambda t, s: (jnp.maximum(t - 1, 0), 0, 0)) for d in flat],
            out_specs=pl.BlockSpec((shards, 1, rb, half), lambda t, s: (0, t, 0, 0)),
        ),
        out_shape=jax.ShapeDtypeStruct((shards, 3, rb, half), B16),
        compiler_params=params(),
        cost_estimate=cost(9),
        name="qkv_side",
    )(ids, normed, normed_other, *dqs, *flat)


def pair_kernel(groups, ids_ref, *refs):
    out_ref = refs[-1]
    block = pl.program_id(0)
    start = 0
    for g, blocks in enumerate(groups):
        left, left_other, right, right_other = refs[4 * g : 4 * g + 4]

        @pl.when((block >= start) & (block < start + blocks))
        def _(left=left, left_other=left_other, right=right, right_other=right_other):
            out = dot(left[...], right[...], TN) + dot(left_other[...], right_other[...], TN)
            out_ref[...] = out.astype(B16).reshape(out_ref.shape)

        start += blocks


def up_side_kernel(blocks, before, ids_ref, mixed_ref, branch_ref, second_ref, pre_ref, *refs):
    out_ref = refs[-1]
    step = pl.program_id(0)

    def finish(out):
        if before:
            out = out + refs[0][...].astype(F32).reshape(out.shape)
        out_ref[...] = out.astype(B16).reshape(out_ref.shape)

    @pl.when(step < blocks)
    def _():
        finish(dot(second_ref[...], pre_ref[...], TN))

    @pl.when(step >= blocks)
    def _():
        finish(dot(mixed_ref[...], branch_ref[...], TN))


def down_side(ids, inner, inner_other, cot, cot_other, into, rb):
    shards = into.shape[0]
    rows, wide = inner.shape
    width = cot.shape[1]
    half = width // 2
    blocks = wide // width
    group = width // (blocks * rb)
    left = pl.BlockSpec((rows, width), lambda g, s: (0, g))
    return pl.pallas_call(
        partial(pair_kernel, [blocks]),
        grid_spec=pltpu.PrefetchScalarGridSpec(
            num_scalar_prefetch=1,
            grid=(blocks,),
            in_specs=[
                left,
                left,
                pl.BlockSpec((rows, half), lambda g, s: (0, s[CORE])),
                pl.BlockSpec((rows, half), lambda g, s: (0, 0)),
                ANYWHERE,
            ],
            out_specs=pl.BlockSpec((group, blocks, rb, half), lambda g, s: (g, 0, 0, 0)),
        ),
        out_shape=jax.ShapeDtypeStruct(into.shape, B16),
        input_output_aliases={5: 0},
        compiler_params=params(),
        cost_estimate=cost(12),
        name="down_side",
    )(ids, inner, inner_other, cot, cot_other, into)


def up_side(ids, mixed, branch, second, pre, into, shards, rb):
    rows, width = mixed.shape
    half = width // 2
    blocks = pre.shape[1] // half
    first = blocks
    shape = (shards, 1 + 2 * blocks, rb, half)
    before = [] if into is None else [into]
    whole = pl.BlockSpec((rows, width), lambda b, s: (0, 0))
    out = pl.BlockSpec((shards, 1, rb, half), lambda b, s: (0, first + jnp.where(b < blocks, b + 1, 0), 0, 0))
    return pl.pallas_call(
        partial(up_side_kernel, blocks, into is not None),
        grid_spec=pltpu.PrefetchScalarGridSpec(
            num_scalar_prefetch=1,
            grid=(1 + blocks,),
            in_specs=[
                whole,
                pl.BlockSpec((rows, half), lambda b, s: (0, 0)),
                whole,
                pl.BlockSpec((rows, half), lambda b, s: (0, jnp.minimum(b, blocks - 1))),
            ]
            + [out] * len(before),
            out_specs=out,
        ),
        out_shape=jax.ShapeDtypeStruct(shape, B16),
        input_output_aliases={} if into is None else {5: 0},
        compiler_params=params(),
        cost_estimate=cost(8),
        name="up_side",
    )(ids, mixed, branch, second, pre, *before)


def terms_kernel(offsets, counts, far, ids_ref, *refs):
    outs = refs[-len(counts) :]
    at = 0
    for out, offset, count in zip(outs, offsets, counts):
        if far:
            total = refs[at][0].astype(F32)
            at += 1
        else:
            total = refs[0][ring_at(ids_ref[SPOT] + offset, refs[0].shape[0])].astype(F32)
            at = max(at, 1)
        for ref in refs[at : at + count]:
            total = total + ref[...].astype(F32)
        out[...] = total.astype(B16)
        at += count


def ring_terms(ids, terms, jobs, far):
    n, piece = terms.shape[0], terms.shape[1:]
    near = pl.BlockSpec(memory_space=pltpu.VMEM)
    zeros = (0,) * len(piece)
    args, specs = ([], []) if far else ([terms], [near])
    for offset, arrived in jobs:
        if far:
            args.append(terms)
            specs.append(
                pl.BlockSpec((1,) + piece, lambda i, s, offset=offset: (ring_at(s[SPOT] + offset, n),) + zeros)
            )
        args += list(arrived)
        specs += [near] * len(arrived)
    out_specs = [near] * len(jobs)
    if far:
        grid = dict(
            grid_spec=pltpu.PrefetchScalarGridSpec(
                num_scalar_prefetch=1, grid=(1,), in_specs=specs, out_specs=out_specs
            )
        )
    else:
        grid = dict(in_specs=[pl.BlockSpec(memory_space=pltpu.SMEM)] + specs, out_specs=out_specs)
    return pl.pallas_call(
        partial(terms_kernel, [offset for offset, _ in jobs], [len(arrived) for _, arrived in jobs], far),
        out_shape=[jax.ShapeDtypeStruct(piece, B16)] * len(jobs),
        compiler_params=params() if far else pltpu.CompilerParams(vmem_limit_bytes=10 * 1024 * 1024),
        cost_estimate=cost(2),
        name="ring_terms",
        **grid,
    )(ids, *args)


def small_kernel(ids_ref, acc_ref, first_ref, second_ref, wide_ref, table_ref, table_send_ref, out_ref):
    width = acc_ref.shape[1]
    core = ids_ref[CORE]
    out_ref[...] = jnp.zeros_like(out_ref)
    out_ref[0:8, :] = acc_ref[...]
    out_ref[8:16, :] = first_ref[...] + second_ref[...]
    blocks = wide_ref.shape[1] // width
    for k in range(3):
        for b in range(blocks):
            row = 16 + k * blocks + b
            out_ref[row : row + 1, :] = wide_ref[k : k + 1, b * width : (b + 1) * width]
    first = 16 + 3 * blocks
    count, lanes = table_ref.shape
    for which in range(2):

        @pl.when(core == which)
        def _(which=which):
            for group, at in ((table_ref, which), (table_send_ref, 1 - which)):
                out_ref[first + at * count : first + (at + 1) * count, 0:lanes] = group[...]


def small_sums(ids, acc, first, second, wide, table, table_send):
    width = acc.shape[1]
    rows = 16 + 3 * (wide.shape[1] // width) + 2 * table.shape[0]
    near = pl.BlockSpec(memory_space=pltpu.VMEM)
    return pl.pallas_call(
        small_kernel,
        in_specs=[pl.BlockSpec(memory_space=pltpu.SMEM)] + [near] * 6,
        out_specs=near,
        out_shape=jax.ShapeDtypeStruct((-(-rows // 8) * 8, width), F32),
        compiler_params=pltpu.CompilerParams(vmem_limit_bytes=4 * 1024 * 1024),
        cost_estimate=cost(2),
        name="small_sums",
    )(ids, acc, first, second, wide, table, table_send)


def finish_kernel(jobs, count, ids_ref, *refs):
    mine, other = refs[:count], refs[count : 2 * count]
    outs = refs[2 * count :]
    half = mine[0].shape[2]
    core = ids_ref[CORE]
    for group, own in ((mine, True), (other, False)):
        for which in range(2):

            @pl.when((core == which) == own)
            def _(group=group, which=which):
                for out, (first, blocks, stacked) in zip(outs, jobs):
                    for b in range(blocks):
                        value = add(*[r[first + b] for r in group])
                        rb = value.shape[0]
                        if stacked:
                            out[b * rb : (b + 1) * rb, which * half : (which + 1) * half] = value
                        else:
                            at = (which * blocks + b) * half
                            out[:, at : at + half] = value


def finish(ids, mine, other, jobs):
    rb, half = mine[0].shape[1:]
    shapes = [
        (blocks * rb, 2 * half) if stacked else (rb, 2 * blocks * half) for _, blocks, stacked in jobs
    ]
    near = pl.BlockSpec(memory_space=pltpu.VMEM)
    return pl.pallas_call(
        partial(finish_kernel, jobs, len(mine)),
        in_specs=[pl.BlockSpec(memory_space=pltpu.SMEM)] + [near] * (2 * len(mine)),
        out_specs=[near] * len(jobs),
        out_shape=[jax.ShapeDtypeStruct(shape, F32) for shape in shapes],
        compiler_params=pltpu.CompilerParams(vmem_limit_bytes=4 * 1024 * 1024),
        cost_estimate=cost(2),
        name="finish",
    )(ids, *mine, *other)


def tie(x, *others):
    return lax.optimization_barrier((x,) + others)[0]


class Places:
    def __init__(self):
        self.n = n = lax.axis_size("dp")
        self.seq = lax.axis_size("seq")
        self.chips = self.seq // 2
        self.ring = list(range(0, n, 2)) + [i for i in range(n) if i % 2][::-1]
        self.shard = shard = lax.axis_index("dp")
        seq = lax.axis_index("seq")
        self.core, self.chip = seq & 1, seq >> 1
        self.spot = jnp.where((shard & 1) == 0, shard >> 1, n - 1 - (shard >> 1))
        lane = lax.broadcasted_iota(jnp.int32, (8,), 0)
        ids = jnp.zeros((8,), jnp.int32)
        values = (self.spot, self.core, self.chip, shard, lax.rem(seq, GROUPS))
        for k, value in enumerate(values):
            ids = jnp.where(lane == k, value, ids)
        self.ids = ids

    def at(self, offset):
        return ring_at(self.spot + offset, self.n)

    def round(self, x, way):
        ring, n = self.ring, self.n
        return lax.ppermute(x, "dp", [(ring[i], ring[(i + way) % n]) for i in range(n)])

    def swap(self, x):
        return lax.ppermute(x, "seq", [(i, i ^ 1) for i in range(self.seq)])

    def chip_turn(self, x, by):
        n = self.chips
        perm = [(2 * i + c, 2 * ((i + by) % n) + c) for i in range(n) for c in range(2)]
        return lax.ppermute(x, "seq", perm)

    def chip_pair(self, x, bit):
        n = self.chips
        perm = [(2 * i + c, 2 * (i ^ bit) + c) for i in range(n) for c in range(2)]
        return lax.ppermute(x, "seq", perm)

    def seq_sums(self, total):
        bit, mine = 1, [total]
        while bit < self.chips:
            low = mine[0] if len(mine) == 1 else add(*mine).astype(B16)
            mine = [low, self.chip_pair(low, bit)]
            bit *= 2
        return mine, [self.swap(x) for x in mine]

    def total_steps(self):
        def over(axis, size, low, high):
            def step(x):
                far = {
                    bit: lax.ppermute(x, axis, [(i, i ^ bit) for i in range(size)])
                    for bit in (low, high, low | high)
                    if bit
                }

                def arrived(value):
                    own = tie(x, value)
                    if low == 0 or high == 0:
                        return own + far[low | high]
                    return (own + far[low]) + (far[high] + far[low | high])

                return arrived

            return step

        steps = []
        for axis, size in (("dp", self.n), ("seq", self.seq)):
            bits = [1 << k for k in range(size.bit_length() - 1)]
            while bits:
                high = bits.pop()
                steps.append(over(axis, size, bits.pop() if bits else 0, high))
        return steps


class RingGather:
    def __init__(self, here, own):
        self.here, self.k = here, 0
        self.forwards, self.backwards = [own], [own]

    def round(self):
        self.k += 1
        self.forwards.append(self.here.round(self.forwards[-1], 1))
        if self.k <= (self.here.n - 1) // 2:
            self.backwards.append(self.here.round(self.backwards[-1], -1))

    def settle(self, *values):
        out = lax.optimization_barrier((self.forwards[-1], self.backwards[-1]) + values)
        self.forwards[-1], self.backwards[-1] = out[:2]
        return out[2:]

    def finish(self):
        while self.k < self.here.n // 2:
            self.round()
        pieces = self.forwards[1:] + self.backwards[1:]
        return pieces, [self.here.swap(piece) for piece in pieces]


class RingSum:
    def __init__(self, here, terms, far):
        self.here, self.terms, self.far = here, terms, far
        self.k = here.n // 2
        self.forward = self.backward = None

    def after(self, *values):
        if self.forward is not None:
            self.forward = tie(self.forward, *values)
        if self.backward is not None:
            self.backward = tie(self.backward, *values)

    def jobs(self, ahead, behind):
        forward = [] if self.forward is None else [self.forward]
        backward = [] if self.backward is None else [self.backward]
        return [(ahead, forward)] + ([] if behind is None else [(behind, backward)])

    def round(self):
        both = self.k <= (self.here.n - 1) // 2
        terms = ring_terms(self.here.ids, self.terms, self.jobs(self.k, -self.k if both else None), self.far)
        self.forward = self.here.round(terms[0], 1)
        if both:
            self.backward = self.here.round(terms[1], -1)
        self.k -= 1
        return terms[0]

    def done(self):
        arrived = [x for x in (self.forward, self.backward) if x is not None]
        return ring_terms(self.here.ids, self.terms, [(0, arrived)], self.far)[0]


def local(
    tokens,
    cotangent,
    segment_ids,
    bucket_ids,
    key_mask,
    query_weight,
    key_weight,
    value_weight,
    output_weight,
    query_bias,
    value_bias,
    output_bias,
    first_gain,
    first_shift,
    mixed_gain,
    mixed_shift,
    up_weight,
    down_weight,
    up_bias,
    down_bias,
    second_gain,
    second_shift,
    inner_gain,
    inner_shift,
    bias_table,
    head_scale,
):
    items, own_rows, width = tokens.shape
    heads = head_scale.shape[0]
    head_width = width // heads
    groups = bias_table.shape[0] // 2
    factor = float(head_width) ** (-0.5)
    wide = up_weight.shape[1]
    wide_rows = wide // width
    rb = query_weight.shape[0]
    here = Places()
    n, chips, ids = here.n, here.chips, here.ids
    whole = items // chips
    left = items - whole * chips
    rows_a = whole * chips * own_rows
    rows_c = left * own_rows

    far = pack_far(ids, up_weight, down_weight)
    far = lax.all_gather(far, ("dp", "seq"), axis=0, tiled=False)
    smalls = [
        query_bias,
        value_bias,
        output_bias,
        first_gain,
        first_shift,
        mixed_gain,
        mixed_shift,
        second_gain,
        second_shift,
        down_bias,
    ]
    wides = [up_bias, inner_gain, inner_shift]
    small = jnp.concatenate([v.reshape(1, rb) for v in smalls] + [v.reshape(-1, rb) for v in wides])
    small = jnp.pad(small, ((0, SMALL_ROWS - small.shape[0]), (0, LANES - rb)))
    own = (query_weight, key_weight, value_weight)
    near = pack_near(ids, own + (output_weight,), small)
    near_ring = RingGather(here, near)
    near_ring.round()

    def take(array, by):
        mine = [
            lax.dynamic_index_in_dim(array, k * chips + lax.rem(here.chip + by, chips), 0, keepdims=False)
            for k in range(whole)
        ]
        return jnp.stack(mine)

    codes = bucket_ids + groups * segment_ids + 2 * groups * (key_mask > 0).astype(jnp.int32)
    turned = [codes] + [here.chip_turn(tie(codes, near), by) for by in range(1, chips)]
    recv = [here.chip_turn(tie(take(tokens, by), near), by) for by in range(1, chips)]
    near_ring.settle()
    near_ring.round()
    out = near_ring.settle(*turned, *recv)
    turned, recv = list(out[:chips]), list(out[chips:])
    turned = turned + [here.swap(c) for c in turned]
    near_ring.round()
    aux, hot, tab, scale = prep(ids, turned, bias_table, head_scale, chips, whole, left, width)
    aux, hot, tab, scale = near_ring.settle(aux, hot, tab, scale)
    near_ring.round()
    mine, other = near_ring.finish()

    x, normed, q, kv_a, kv_c, vec = project(
        tie(ids, aux), tokens, recv, own, small, mine, other, n, chips, whole, factor
    )
    kv_c = kv_c.reshape(2, left, own_rows, width)
    kvs_c = [here.chip_turn(kv_c, by) for by in range(1, chips)]
    kv_a = kv_a.reshape(2, whole, chips * own_rows, width)
    kvs_a = [kv_a, here.swap(kv_a)]
    own_c = [kv_c, here.swap(kv_c)]
    normed_other = here.swap(normed)
    q_a, q_c = chips * own_rows, own_rows
    ff = vec[len(smalls) : len(smalls) + 3 * wide_rows]
    ff = ff.reshape(3, wide_rows, n, rb).transpose(0, 2, 1, 3).reshape(3, wide)
    ff = jnp.pad(ff, ((0, 5), (0, 0)))

    head_rows, logs_a = attend(q, kvs_a, tie(aux, ff), hot, tab, 0, 0, q_a, whole, None)
    kvs_c = [tie(kv, logs_a) for kv in kvs_c]
    cot = [take(cotangent, by) for by in range(1, chips)]
    cot = [here.chip_turn(tie(x, *kvs_c), by) for by, x in enumerate(cot, 1)]
    kvs_c = own_c[:1] + kvs_c + own_c[1:] + [here.swap(kv) for kv in kvs_c]
    head_rows, logs_c = attend(q, kvs_c, aux, hot, tab, whole, rows_a, q_c, left, head_rows)
    cot = jnp.concatenate([take(cotangent, 0)] + [tie(x, logs_c) for x in cot], axis=1)
    cot = jnp.concatenate([cot.reshape(rows_a, width), cotangent[whole * chips :].reshape(rows_c, width)])
    cot_half = lax.dynamic_slice_in_dim(cot, (1 - here.core) * (width // 2), width // 2, axis=1)
    cot_other = here.swap(cot_half)

    outs = feed(
        ids, x, cot, head_rows, vec, ff, scale, far, output_weight, mine, other, n, chips, whole, own_rows
    )
    mixed, second, inner, pre, pre_send, branch, branch_send = outs[:7]
    result, mid, head_grad, acc, ff_acc = outs[7:12]
    pre_other, second_other, mixed_other, branch_other = [
        here.swap(part) for part in (pre_send, second, mixed, branch_send)
    ]
    far_terms = up_side(ids, mixed, branch, second, pre, None, n, rb)
    inner_other = here.swap(inner)
    far_terms = up_side(ids, mixed_other, branch_other, second_other, pre_other, far_terms, n, rb)
    far_terms = down_side(ids, inner, inner_other, cot, cot_other, far_terms, rb)
    far_total = lax.psum_scatter(far_terms, "dp", scatter_dimension=0, tiled=False)
    result_away = [here.chip_turn(part, -by) for by, part in enumerate(outs[12:], 1)]

    pairs = heads // 2

    def back(unit, own, aux):
        kvs, logs, item, row, q_rows, count = unit
        return attend_back(
            ids, q, kvs, aux, hot, tab, head_grad, head_rows, logs, item, row, q_rows, count, own
        )

    unit_c = (kvs_c, logs_c, whole, rows_a, q_c, left)
    unit_a = (kvs_a, logs_a, 0, 0, q_a, whole)
    dq_c_send, own_c_send, other_c_send, g_c_send = back(unit_c, False, tie(aux, far_terms))
    dq_c, own_c, other_c, g_c = back(unit_c, True, aux)

    def near_sum(mine, theirs):
        return add(mine, theirs).astype(B16).reshape(2, left, chips, own_rows, -1)

    def far_parts(near):
        return [near[:, :, 0]] + [here.chip_turn(near[:, :, by], -by) for by in range(1, chips)]

    parts_c = far_parts(near_sum(own_c, here.swap(other_c_send)))
    other_c = here.swap(other_c)
    dq_a_send, own_a_send, other_a_send, g_a_send = back(unit_a, False, tie(aux, parts_c[0]))
    parts_c_send = far_parts(near_sum(own_c_send, tie(other_c, dq_a_send)))
    dq_a_other, own_a_other, other_a_other = [here.swap(x) for x in (dq_a_send, own_a_send, other_a_send)]
    dq_a, own_a, other_a, g_a = back(unit_a, True, tie(aux, parts_c_send[0], *result_away))
    mine_a = here.swap(other_a)

    def c_rows(parts):
        return add(*[tie(p, dq_a) for p in parts]).astype(B16).reshape(2, rows_c, -1)

    dkv_c, dkv_c_send = c_rows(parts_c), c_rows(parts_c_send)
    dkv_c_other, dq_c_other = here.swap(dkv_c_send), here.swap(dq_c_send)

    def a_rows(x):
        return x.reshape(2, rows_a, -1)

    qkv_terms = qkv_side(
        ids,
        normed,
        normed_other,
        [dq_a, dq_c, dq_a_other, dq_c_other],
        [
            ([a_rows(own_a), a_rows(other_a_other)], dkv_c),
            ([a_rows(other_a), a_rows(own_a_other)], dkv_c_other),
        ],
        n,
        rb,
        factor,
    )
    qkv_ring = RingSum(here, qkv_terms, False)

    def rows_back(span, x, dqs, dkvs, into):
        return project_back(
            ids, x, dqs, dkvs, mid, vec, own, mine, other, n, chips, whole, own_rows, factor, span, into
        )

    sent = qkv_ring.round()
    chunks_a = whole * chips
    grad_rows, late_c = rows_back(
        (chunks_a, left), tie(x, sent), [dq_c, dq_c_send], [[dkv_c], [dkv_c_send]], None
    )
    qkv_ring.after(late_c)
    sent = qkv_ring.round()
    grad_rows, late_a, *grad_away = rows_back(
        (0, chunks_a),
        tie(x, sent),
        [dq_a, dq_a_send],
        [
            [a_rows(own_a), a_rows(other_a_other)],
            [a_rows(own_a_send), a_rows(mine_a)],
        ],
        grad_rows,
    )

    offset = jnp.arange(groups)
    spread = (
        (offset[:, None, None] - offset[None, :, None]) % groups == offset[None, None, :]
    ).astype(F32)

    def table_of(*parts):
        g = sum(jnp.sum(tie(part, late_c), axis=0) for part in parts)
        g = g.reshape(heads // 2, groups, 2, groups)
        table = jnp.einsum("hcsb,cbo->hso", g, spread, precision=lax.Precision.HIGHEST)
        return table.reshape(heads // 2, 2 * groups)

    summed = small_sums(ids, acc, late_a, late_c, ff_acc, table_of(g_c, g_a), table_of(g_c_send, g_a_send))

    steps = here.total_steps()
    qkv_ring.after(late_a)
    sent = qkv_ring.round()
    grad_away = [here.chip_turn(tie(part, sent), -by) for by, part in enumerate(grad_away, 1)]
    moved = steps.pop(0)(tie(summed, sent))
    while qkv_ring.k > 0:
        sent = qkv_ring.round()
        if steps:
            moved = steps.pop(0)(moved(sent))
    qkv_ring.after(*grad_away)
    qkv_total = qkv_ring.done()
    far_sums = here.seq_sums(tie(far_total, qkv_total))
    while steps:
        moved = steps.pop(0)(moved(qkv_total))
    summed = moved(qkv_total)

    down_weight_grad, output_weight_grad, up_weight_grad = finish(
        ids, *far_sums, [(0, wide_rows, True), (wide_rows, 1, False), (wide_rows + 1, wide_rows, False)]
    )
    query_weight_grad, key_weight_grad, value_weight_grad = finish(
        tie(ids, down_weight_grad), *here.seq_sums(qkv_total), [(0, 1, False), (1, 1, False), (2, 1, False)]
    )
    mine = lax.dynamic_slice_in_dim(summed[:16], here.shard * rb, rb, axis=1)
    ff_sums = summed[16 : 16 + 3 * wide_rows].reshape(3, wide)
    ff_mine = lax.dynamic_slice_in_dim(ff_sums, here.shard * (wide // n), wide // n, axis=1)
    first = 16 + 3 * wide_rows
    table_grad = jnp.transpose(summed[first : first + heads, : 2 * groups])
    scale_grad = jnp.sum(summed[6].reshape(heads, head_width), axis=1)

    def home(array, away):
        for by, part in enumerate(away, 1):
            part = part.astype(array.dtype)
            for k in range(whole):
                item = k * chips + lax.rem(here.chip + by, chips)
                array = lax.dynamic_update_index_in_dim(array, part[k], item, 0)
        return array

    return (
        home(result, result_away),
        home(grad_rows, grad_away),
        query_weight_grad,
        key_weight_grad,
        value_weight_grad,
        output_weight_grad,
        mine[10],
        mine[11],
        mine[2],
        mine[8],
        mine[9],
        mine[4],
        mine[5],
        up_weight_grad,
        down_weight_grad,
        ff_mine[0],
        mine[3],
        mine[0],
        mine[1],
        ff_mine[1],
        ff_mine[2],
        table_grad,
        scale_grad,
    )


def solution(mesh):
    rowed, shard, vector, whole = P("dp", "seq", None), P("dp", None), P("dp"), P()
    flat = P("dp", "seq")
    placed = (rowed,) * 2 + (flat,) * 3 + (shard,) * 4 + (vector,) * 7 + (shard,) * 2 + (vector,) * 6
    placed = placed + (whole,) * 2
    outs = (rowed,) * 2 + (shard,) * 4 + (vector,) * 7 + (shard,) * 2 + (vector,) * 6 + (whole,) * 2
    return jax.shard_map(local, mesh=mesh, in_specs=placed, out_specs=outs, check_vma=False)
```
